32 devices in a mesh: grp: 4 (over z), work: 8 (over y, x, core).
Axes of the slice: x: 2, y: 2, z: 4, core: 2. Of those that a mesh axis runs over, the one named last changes fastest.
Arguments:
- embeddings: bfloat16 [32768, 1024], P(('grp', 'work')), may hold values from -250 to 250
- offsets: int32 [65], replicated, may hold values from 0 to 32768, as said below
Outputs:
- best_match: float32 [32768], P(('grp', 'work'))
The draws below stay inside these ranges and needn't reach their ends.
Inputs may be any that keep to these rules, and one draw needn't show every extreme that they name: offsets[0] is 0 and each later entry exceeds the one before by 512 to 6144 rows, by exactly 6144 at least once, except that the last cluster may be shorter so as to end at 32768; all entries after it equal 32768. Cluster c holds rows offsets[c] up to offsets[c+1] - 1.
All inputs are finite; a program needn't handle non-finite values.
Results may differ from the reference program's by a relative error of at most 0.00048.
Values may be sent and summed in bfloat16 or wider, within the bound.
No kernel may reach another device: no remote copies, remote signals or barrier semaphores. Data moves between devices by JAX's collectives and lax.ppermute only.
A program may use at most 64 MiB of HBM per device.

```python
import math
import jax
import jax.numpy as jnp
from jax import lax

D = 1024
MOST = 6144
MIN_C = 512
ROWS = 32768
CLUSTER_CAP = 64


def make_offsets(key):
    base_key = jax.random.fold_in(key, 7331)
    key_sizes, key_place = jax.random.split(base_key)
    cluster_sizes = jax.random.randint(key_sizes, (CLUSTER_CAP,), MIN_C, MOST + 1)
    chosen = jax.random.randint(key_place, (), 0, ROWS // MOST)
    cluster_sizes = jnp.where(jnp.arange(CLUSTER_CAP) == chosen, MOST, cluster_sizes)
    cumulative = jnp.minimum(jnp.cumsum(cluster_sizes), ROWS).astype(jnp.int32)
    return jnp.concatenate([jnp.zeros((1,), jnp.int32), cumulative])


def draw_offsets(key, part):
    return make_offsets(key)


def draw_embeddings(key, part):
    offset_table = make_offsets(key)
    row_index = jnp.arange(ROWS, dtype=jnp.int32)
    cluster_ids = jnp.searchsorted(offset_table[1:], row_index, side='right').astype(jnp.int32)
    cluster_ids = jnp.minimum(cluster_ids, CLUSTER_CAP - 1)
    cluster_starts = offset_table[cluster_ids]
    cluster_ends = offset_table[cluster_ids + 1]
    base_key = jax.random.fold_in(key, 99)
    keys_all = jax.random.split(base_key, 8)
    key_center, key_weight, key_noise, key_scale = (keys_all[0], keys_all[1], keys_all[2], keys_all[3])
    key_pick, key_partner, key_close = (keys_all[5], keys_all[6], keys_all[7])
    centroid = jnp.clip(jax.random.normal(key_center, (CLUSTER_CAP, D), jnp.float32), -6.0, 6.0)
    weight = jnp.exp(jax.random.uniform(key_weight, (CLUSTER_CAP,), jnp.float32, math.log(0.3), math.log(3.0)))
    row_scale = jnp.exp(jax.random.uniform(key_scale, (ROWS, 1), jnp.float32, 0.0, math.log(10.0)))
    noise_part = jnp.clip(jax.random.normal(key_noise, (ROWS, D), jnp.float32), -6.0, 6.0)
    is_copy = jax.random.randint(key_pick, (ROWS,), 0, 20) == 0
    partner = jax.random.randint(key_partner, (ROWS,), cluster_starts, cluster_ends).astype(jnp.int32)
    cluster_width = jnp.maximum(cluster_ends - cluster_starts, 1)
    partner = jnp.where(partner == row_index, cluster_starts + (row_index - cluster_starts + 1) % cluster_width, partner)
    close_noise = jnp.clip(jax.random.normal(key_close, (ROWS, D), jnp.float32), -3.0, 3.0)
    copied = noise_part[partner] + 0.02 * close_noise
    noise_part = jnp.where(is_copy[:, None], copied, noise_part)
    values = row_scale * (weight[cluster_ids][:, None] * centroid[cluster_ids] + noise_part)
    return values.astype(jnp.bfloat16)


def setup_inputs(seed: int = 0) -> dict:
    keys = jax.random.split(jax.random.key(seed), 3)
    embeddings = draw_embeddings(jax.random.fold_in(keys[2], 71), 0)
    offsets = draw_offsets(jax.random.fold_in(keys[2], 71), 0)
    return dict(embeddings=embeddings, offsets=offsets)


def to_unit(values):
    widened = values.astype(jnp.float32)
    factor = lax.rsqrt(lax.optimization_barrier(jnp.mean(widened * widened, axis=1, keepdims=True)) + 1e-06) / math.sqrt(values.shape[1])
    return (widened * factor).astype(jnp.bfloat16)

def reference(embeddings, offsets):
    unit_rows = to_unit(embeddings)
    row_index = jnp.arange(ROWS, dtype=jnp.int32)
    cluster_ids = jnp.searchsorted(offsets[1:], row_index, side='right').astype(jnp.int32)
    margin_rows = jnp.zeros((MOST, D), jnp.bfloat16)
    padded_rows = jnp.concatenate([margin_rows, unit_rows, margin_rows], axis=0)
    margin_ids = jnp.full((MOST,), -2, jnp.int32)
    padded_ids = jnp.concatenate([margin_ids, cluster_ids, margin_ids], axis=0)
    block_rows = math.gcd(512, ROWS)
    window = block_rows + 2 * MOST

    def one_block(block_index):
        first_row = (block_index * block_rows).astype(jnp.int32)
        left_rows = lax.dynamic_slice(unit_rows, (first_row, jnp.int32(0)), (block_rows, D))
        left_ids = lax.dynamic_slice(cluster_ids, (first_row,), (block_rows,))
        right_rows = lax.dynamic_slice(padded_rows, (first_row, jnp.int32(0)), (window, D))
        right_ids = lax.dynamic_slice(padded_ids, (first_row,), (window,))
        scores = jnp.dot(left_rows, right_rows.T, preferred_element_type=jnp.float32)
        left_global = first_row + jnp.arange(block_rows, dtype=jnp.int32)
        right_global = first_row - MOST + jnp.arange(window, dtype=jnp.int32)
        same_cluster = (left_ids[:, None] == right_ids[None, :]) & (left_global[:, None] != right_global[None, :])
        masked = jnp.where(same_cluster, scores, jnp.full(scores.shape, -1.0, scores.dtype))
        return lax.optimization_barrier(jnp.max(masked, axis=1))
    blocks = lax.map(one_block, jnp.arange(ROWS // block_rows, dtype=jnp.int32))
    return blocks.reshape(ROWS)
```

```python
import functools
import math

import jax
import jax.numpy as jnp
from jax import lax
from jax.experimental import pallas as pl
from jax.experimental.pallas import tpu as pltpu
from jax.sharding import PartitionSpec as P

AXES = ("grp", "work")
CORES = 2
MIN_C = 512
CHUNKS = (2, 2)
TM = 256
TN = 512
VMEM = 48 * 1024 * 1024


def routes(chips):
    last = chips - 1
    first = [(b, b + 1) for b in range(0, chips, 2) if b + 1 != last]
    first += [(b, b + 3) for b in range(1, chips, 2) if b + 3 < chips]
    first += [(last - 2, last)]
    second = [(b, b + 2) for b in range(0, chips, 2) if b + 2 < chips]
    second += [(b, b - 2) for b in range(1, chips, 2) if b >= 3]
    second += [(last - 1, last)]
    return first, second


def on_cores(pairs):
    return [(CORES * s + k, CORES * d + k) for s, d in pairs for k in range(CORES)]


def flipped(pairs):
    return [(d, s) for s, d in pairs]


def sources(pairs, chips):
    table = [-1] * chips
    for s, d in pairs:
        table[d] = s
    return table


def unit_of(raw):
    wide = raw.astype(jnp.float32)
    mean = jnp.sum(wide * wide, axis=1, keepdims=True) * (1.0 / raw.shape[1])
    factor = lax.rsqrt(mean + 1e-06) * (1.0 / math.sqrt(raw.shape[1]))
    return (wide * factor).astype(jnp.bfloat16)


def normalize(src, dst):
    rows = src.shape[0]
    step = min(128, rows)

    @pl.loop(0, rows // step)
    def _(i):
        at = pl.ds(pl.multiple_of(i * step, step), step)
        dst[at, :] = unit_of(src[at, :])


def product(left, right):
    return lax.dot_general(
        left, right, (((1,), (1,)), ((), ())), preferred_element_type=jnp.float32
    )


def lanes_max(scores):
    parts = [scores[:, j : j + 128] for j in range(0, scores.shape[1], 128)]
    return functools.reduce(jnp.maximum, parts)


def own_kernel(span_ref, own_ref, other_ref, unit_own, unit_other, best_ref, rowpart):
    rows = own_ref.shape[0]
    normalize(own_ref, unit_own)
    normalize(other_ref, unit_other)
    base = span_ref[0, 0]
    shift = span_ref[0, 1]
    rowpart[...] = jnp.full(rowpart.shape, -1.0, jnp.float32)

    @pl.loop(0, rows // TM)
    def _(i):
        at = pl.ds(pl.multiple_of(i * TM, TM), TM)
        left = unit_own[at, :]
        position = base + i * TM + lax.broadcasted_iota(jnp.int32, (TM, 1), 0)
        low = jnp.zeros((TM, 1), jnp.int32)
        high = jnp.zeros((TM, 1), jnp.int32)
        for c in range(1, span_ref.shape[0]):
            here = (position >= span_ref[c, 0]) & (position < span_ref[c, 1])
            low = jnp.where(here, span_ref[c, 0], low)
            high = jnp.where(here, span_ref[c, 1], high)
        for right_ref, start in ((unit_own, base), (unit_other, shift)):

            @pl.loop(0, rows // TN)
            def _(j):
                right = right_ref[pl.ds(pl.multiple_of(j * TN, TN), TN), :]
                scores = product(left, right)
                column = start + j * TN + lax.broadcasted_iota(jnp.int32, (1, TN), 1)
                keep = (column >= low) & (column < high) & (column != position)
                rowpart[at, :] = jnp.maximum(
                    rowpart[at, :], lanes_max(jnp.where(keep, scores, -1.0))
                )

    best_ref[...] = jnp.max(rowpart[...].T, axis=0, keepdims=True)


def meet(left_ref, right_ref, rowpart, colbest, col_at, inside):
    rows, cols = left_ref.shape[0], right_ref.shape[0]
    tm, tn = min(TM, rows), min(TN, cols)
    x0, x1, y0, y1 = inside

    @pl.loop(0, cols // tn)
    def _(j):
        @pl.loop(0, rows // tm)
        def _(i):
            xa, xb = x0 - i * tm, x1 - i * tm
            ya, yb = y0 - j * tn, y1 - j * tn

            @pl.when((xa < tm) & (xb > 0) & (ya < tn) & (yb > 0) & (xa < xb) & (ya < yb))
            def _():
                at = pl.ds(pl.multiple_of(i * tm, tm), tm)
                scores = product(
                    left_ref[at, :], right_ref[pl.ds(pl.multiple_of(j * tn, tn), tn), :]
                )
                row = lax.broadcasted_iota(jnp.int32, (tm, 1), 0)
                col = lax.broadcasted_iota(jnp.int32, (1, tn), 1)
                keep = ((row >= xa) & (row < xb)) & ((col >= ya) & (col < yb))
                scores = jnp.where(keep, scores, -1.0)
                rowpart[at, :] = jnp.maximum(rowpart[at, :], lanes_max(scores))
                to = pl.ds(pl.multiple_of(col_at + j * tn, 128), tn)
                colbest[:, to] = jnp.maximum(
                    colbest[:, to], jnp.max(scores, axis=0, keepdims=True)
                )


def stage_kernel(at, previous, last, *refs):
    refs = list(refs)
    take = lambda n: [refs.pop(0) for _ in range(n)]
    (table,) = take(1)
    a_raw, ax_raw, b_raw = take(3)
    own, other = take(2)
    past = [take(3) for _ in range(previous)]
    acc_in = take(5)
    units = take(3)
    acc = take(5)
    parts = take(3)
    best_own, best_other, best_a, best_ax, best_b = acc
    for src, dst in zip(acc_in, acc):
        dst[...] = src[...]
    for p in parts:
        p[...] = jnp.full(p.shape, -1.0, jnp.float32)
    a, ax, b = units
    normalize(a_raw, a)
    normalize(ax_raw, ax)
    normalize(b_raw, b)
    size = a.shape[0]
    mine = table[12]
    rest = table[13]

    def rect(which, left_from, right_from):
        l0, l1, r0, r1 = (table[4 * which + k] for k in range(4))
        return l0 - left_from, l1 - left_from, r0 - right_from, r1 - right_from

    OA, OB, AB = 0, 1, 2

    def swap(inside):
        x0, x1, y0, y1 = inside
        return y0, y1, x0, x1

    for right, best, start in ((own, best_own, mine), (other, best_other, rest)):
        meet(a, right, parts[0], best, 0, swap(rect(OA, start, mine + at)))
        meet(b, right, parts[2], best, 0, swap(rect(OB, start, mine + at)))
    old = 0
    for pa, pax, pb in past:
        n = pa.shape[0]
        meet(b, pa, parts[2], best_a, old, swap(rect(AB, mine + old, mine + at)))
        meet(b, pax, parts[2], best_ax, old, swap(rect(AB, rest + old, mine + at)))
        meet(a, pb, parts[0], best_b, old, rect(AB, mine + at, mine + old))
        meet(ax, pb, parts[1], best_b, old, rect(AB, rest + at, mine + old))
        old += n
    meet(b, a, parts[2], best_a, at, swap(rect(AB, mine + at, mine + at)))
    meet(b, ax, parts[2], best_ax, at, swap(rect(AB, rest + at, mine + at)))
    to = pl.ds(at, size)
    for part, best in zip(parts, (best_a, best_ax, best_b)):
        best[:, to] = jnp.maximum(best[:, to], jnp.max(part[...].T, axis=0, keepdims=True))


def rectangles(offsets, index, chip_rows, first_of, second_of):
    blocks = jnp.stack([index, first_of, second_of])
    start = blocks * chip_rows
    end = start + chip_rows
    lower = offsets[:-1][None, :]
    upper = offsets[1:][None, :]
    holds = (lower < end[:, None]) & (upper >= end[:, None])
    low = jnp.sum(jnp.where(holds, lower, 0), axis=1)
    high = jnp.sum(jnp.where(holds, upper, 0), axis=1)
    real = (blocks >= 0) & jnp.any(holds, axis=1)
    table = []
    for p, q in ((0, 1), (0, 2), (1, 2)):
        p_first = blocks[p] < blocks[q]
        s = jnp.where(p_first, low[p], low[q])
        e = jnp.where(p_first, high[p], high[q])
        later = jnp.where(p_first, start[q], start[p])
        ok = real[p] & real[q] & (e > later)
        for k, is_first in ((p, p_first), (q, ~p_first)):
            a = jnp.where(is_first, s - start[k], 0)
            z = jnp.where(is_first, chip_rows, e - start[k])
            a = jnp.clip(a, 0, chip_rows)
            z = jnp.clip(z, 0, chip_rows)
            table += [a, jnp.where(ok, z, a)]
    return table


def vmem_call(kernel, ins, outs, scratch, flops):
    vm = pl.BlockSpec(memory_space=pltpu.VMEM)
    sm = pl.BlockSpec(memory_space=pltpu.SMEM)
    moved = sum(x.size * x.dtype.itemsize for x in [*ins, *outs])
    return pl.pallas_call(
        kernel,
        out_shape=outs,
        in_specs=[sm] + [vm] * (len(ins) - 1),
        out_specs=[vm] * len(outs),
        scratch_shapes=scratch,
        compiler_params=pltpu.CompilerParams(vmem_limit_bytes=VMEM),
        cost_estimate=pl.CostEstimate(flops=flops, bytes_accessed=moved, transcendentals=0),
    )(*ins)


def shards(embeddings, offsets):
    rows, depth = embeddings.shape
    chips = lax.axis_size(AXES) // CORES
    me = lax.axis_index(AXES)
    chip, core = me // CORES, me % CORES
    chip_rows = CORES * rows
    first, second = routes(chips)
    swap = [(i, i ^ 1) for i in range(CORES * chips)]
    send = lambda x, pairs: lax.ppermute(x, AXES, pairs)

    sizes = [rows // c for c in CHUNKS]
    starts = [sum(sizes[:k]) for k in range(len(sizes))]
    pieces = [embeddings[s : s + n] for s, n in zip(starts, sizes)]
    a_new = [send(x, on_cores(first)) for x in pieces]
    b_new = [send(x, on_cores(second)) for x in pieces]
    other_raw = send(embeddings, swap)
    ax_new = [send(x, swap) for x in a_new]

    first_of = jnp.array(sources(first, chips), jnp.int32)[chip]
    second_of = jnp.array(sources(second, chips), jnp.int32)[chip]
    mine = core * rows
    rest = (1 - core) * rows
    table = jnp.stack(
        rectangles(offsets, chip, chip_rows, first_of, second_of) + [mine, rest]
    ).astype(jnp.int32)

    base = chip * chip_rows
    here = (offsets[1:] > base) & (offsets[:-1] < base + chip_rows)
    many = chip_rows // MIN_C + 2
    rank = jnp.cumsum(here.astype(jnp.int32)) - 1
    pick = here[None, :] & (rank[None, :] == jnp.arange(many)[:, None])
    low = jnp.sum(jnp.where(pick, offsets[None, :-1], 0), axis=1)
    high = jnp.sum(jnp.where(pick, offsets[None, 1:], 0), axis=1)
    spans = jnp.concatenate(
        [jnp.stack([base + mine, base + rest])[None, :], jnp.stack([low, high], axis=1)]
    ).astype(jnp.int32)

    line = jax.ShapeDtypeStruct((1, rows), jnp.float32)
    block = jax.ShapeDtypeStruct((rows, depth), jnp.bfloat16)
    part = lambda n: pltpu.VMEM((n, 128), jnp.float32)
    own, other, best_own = vmem_call(
        own_kernel,
        [spans, embeddings, other_raw],
        [block, block, line],
        [part(rows)],
        2 * rows * chip_rows * depth,
    )
    blank = jnp.full((1, rows), -1.0, jnp.float32)
    acc = [best_own, blank, blank, blank, blank]
    past = []
    for k, (at, n) in enumerate(zip(starts, sizes)):
        piece = jax.ShapeDtypeStruct((n, depth), jnp.bfloat16)
        done = at
        work = 2 * chip_rows + 2 * (at + n) + 2 * at
        outs = vmem_call(
            functools.partial(stage_kernel, at, k, k == len(sizes) - 1),
            [table, a_new[k], ax_new[k], b_new[k], own, other]
            + [x for triple in past for x in triple]
            + acc,
            [piece] * 3 + [line] * 5,
            [part(n)] * 3,
            2 * n * work * depth,
        )
        past.append(list(outs[:3]))
        acc = list(outs[3:])
    best_own, best_other, best_a, best_ax, best_b = acc

    from_first = send(jnp.concatenate([best_a, best_ax]), on_cores(flipped(first)))
    from_second = send(best_b, on_cores(flipped(second)))
    sent_first = jnp.array([s for s, _ in sorted(first)], jnp.int32)
    has_first = jnp.any(sent_first == chip)
    sent_second = jnp.array([s for s, _ in sorted(second)], jnp.int32)
    has_second = jnp.any(sent_second == chip)
    from_first = jnp.where(has_first, from_first, -1.0)
    from_second = jnp.where(has_second, from_second, -1.0)
    best_other = jnp.maximum(best_other[0], from_first[1])
    best_own = jnp.maximum(jnp.maximum(best_own[0], from_first[0]), from_second[0])
    return jnp.maximum(best_own, send(best_other, swap))


def solution(mesh):
    return jax.shard_map(
        shards,
        mesh=mesh,
        in_specs=(P(AXES, None), P()),
        out_specs=P(AXES),
        check_vma=False,
    )
```

```python
import dataclasses
import functools
import math

import jax
import jax.numpy as jnp
from jax import lax
from jax.experimental import pallas as pl
from jax.experimental.pallas import tpu as pltpu
from jax.sharding import PartitionSpec as P

AXES = ("grp", "work")
CORES = 2
MIN_C = 512
TILE = 512
VMEM = 24 * 1024 * 1024


def routes(chips):
    last = chips - 1
    first = [(b, b + 1) for b in range(0, chips, 2) if b + 1 != last]
    first += [(b, b + 3) for b in range(1, chips, 2) if b + 3 < chips]
    first += [(last - 2, last)]
    second = [(b, b + 2) for b in range(0, chips, 2) if b + 2 < chips]
    second += [(b, b - 2) for b in range(1, chips, 2) if b >= 3]
    second += [(last - 1, last)]
    return first, second


def on_cores(pairs):
    return [(CORES * s + k, CORES * d + k) for s, d in pairs for k in range(CORES)]


def flipped(pairs):
    return [(d, s) for s, d in pairs]


def rectangles(offsets, index, chip_rows, first_of, second_of):
    blocks = jnp.stack([index, first_of, second_of])
    start = blocks * chip_rows
    end = start + chip_rows
    lower = offsets[:-1][None, :]
    upper = offsets[1:][None, :]
    holds = (lower < end[:, None]) & (upper >= end[:, None])
    low = jnp.sum(jnp.where(holds, lower, 0), axis=1)
    high = jnp.sum(jnp.where(holds, upper, 0), axis=1)
    real = (blocks >= 0) & jnp.any(holds, axis=1)
    table = []
    for p, q in ((0, 1), (0, 2), (1, 2)):
        p_first = blocks[p] < blocks[q]
        s = jnp.where(p_first, low[p], low[q])
        e = jnp.where(p_first, high[p], high[q])
        later = jnp.where(p_first, start[q], start[p])
        ok = real[p] & real[q] & (e > later)
        for k, is_first in ((p, p_first), (q, ~p_first)):
            a = jnp.where(is_first, s - start[k], 0)
            z = jnp.where(is_first, chip_rows, e - start[k])
            a = jnp.clip(a, 0, chip_rows)
            z = jnp.clip(z, 0, chip_rows)
            table += [a, jnp.where(ok, z, a)]
    return table


def unit_of(raw):
    wide = raw.astype(jnp.float32)
    mean = jnp.sum(wide * wide, axis=1, keepdims=True) * (1.0 / raw.shape[1])
    factor = lax.rsqrt(mean + 1e-06) * (1.0 / math.sqrt(raw.shape[1]))
    return (wide * factor).astype(jnp.bfloat16)


def unit_kernel(raw_ref, *outs):
    rows = raw_ref.shape[0]
    step = math.gcd(128, min(out.shape[0] for out in outs))
    for first in range(0, rows, step):
        unit = unit_of(raw_ref[first : first + step, :])
        for out in outs:
            out[first % out.shape[0] : first % out.shape[0] + step, :] = unit


def units_of(raw, which, count):
    rows, depth = raw.shape[0] // count, raw.shape[1]
    return pl.pallas_call(
        unit_kernel,
        grid=(1,),
        in_specs=[pl.BlockSpec((rows, depth), lambda i: (which, 0))],
        out_specs=pl.BlockSpec((rows, depth), lambda i: (0, 0)),
        out_shape=jax.ShapeDtypeStruct((rows, depth), jnp.bfloat16),
        compiler_params=pltpu.CompilerParams(vmem_limit_bytes=VMEM),
        cost_estimate=pl.CostEstimate(
            flops=8 * rows * depth, bytes_accessed=4 * rows * depth, transcendentals=0
        ),
    )(raw)


def product(left, right):
    return lax.dot_general(
        left, right, (((1,), (1,)), ((), ())), preferred_element_type=jnp.float32
    )


def lanes_max(scores):
    parts = [scores[:, j : j + 128] for j in range(0, scores.shape[1], 128)]
    return functools.reduce(jnp.maximum, parts)


def across(part):
    return jnp.max(part.T, axis=0, keepdims=True)


@dataclasses.dataclass
class Piece:
    rows: jax.Array
    block: int
    side: int
    at: int

    @property
    def n(self):
        return self.rows.shape[0]


def own_kernel(lefts, rights, span_ref, *refs):
    refs = list(refs)
    lines = [refs.pop(0) for _ in lefts]
    fars = [refs.pop(0) for _ in rights]
    best_ref, rowpart = refs
    everything = list(zip(lefts, lines, [0] * len(lefts)))
    everything += list(zip(rights, fars, [1] * len(rights)))
    best_ref[...] = jnp.full(best_ref.shape, -1.0, jnp.float32)
    for left, left_ref in zip(lefts, lines):
        size = left_ref.shape[0]
        position = span_ref[0, 0] + left.at + lax.broadcasted_iota(jnp.int32, (size, 1), 0)
        low = jnp.zeros((size, 1), jnp.int32)
        high = jnp.zeros((size, 1), jnp.int32)
        for c in range(1, span_ref.shape[0]):
            here = (position >= span_ref[c, 0]) & (position < span_ref[c, 1])
            low = jnp.where(here, span_ref[c, 0], low)
            high = jnp.where(here, span_ref[c, 1], high)
        rowpart[...] = jnp.full(rowpart.shape, -1.0, jnp.float32)
        for right, right_ref, far in everything:
            start = span_ref[0, far] + right.at
            scores = product(left_ref[...], right_ref[...])
            column = start + lax.broadcasted_iota(jnp.int32, (1, right_ref.shape[0]), 1)
            keep = (column >= low) & (column < high) & (column != position)
            rowpart[...] = jnp.maximum(
                rowpart[...], lanes_max(jnp.where(keep, scores, -1.0))
            )
        best_ref[0:1, left.at : left.at + size] = across(rowpart[...])


PAIRS = {(0, 1): 0, (0, 2): 1, (1, 2): 2}


def rect(table, left, right):
    flip = left.block > right.block
    which = PAIRS[(right.block, left.block) if flip else (left.block, right.block)]
    ends = [table[4 * which + k] for k in range(4)]
    if flip:
        ends = ends[2:] + ends[:2]
    x, y = table[12 + left.side] + left.at, table[12 + right.side] + right.at
    return ends[0] - x, ends[1] - x, ends[2] - y, ends[3] - y


def meet_kernel(pieces, groups, table, *refs):
    refs = list(refs)
    held = [refs.pop(0) for _ in pieces]
    acc_in = [refs.pop(0) for _ in range(3)]
    acc = [refs.pop(0) for _ in range(3)]
    (rowpart,) = refs
    for src, dst in zip(acc_in, acc):
        dst[...] = src[...]
    for l, partners in groups:
        left, left_ref = pieces[l], held[l]
        tm = left_ref.shape[0]
        part = rowpart.at[0:tm]
        part[...] = jnp.full(part.shape, -1.0, jnp.float32)
        for r in partners:
            right, right_ref = pieces[r], held[r]
            tn = right_ref.shape[0]
            xa, xb, ya, yb = rect(table, left, right)
            some = (xa < tm) & (xb > 0) & (ya < tn) & (yb > 0) & (xa < xb) & (ya < yb)

            @pl.when(some)
            def _():
                scores = product(left_ref[...], right_ref[...])
                row = lax.broadcasted_iota(jnp.int32, (tm, 1), 0)
                col = lax.broadcasted_iota(jnp.int32, (1, tn), 1)
                keep = ((row >= xa) & (row < xb)) & ((col >= ya) & (col < yb))
                scores = jnp.where(keep, scores, -1.0)
                part[...] = jnp.maximum(part[...], lanes_max(scores))
                to = (slice(right.side, right.side + 1), slice(right.at, right.at + tn))
                best = acc[right.block]
                best[to] = jnp.maximum(best[to], jnp.max(scores, axis=0, keepdims=True))

        to = (slice(left.side, left.side + 1), slice(left.at, left.at + tm))
        best = acc[left.block]
        best[to] = jnp.maximum(best[to], across(part[...]))


def vmem_call(kernel, ins, outs, scratch, flops):
    vm = pl.BlockSpec(memory_space=pltpu.VMEM)
    sm = pl.BlockSpec(memory_space=pltpu.SMEM)
    moved = sum(x.size * x.dtype.itemsize for x in [*ins, *outs])
    return pl.pallas_call(
        kernel,
        out_shape=outs,
        in_specs=[sm] + [vm] * (len(ins) - 1),
        out_specs=[vm] * len(outs),
        scratch_shapes=scratch,
        compiler_params=pltpu.CompilerParams(vmem_limit_bytes=VMEM),
        cost_estimate=pl.CostEstimate(flops=flops, bytes_accessed=moved, transcendentals=0),
    )(*ins)


def meet(table, pairs, acc):
    pieces, groups = [], []

    def index(piece):
        for i, other in enumerate(pieces):
            if other is piece:
                return i
        pieces.append(piece)
        return len(pieces) - 1

    for left, rights in pairs:
        groups.append((index(left), [index(r) for r in rights]))
    depth = pieces[0].rows.shape[1]
    flops = sum(2 * left.n * r.n * depth for left, rights in pairs for r in rights)
    most = max(left.n for left, _ in pairs)
    return vmem_call(
        functools.partial(
            meet_kernel, [dataclasses.replace(p, rows=None) for p in pieces], groups
        ),
        [table] + [p.rows for p in pieces] + list(acc),
        [jax.ShapeDtypeStruct(a.shape, a.dtype) for a in acc],
        [pltpu.VMEM((most, 128), jnp.float32)],
        flops,
    )


def after(value, *others):
    return lax.optimization_barrier((value, *others))[0]


def shards(embeddings, offsets):
    rows, depth = embeddings.shape
    chips = lax.axis_size(AXES) // CORES
    me = lax.axis_index(AXES)
    chip, core = me // CORES, me % CORES
    chip_rows = CORES * rows
    first, second = routes(chips)
    to_first, to_second = on_cores(first), on_cores(second)
    swap = [(i, i ^ 1) for i in range(CORES * chips)]
    send = lambda x, pairs: lax.ppermute(x, AXES, pairs)

    half, quarter = rows // 2, rows // 4
    u1 = units_of(embeddings, 0, 2)
    a1, b1 = send(u1, to_first), send(u1, to_second)
    later = after(embeddings, u1)
    u2 = units_of(later, 1, 2)
    u3, u4 = units_of(later, 2, 4), units_of(later, 3, 4)
    a2 = send(u2, to_first)
    b2, b3 = send(u3, to_second), send(u4, to_second)
    far1, far2 = send(u1, swap), send(u2, swap)

    mine = core * rows
    rest = (1 - core) * rows
    odd = chip % 2 == 1
    at_end = chip == chips - 1
    first_of = jnp.where(odd, jnp.where(at_end, chip - 2, chip - 1), chip - 3)
    second_of = jnp.where(odd, jnp.where(at_end, chip - 1, chip + 2), chip - 2)
    table = jnp.stack(
        rectangles(offsets, chip, chip_rows, first_of, second_of) + [mine, rest]
    ).astype(jnp.int32)

    base = chip * chip_rows
    here = (offsets[1:] > base) & (offsets[:-1] < base + chip_rows)
    many = chip_rows // MIN_C + 2
    rank = jnp.cumsum(here.astype(jnp.int32)) - 1
    pick = here[None, :] & (rank[None, :] == jnp.arange(many)[:, None])
    low = jnp.sum(jnp.where(pick, offsets[None, :-1], 0), axis=1)
    high = jnp.sum(jnp.where(pick, offsets[None, 1:], 0), axis=1)
    spans = jnp.concatenate(
        [jnp.stack([base + mine, base + rest])[None, :], jnp.stack([low, high], axis=1)]
    ).astype(jnp.int32)

    own = [Piece(u1, 0, 0, 0), Piece(u2, 0, 0, half)]
    far = [Piece(far1, 0, 1, 0), Piece(far2, 0, 1, half)]
    (best_own,) = vmem_call(
        functools.partial(
            own_kernel,
            [dataclasses.replace(p, rows=None) for p in own],
            [dataclasses.replace(p, rows=None) for p in far],
        ),
        [spans] + [p.rows for p in own + far],
        [jax.ShapeDtypeStruct((CORES, rows), jnp.float32)],
        [pltpu.VMEM((half, 128), jnp.float32)],
        2 * rows * chip_rows * depth,
    )
    blank = jnp.full((CORES, rows), -1.0, jnp.float32)
    acc = [best_own, blank, blank[:1]]
    chip_own = own + far

    pa1, pb1 = Piece(a1, 1, 0, 0), Piece(b1, 2, 0, 0)
    pax1 = Piece(send(after(a1, acc[0]), swap), 1, 1, 0)
    acc = meet(table, [(pa1, chip_own), (pb1, chip_own + [pa1])], acc)
    acc = meet(table, [(pb1, [pax1])], acc)

    pa2, pb2, pb3 = Piece(a2, 1, 0, half), Piece(b2, 2, 0, half), Piece(b3, 2, 0, half + quarter)
    pax2 = Piece(send(after(a2, acc[0]), swap), 1, 1, half)
    acc = meet(table, [(pa2, chip_own + [pb1]), (pb2, chip_own + [pa1, pax1, pa2])], acc)
    acc = meet(
        table, [(pb3, chip_own + [pa1, pax1, pa2, pax2]), (pax2, [pb1, pb2])], acc
    )

    best_own, best_first, best_second = acc
    from_first = send(best_first, on_cores(flipped(first)))
    from_second = send(best_second, on_cores(flipped(second)))
    has_first = jnp.where(odd, (chip + 3 < chips) | (chip == chips - 3), chip + 2 < chips)
    has_second = jnp.where(odd, chip >= 3, (chip + 2 < chips) | (chip == chips - 2))
    from_first = jnp.where(has_first, from_first, -1.0)
    from_second = jnp.where(has_second, from_second, -1.0)
    other = jnp.maximum(best_own[1], from_first[1])
    mine_best = jnp.maximum(jnp.maximum(best_own[0], from_first[0]), from_second[0])
    return jnp.maximum(mine_best, send(other, swap))


def solution(mesh):
    return jax.shard_map(
        shards,
        mesh=mesh,
        in_specs=(P(AXES, None), P()),
        out_specs=P(AXES),
        check_vma=False,
    )
```

```python
import dataclasses
import functools
import math

import jax
import jax.numpy as jnp
from jax import lax
from jax.experimental import pallas as pl
from jax.experimental.pallas import tpu as pltpu
from jax.sharding import PartitionSpec as P

AXES = ("grp", "work")
CORES = 2
MIN_C = 512
TILE = 512
VMEM = 24 * 1024 * 1024


def routes(chips):
    last = chips - 1
    first = [(b, b + 1) for b in range(0, chips, 2) if b + 1 != last]
    first += [(b, b + 3) for b in range(1, chips, 2) if b + 3 < chips]
    first += [(last - 2, last)]
    second = [(b, b + 2) for b in range(0, chips, 2) if b + 2 < chips]
    second += [(b, b - 2) for b in range(1, chips, 2) if b >= 3]
    second += [(last - 1, last)]
    return first, second


def on_cores(pairs):
    return [(CORES * s + k, CORES * d + k) for s, d in pairs for k in range(CORES)]


def flipped(pairs):
    return [(d, s) for s, d in pairs]


def rectangles(offsets, index, chip_rows, first_of, second_of):
    blocks = jnp.stack([index, first_of, second_of])
    start = blocks * chip_rows
    end = start + chip_rows
    lower = offsets[:-1][None, :]
    upper = offsets[1:][None, :]
    holds = (lower < end[:, None]) & (upper >= end[:, None])
    low = jnp.sum(jnp.where(holds, lower, 0), axis=1)
    high = jnp.sum(jnp.where(holds, upper, 0), axis=1)
    real = (blocks >= 0) & jnp.any(holds, axis=1)
    table = []
    for p, q in ((0, 1), (0, 2), (1, 2)):
        p_first = blocks[p] < blocks[q]
        s = jnp.where(p_first, low[p], low[q])
        e = jnp.where(p_first, high[p], high[q])
        later = jnp.where(p_first, start[q], start[p])
        ok = real[p] & real[q] & (e > later)
        for k, is_first in ((p, p_first), (q, ~p_first)):
            a = jnp.where(is_first, s - start[k], 0)
            z = jnp.where(is_first, chip_rows, e - start[k])
            a = jnp.clip(a, 0, chip_rows)
            z = jnp.clip(z, 0, chip_rows)
            table += [a, jnp.where(ok, z, a)]
    return table


def unit_of(raw):
    wide = raw.astype(jnp.float32)
    mean = jnp.sum(wide * wide, axis=1, keepdims=True) * (1.0 / raw.shape[1])
    factor = lax.rsqrt(mean + 1e-06) * (1.0 / math.sqrt(raw.shape[1]))
    return (wide * factor).astype(jnp.bfloat16)


def unit_kernel(raw_ref, *outs):
    rows = raw_ref.shape[0]
    step = math.gcd(128, min(out.shape[0] for out in outs))
    for first in range(0, rows, step):
        unit = unit_of(raw_ref[first : first + step, :])
        for out in outs:
            out[first % out.shape[0] : first % out.shape[0] + step, :] = unit


def units_of(raw, which, count):
    rows, depth = raw.shape[0] // count, raw.shape[1]
    return pl.pallas_call(
        unit_kernel,
        grid=(1,),
        in_specs=[pl.BlockSpec((rows, depth), lambda i: (which, 0))],
        out_specs=pl.BlockSpec((rows, depth), lambda i: (0, 0)),
        out_shape=jax.ShapeDtypeStruct((rows, depth), jnp.bfloat16),
        compiler_params=pltpu.CompilerParams(vmem_limit_bytes=VMEM),
        cost_estimate=pl.CostEstimate(
            flops=8 * rows * depth, bytes_accessed=4 * rows * depth, transcendentals=0
        ),
    )(raw)


def product(left, right):
    return lax.dot_general(
        left, right, (((1,), (1,)), ((), ())), preferred_element_type=jnp.float32
    )


def lanes_max(scores):
    parts = [scores[:, j : j + 128] for j in range(0, scores.shape[1], 128)]
    return functools.reduce(jnp.maximum, parts)


def across(part):
    return jnp.max(part.T, axis=0, keepdims=True)


@dataclasses.dataclass
class Piece:
    rows: jax.Array
    block: int
    side: int
    at: int

    @property
    def n(self):
        return self.rows.shape[0]


def own_kernel(lefts, rights, span_ref, *refs):
    refs = list(refs)
    lines = [refs.pop(0) for _ in lefts]
    fars = [refs.pop(0) for _ in rights]
    best_ref, rowpart = refs
    everything = list(zip(lefts, lines, [0] * len(lefts)))
    everything += list(zip(rights, fars, [1] * len(rights)))
    best_ref[...] = jnp.full(best_ref.shape, -1.0, jnp.float32)
    for left, left_ref in zip(lefts, lines):
        size = left_ref.shape[0]
        position = span_ref[0, 0] + left.at + lax.broadcasted_iota(jnp.int32, (size, 1), 0)
        low = jnp.zeros((size, 1), jnp.int32)
        high = jnp.zeros((size, 1), jnp.int32)
        for c in range(1, span_ref.shape[0]):
            here = (position >= span_ref[c, 0]) & (position < span_ref[c, 1])
            low = jnp.where(here, span_ref[c, 0], low)
            high = jnp.where(here, span_ref[c, 1], high)
        rowpart[...] = jnp.full(rowpart.shape, -1.0, jnp.float32)
        for right, right_ref, far in everything:
            start = span_ref[0, far] + right.at
            scores = product(left_ref[...], right_ref[...])
            column = start + lax.broadcasted_iota(jnp.int32, (1, right_ref.shape[0]), 1)
            keep = (column >= low) & (column < high) & (column != position)
            rowpart[...] = jnp.maximum(
                rowpart[...], lanes_max(jnp.where(keep, scores, -1.0))
            )
        best_ref[0:1, left.at : left.at + size] = across(rowpart[...])


PAIRS = {(0, 1): 0, (0, 2): 1, (1, 2): 2}


def rect(table, left, right):
    flip = left.block > right.block
    which = PAIRS[(right.block, left.block) if flip else (left.block, right.block)]
    ends = [table[4 * which + k] for k in range(4)]
    if flip:
        ends = ends[2:] + ends[:2]
    x, y = table[12 + left.side] + left.at, table[12 + right.side] + right.at
    return ends[0] - x, ends[1] - x, ends[2] - y, ends[3] - y


def meet_kernel(pieces, groups, table, *refs):
    refs = list(refs)
    held = [refs.pop(0) for _ in pieces]
    acc_in = [refs.pop(0) for _ in range(3)]
    acc = [refs.pop(0) for _ in range(3)]
    (rowpart,) = refs
    for src, dst in zip(acc_in, acc):
        dst[...] = src[...]
    for l, partners in groups:
        left, left_ref = pieces[l], held[l]
        tm = left_ref.shape[0]
        part = rowpart.at[0:tm]
        part[...] = jnp.full(part.shape, -1.0, jnp.float32)
        for r in partners:
            right, right_ref = pieces[r], held[r]
            tn = right_ref.shape[0]
            xa, xb, ya, yb = rect(table, left, right)
            some = (xa < tm) & (xb > 0) & (ya < tn) & (yb > 0) & (xa < xb) & (ya < yb)

            @pl.when(some)
            def _():
                scores = product(left_ref[...], right_ref[...])
                row = lax.broadcasted_iota(jnp.int32, (tm, 1), 0)
                col = lax.broadcasted_iota(jnp.int32, (1, tn), 1)
                keep = ((row >= xa) & (row < xb)) & ((col >= ya) & (col < yb))
                scores = jnp.where(keep, scores, -1.0)
                part[...] = jnp.maximum(part[...], lanes_max(scores))
                to = (slice(right.side, right.side + 1), slice(right.at, right.at + tn))
                best = acc[right.block]
                best[to] = jnp.maximum(best[to], jnp.max(scores, axis=0, keepdims=True))

        to = (slice(left.side, left.side + 1), slice(left.at, left.at + tm))
        best = acc[left.block]
        best[to] = jnp.maximum(best[to], across(part[...]))


def vmem_call(kernel, ins, outs, scratch, flops):
    vm = pl.BlockSpec(memory_space=pltpu.VMEM)
    sm = pl.BlockSpec(memory_space=pltpu.SMEM)
    moved = sum(x.size * x.dtype.itemsize for x in [*ins, *outs])
    return pl.pallas_call(
        kernel,
        out_shape=outs,
        in_specs=[sm] + [vm] * (len(ins) - 1),
        out_specs=[vm] * len(outs),
        scratch_shapes=scratch,
        compiler_params=pltpu.CompilerParams(vmem_limit_bytes=VMEM),
        cost_estimate=pl.CostEstimate(flops=flops, bytes_accessed=moved, transcendentals=0),
    )(*ins)


def meet(table, pairs, acc):
    pieces, groups = [], []

    def index(piece):
        for i, other in enumerate(pieces):
            if other is piece:
                return i
        pieces.append(piece)
        return len(pieces) - 1

    for left, rights in pairs:
        groups.append((index(left), [index(r) for r in rights]))
    depth = pieces[0].rows.shape[1]
    flops = sum(2 * left.n * r.n * depth for left, rights in pairs for r in rights)
    most = max(left.n for left, _ in pairs)
    return vmem_call(
        functools.partial(
            meet_kernel, [dataclasses.replace(p, rows=None) for p in pieces], groups
        ),
        [table] + [p.rows for p in pieces] + list(acc),
        [jax.ShapeDtypeStruct(a.shape, a.dtype) for a in acc],
        [pltpu.VMEM((most, 128), jnp.float32)],
        flops,
    )


def after(value, *others):
    return lax.optimization_barrier((value, *others))[0]


def shards(embeddings, offsets):
    rows, depth = embeddings.shape
    chips = lax.axis_size(AXES) // CORES
    me = lax.axis_index(AXES)
    chip, core = me // CORES, me % CORES
    chip_rows = CORES * rows
    first, second = routes(chips)
    to_first, to_second = on_cores(first), on_cores(second)
    swap = [(i, i ^ 1) for i in range(CORES * chips)]
    send = lambda x, pairs: lax.ppermute(x, AXES, pairs)

    half = rows // 2
    u1 = units_of(embeddings, 0, 2)
    a1, b1 = send(u1, to_first), send(u1, to_second)
    far1 = send(u1, swap)
    u2 = units_of(after(embeddings, far1), 1, 2)
    a2 = send(u2, to_first)
    b2 = send(u2, to_second)
    far2 = send(u2, swap)

    mine = core * rows
    rest = (1 - core) * rows
    odd = chip % 2 == 1
    at_end = chip == chips - 1
    first_of = jnp.where(odd, jnp.where(at_end, chip - 2, chip - 1), chip - 3)
    second_of = jnp.where(odd, jnp.where(at_end, chip - 1, chip + 2), chip - 2)
    table = jnp.stack(
        rectangles(offsets, chip, chip_rows, first_of, second_of) + [mine, rest]
    ).astype(jnp.int32)

    base = chip * chip_rows
    here = (offsets[1:] > base) & (offsets[:-1] < base + chip_rows)
    many = chip_rows // MIN_C + 2
    rank = jnp.cumsum(here.astype(jnp.int32)) - 1
    pick = here[None, :] & (rank[None, :] == jnp.arange(many)[:, None])
    low = jnp.sum(jnp.where(pick, offsets[None, :-1], 0), axis=1)
    high = jnp.sum(jnp.where(pick, offsets[None, 1:], 0), axis=1)
    spans = jnp.concatenate(
        [jnp.stack([base + mine, base + rest])[None, :], jnp.stack([low, high], axis=1)]
    ).astype(jnp.int32)

    own = [Piece(u1, 0, 0, 0), Piece(u2, 0, 0, half)]
    far = [Piece(far1, 0, 1, 0), Piece(far2, 0, 1, half)]
    (best_own,) = vmem_call(
        functools.partial(
            own_kernel,
            [dataclasses.replace(p, rows=None) for p in own],
            [dataclasses.replace(p, rows=None) for p in far],
        ),
        [spans] + [p.rows for p in own + far],
        [jax.ShapeDtypeStruct((CORES, rows), jnp.float32)],
        [pltpu.VMEM((half, 128), jnp.float32)],
        2 * rows * chip_rows * depth,
    )
    blank = jnp.full((CORES, rows), -1.0, jnp.float32)
    acc = [best_own, blank, blank[:1]]
    chip_own = own + far

    pa1, pb1 = Piece(a1, 1, 0, 0), Piece(b1, 2, 0, 0)
    pax1 = Piece(send(after(a1, acc[0]), swap), 1, 1, 0)
    acc = meet(table, [(pa1, chip_own), (pb1, chip_own + [pa1])], acc)
    acc = meet(table, [(pb1, [pax1])], acc)

    pa2, pb2 = Piece(a2, 1, 0, half), Piece(b2, 2, 0, half)
    pax2 = Piece(send(after(a2, acc[0]), swap), 1, 1, half)
    acc = meet(table, [(pa2, chip_own + [pb1])], acc)
    acc = meet(
        table, [(pb2, chip_own + [pa1, pax1, pa2, pax2]), (pax2, [pb1])], acc
    )

    best_own, best_first, best_second = acc
    from_first = send(best_first, on_cores(flipped(first)))
    from_second = send(best_second, on_cores(flipped(second)))
    has_first = jnp.where(odd, (chip + 3 < chips) | (chip == chips - 3), chip + 2 < chips)
    has_second = jnp.where(odd, chip >= 3, (chip + 2 < chips) | (chip == chips - 2))
    from_first = jnp.where(has_first, from_first, -1.0)
    from_second = jnp.where(has_second, from_second, -1.0)
    other = jnp.maximum(best_own[1], from_first[1])
    mine_best = jnp.maximum(jnp.maximum(best_own[0], from_first[0]), from_second[0])
    return jnp.maximum(mine_best, send(other, swap))


def solution(mesh):
    return jax.shard_map(
        shards,
        mesh=mesh,
        in_specs=(P(AXES, None), P()),
        out_specs=P(AXES),
        check_vma=False,
    )
```

```python
import dataclasses
import functools
import math

import jax
import jax.numpy as jnp
from jax import lax
from jax.experimental import pallas as pl
from jax.experimental.pallas import tpu as pltpu
from jax.sharding import PartitionSpec as P

AXES = ("grp", "work")
CORES = 2
MIN_C = 512
TILE = 512
VMEM = 24 * 1024 * 1024
PACE = 10


def routes(chips):
    last = chips - 1
    first = [(b, b + 1) for b in range(0, chips, 2) if b + 1 != last]
    first += [(b, b + 3) for b in range(1, chips, 2) if b + 3 < chips]
    first += [(last - 2, last)]
    second = [(b, b + 2) for b in range(0, chips, 2) if b + 2 < chips]
    second += [(b, b - 2) for b in range(1, chips, 2) if b >= 3]
    second += [(last - 1, last)]
    return first, second


def on_cores(pairs):
    return [(CORES * s + k, CORES * d + k) for s, d in pairs for k in range(CORES)]


def flipped(pairs):
    return [(d, s) for s, d in pairs]


RECT, SIDE, HAS, BASE, SPAN = 0, 12, 14, 16, 17


def plan_kernel(chips, chip_rows, spans, me_ref, offsets, out):
    chip, core = me_ref[0] // CORES, me_ref[0] % CORES
    rows = chip_rows // CORES
    odd = chip % 2 == 1
    at_end = chip == chips - 1
    first = jnp.where(odd, jnp.where(at_end, chip - 2, chip - 1), chip - 3)
    second = jnp.where(odd, jnp.where(at_end, chip - 1, chip + 2), chip - 2)
    starts = [b * chip_rows for b in (chip, first, second)]
    for k in range(spans):
        out[SPAN + 2 * k] = 0
        out[SPAN + 2 * k + 1] = 0

    def look(c, state):
        lower, upper = offsets[c], offsets[c + 1]
        lows, highs, count = state[:3], state[3:6], state[6]
        here = (upper > starts[0]) & (lower < starts[0] + chip_rows)

        @pl.when(here)
        def _():
            at = SPAN + 2 * jnp.minimum(count, spans - 1)
            out[at] = lower
            out[at + 1] = upper

        holds = [(lower < s + chip_rows) & (upper >= s + chip_rows) for s in starts]
        lows = [jnp.where(h, lower, v) for h, v in zip(holds, lows)]
        highs = [jnp.where(h, upper, v) for h, v in zip(holds, highs)]
        return (*lows, *highs, count + here.astype(jnp.int32))

    none = jnp.int32(-1)
    state = lax.fori_loop(0, offsets.shape[0] - 1, look, (none,) * 6 + (jnp.int32(0),))
    lows, highs = state[:3], state[3:6]
    for which, (p, q) in enumerate(((0, 1), (0, 2), (1, 2))):
        p_first = starts[p] < starts[q]
        s = jnp.where(p_first, lows[p], lows[q])
        e = jnp.where(p_first, highs[p], highs[q])
        later = jnp.where(p_first, starts[q], starts[p])
        ok = (lows[p] >= 0) & (lows[q] >= 0) & (e > later)
        for k, (b, is_first) in enumerate(((p, p_first), (q, ~p_first))):
            a = jnp.where(is_first, jnp.maximum(s - starts[b], 0), 0)
            z = jnp.where(is_first, chip_rows, jnp.minimum(e - starts[b], chip_rows))
            out[RECT + 4 * which + 2 * k] = a
            out[RECT + 4 * which + 2 * k + 1] = jnp.where(ok, z, a)
    out[SIDE] = core * rows
    out[SIDE + 1] = (1 - core) * rows
    has_first = jnp.where(odd, (chip + 3 < chips) | (chip == chips - 3), chip + 2 < chips)
    has_second = jnp.where(odd, chip >= 3, (chip + 2 < chips) | (chip == chips - 2))
    out[HAS] = has_first.astype(jnp.int32)
    out[HAS + 1] = has_second.astype(jnp.int32)
    out[BASE] = starts[0]


def join_kernel(table, own_ref, first_ref, second_ref, mine_ref, other_ref):
    first = jnp.where(table[HAS] == 1, first_ref[...], -1.0)
    second = jnp.where(table[HAS + 1] == 1, second_ref[...], -1.0)
    both = jnp.maximum(own_ref[...], first)
    mine_ref[...] = jnp.maximum(both[0:1], second)
    other_ref[...] = both[1:2]


def unit_of(raw):
    wide = raw.astype(jnp.float32)
    mean = jnp.sum(wide * wide, axis=1, keepdims=True) * (1.0 / raw.shape[1])
    factor = lax.rsqrt(mean + 1e-06) * (1.0 / math.sqrt(raw.shape[1]))
    return (wide * factor).astype(jnp.bfloat16)


def unit_kernel(first, cuts, raw_ref, *refs):
    outs, (held, sems) = refs[:-2], refs[-2:]
    step = held.shape[1]
    copies = [
        pltpu.make_async_copy(raw_ref.at[first + k * step : first + (k + 1) * step], held.at[k], sems.at[k])
        for k in range(held.shape[0])
    ]
    for copy in copies:
        copy.start()
    part = math.gcd(128, step)
    for k, copy in enumerate(copies):
        copy.wait()
        for at in range(0, step, part):
            unit = unit_of(held[k, at : at + part, :])
            for (start, n), out in zip(cuts, outs):
                row = k * step + at - start
                if 0 <= row < n:
                    out[row : row + part, :] = unit


def units_of(raw, first, count, cuts):
    depth = raw.shape[1]
    step = math.gcd(256, count)
    return pl.pallas_call(
        functools.partial(unit_kernel, first, cuts),
        in_specs=[pl.BlockSpec(memory_space=pltpu.HBM)],
        out_specs=[pl.BlockSpec(memory_space=pltpu.VMEM)] * len(cuts),
        out_shape=[jax.ShapeDtypeStruct((n, depth), jnp.bfloat16) for _, n in cuts],
        scratch_shapes=[
            pltpu.VMEM((count // step, step, depth), jnp.bfloat16),
            pltpu.SemaphoreType.DMA((count // step,)),
        ],
        compiler_params=pltpu.CompilerParams(vmem_limit_bytes=VMEM),
        cost_estimate=pl.CostEstimate(
            flops=8 * count * depth, bytes_accessed=4 * count * depth, transcendentals=0
        ),
    )(raw)


def product(left, right):
    return lax.dot_general(
        left, right, (((1,), (1,)), ((), ())), preferred_element_type=jnp.float32
    )


def lanes_max(scores):
    parts = [scores[:, j : j + 128] for j in range(0, scores.shape[1], 128)]
    return functools.reduce(jnp.maximum, parts)


def across(part):
    return jnp.max(part.T, axis=0, keepdims=True)


@dataclasses.dataclass
class Piece:
    rows: jax.Array
    block: int
    side: int
    at: int

    @property
    def n(self):
        return self.rows.shape[0]


def own_kernel(lefts, rights, table, *refs):
    refs = list(refs)
    lines = [refs.pop(0) for _ in lefts]
    fars = [refs.pop(0) for _ in rights] if rights[0].side else lines
    so_far = refs.pop(0)
    best_ref, rowpart = refs
    base = table[BASE]
    best_ref[...] = so_far[...]
    for left, left_ref in zip(lefts, lines):
        size = left_ref.shape[0]
        position = base + table[SIDE] + left.at
        position = position + lax.broadcasted_iota(jnp.int32, (size, 1), 0)
        low = jnp.zeros((size, 1), jnp.int32)
        high = jnp.zeros((size, 1), jnp.int32)
        for c in range(SPAN, table.shape[0], 2):
            here = (position >= table[c]) & (position < table[c + 1])
            low = jnp.where(here, table[c], low)
            high = jnp.where(here, table[c + 1], high)
        rowpart[...] = jnp.full(rowpart.shape, -1.0, jnp.float32)
        for right, right_ref in zip(rights, fars):
            start = base + table[SIDE + right.side] + right.at
            scores = product(left_ref[...], right_ref[...])
            column = start + lax.broadcasted_iota(jnp.int32, (1, right_ref.shape[0]), 1)
            keep = (column >= low) & (column < high) & (column != position)
            rowpart[...] = jnp.maximum(
                rowpart[...], lanes_max(jnp.where(keep, scores, -1.0))
            )
        to = (slice(0, 1), slice(left.at, left.at + size))
        best_ref[to] = jnp.maximum(best_ref[to], across(rowpart[...]))


def own_rows(table, lefts, rights, best):
    bare = lambda pieces: [dataclasses.replace(p, rows=None) for p in pieces]
    pieces = lefts + (rights if rights[0].side else [])
    work = sum(l.n for l in lefts) * sum(r.n for r in rights) * lefts[0].rows.shape[1]
    return vmem_call(
        functools.partial(own_kernel, bare(lefts), bare(rights)),
        [table] + [p.rows for p in pieces] + [best],
        [jax.ShapeDtypeStruct(best.shape, best.dtype)],
        [pltpu.VMEM((lefts[0].n, 128), jnp.float32)],
        2 * work,
    )[0]


PAIRS = {(0, 1): 0, (0, 2): 1, (1, 2): 2}


def rect(table, left, right):
    flip = left.block > right.block
    which = PAIRS[(right.block, left.block) if flip else (left.block, right.block)]
    ends = [table[RECT + 4 * which + k] for k in range(4)]
    if flip:
        ends = ends[2:] + ends[:2]
    x, y = table[SIDE + left.side] + left.at, table[SIDE + right.side] + right.at
    return ends[0] - x, ends[1] - x, ends[2] - y, ends[3] - y


def meet_kernel(pieces, groups, table, *refs):
    refs = list(refs)
    held = [refs.pop(0) for _ in pieces]
    acc_in = [refs.pop(0) for _ in range(3)]
    acc = [refs.pop(0) for _ in range(3)]
    (rowpart,) = refs
    for src, dst in zip(acc_in, acc):
        dst[...] = src[...]
    for l, partners in groups:
        left, left_ref = pieces[l], held[l]
        tm = left_ref.shape[0]
        part = rowpart.at[0:tm]
        part[...] = jnp.full(part.shape, -1.0, jnp.float32)
        for r in partners:
            right, right_ref = pieces[r], held[r]
            tn = right_ref.shape[0]
            xa, xb, ya, yb = rect(table, left, right)
            some = (xa < tm) & (xb > 0) & (ya < tn) & (yb > 0) & (xa < xb) & (ya < yb)

            @pl.when(some)
            def _():
                scores = product(left_ref[...], right_ref[...])
                row = lax.broadcasted_iota(jnp.int32, (tm, 1), 0)
                col = lax.broadcasted_iota(jnp.int32, (1, tn), 1)
                keep = ((row >= xa) & (row < xb)) & ((col >= ya) & (col < yb))
                scores = jnp.where(keep, scores, -1.0)
                part[...] = jnp.maximum(part[...], lanes_max(scores))
                to = (slice(right.side, right.side + 1), slice(right.at, right.at + tn))
                best = acc[right.block]
                best[to] = jnp.maximum(best[to], jnp.max(scores, axis=0, keepdims=True))

        to = (slice(left.side, left.side + 1), slice(left.at, left.at + tm))
        best = acc[left.block]
        best[to] = jnp.maximum(best[to], across(part[...]))


def vmem_call(kernel, ins, outs, scratch, flops):
    vm = pl.BlockSpec(memory_space=pltpu.VMEM)
    sm = pl.BlockSpec(memory_space=pltpu.SMEM)
    moved = sum(x.size * x.dtype.itemsize for x in [*ins, *outs])
    return pl.pallas_call(
        kernel,
        out_shape=outs,
        in_specs=[sm] + [vm] * (len(ins) - 1),
        out_specs=[vm] * len(outs),
        scratch_shapes=scratch,
        compiler_params=pltpu.CompilerParams(vmem_limit_bytes=VMEM),
        cost_estimate=pl.CostEstimate(flops=PACE * flops, bytes_accessed=moved, transcendentals=0),
    )(*ins)


def meet(table, pairs, acc):
    pieces, groups = [], []

    def index(piece):
        for i, other in enumerate(pieces):
            if other is piece:
                return i
        pieces.append(piece)
        return len(pieces) - 1

    for left, rights in pairs:
        groups.append((index(left), [index(r) for r in rights]))
    depth = pieces[0].rows.shape[1]
    flops = sum(2 * left.n * r.n * depth for left, rights in pairs for r in rights)
    most = max(left.n for left, _ in pairs)
    return vmem_call(
        functools.partial(
            meet_kernel, [dataclasses.replace(p, rows=None) for p in pieces], groups
        ),
        [table] + [p.rows for p in pieces] + list(acc),
        [jax.ShapeDtypeStruct(a.shape, a.dtype) for a in acc],
        [pltpu.VMEM((most, 128), jnp.float32)],
        flops,
    )


def after(value, *others):
    return lax.optimization_barrier((value, *others))[0]


def shards(embeddings, offsets):
    rows, depth = embeddings.shape
    chips = lax.axis_size(AXES) // CORES
    me = lax.axis_index(AXES)
    chip_rows = CORES * rows
    first, second = routes(chips)
    to_first, to_second = on_cores(first), on_cores(second)
    swap = [(i, i ^ 1) for i in range(CORES * chips)]
    send = lambda x, pairs: lax.ppermute(x, AXES, pairs)

    half, most = rows // 2, rows * 3 // 4
    u1, w1 = units_of(embeddings, 0, most, [(0, half), (0, most)])
    a1, b1 = send(u1, to_first), send(w1, to_second)
    far1 = send(u1, swap)
    later = after(embeddings, far1)
    u2, w2 = units_of(later, half, rows - half, [(0, rows - half), (most - half, rows - most)])
    a2, b2 = send(u2, to_first), send(w2, to_second)
    far2 = send(u2, swap)

    spans = chip_rows // MIN_C + 2
    scalars = pl.BlockSpec(memory_space=pltpu.SMEM)
    table = pl.pallas_call(
        functools.partial(plan_kernel, chips, chip_rows, spans),
        out_shape=jax.ShapeDtypeStruct((SPAN + 2 * spans,), jnp.int32),
        in_specs=[scalars] * 2,
        out_specs=scalars,
    )(me.reshape(1).astype(jnp.int32), offsets)

    own = [Piece(u1, 0, 0, 0), Piece(u2, 0, 0, half)]
    far = [Piece(far1, 0, 1, 0), Piece(far2, 0, 1, half)]
    blank = jnp.full((CORES, rows), -1.0, jnp.float32)
    best_near = own_rows(table, own, own, blank)
    best_own = own_rows(table, own, far, best_near)
    acc = [best_own, blank, blank[:1]]
    chip_own = own + far

    pa1, pb1 = Piece(a1, 1, 0, 0), Piece(b1, 2, 0, 0)
    pax1 = Piece(send(after(a1, best_near), swap), 1, 1, 0)
    acc = meet(table, [(pa1, chip_own), (pb1, chip_own + [pa1])], acc)
    acc = meet(table, [(pb1, [pax1])], acc)

    pa2, pb2 = Piece(a2, 1, 0, half), Piece(b2, 2, 0, most)
    pax2 = Piece(send(after(a2, acc[0]), swap), 1, 1, half)
    acc = meet(table, [(pa2, chip_own + [pb1])], acc)
    acc = meet(
        table, [(pb2, chip_own + [pa1, pax1, pa2, pax2]), (pax2, [pb1])], acc
    )

    best_own, best_first, best_second = acc
    from_first = send(best_first, on_cores(flipped(first)))
    from_second = send(best_second, on_cores(flipped(second)))
    line = jax.ShapeDtypeStruct((1, rows), jnp.float32)
    mine, other = vmem_call(
        join_kernel, [table, best_own, from_first, from_second], [line] * 2, [], rows
    )
    return jnp.maximum(mine, send(other, swap)).reshape(rows)


def solution(mesh):
    return jax.shard_map(
        shards,
        mesh=mesh,
        in_specs=(P(AXES, None), P()),
        out_specs=P(AXES),
        check_vma=False,
    )
```

```python
import dataclasses
import functools
import math

import jax
import jax.numpy as jnp
from jax import lax
from jax.experimental import pallas as pl
from jax.experimental.pallas import tpu as pltpu
from jax.sharding import PartitionSpec as P

AXES = ("grp", "work")
CORES = 2
MIN_C = 512
TILE = 512
VMEM = 24 * 1024 * 1024
UNIT_VMEM = 58 * 1024 * 1024
PACE = 10


def routes(chips):
    last = chips - 1
    first = [(b, b + 1) for b in range(0, chips, 2) if b + 1 != last]
    first += [(b, b + 3) for b in range(1, chips, 2) if b + 3 < chips]
    first += [(last - 2, last)]
    second = [(b, b + 2) for b in range(0, chips, 2) if b + 2 < chips]
    second += [(b, b - 2) for b in range(1, chips, 2) if b >= 3]
    second += [(last - 1, last)]
    return first, second


def on_cores(pairs):
    return [(CORES * s + k, CORES * d + k) for s, d in pairs for k in range(CORES)]


def flipped(pairs):
    return [(d, s) for s, d in pairs]


RECT, SIDE, HAS, BASE, SPAN = 0, 12, 14, 16, 17


def plan_kernel(chips, chip_rows, spans, me_ref, offsets, out):
    chip, core = me_ref[0] // CORES, me_ref[0] % CORES
    rows = chip_rows // CORES
    odd = chip % 2 == 1
    at_end = chip == chips - 1
    first = jnp.where(odd, jnp.where(at_end, chip - 2, chip - 1), chip - 3)
    second = jnp.where(odd, jnp.where(at_end, chip - 1, chip + 2), chip - 2)
    starts = [b * chip_rows for b in (chip, first, second)]
    for k in range(spans):
        out[SPAN + 2 * k] = 0
        out[SPAN + 2 * k + 1] = 0

    def look(c, state):
        lower, upper = offsets[c], offsets[c + 1]
        lows, highs, count = state[:3], state[3:6], state[6]
        here = (upper > starts[0]) & (lower < starts[0] + chip_rows)

        @pl.when(here)
        def _():
            at = SPAN + 2 * jnp.minimum(count, spans - 1)
            out[at] = lower
            out[at + 1] = upper

        holds = [(lower < s + chip_rows) & (upper >= s + chip_rows) for s in starts]
        lows = [jnp.where(h, lower, v) for h, v in zip(holds, lows)]
        highs = [jnp.where(h, upper, v) for h, v in zip(holds, highs)]
        return (*lows, *highs, count + here.astype(jnp.int32))

    none = jnp.int32(-1)
    state = lax.fori_loop(0, offsets.shape[0] - 1, look, (none,) * 6 + (jnp.int32(0),))
    lows, highs = state[:3], state[3:6]
    for which, (p, q) in enumerate(((0, 1), (0, 2), (1, 2))):
        p_first = starts[p] < starts[q]
        s = jnp.where(p_first, lows[p], lows[q])
        e = jnp.where(p_first, highs[p], highs[q])
        later = jnp.where(p_first, starts[q], starts[p])
        ok = (lows[p] >= 0) & (lows[q] >= 0) & (e > later)
        for k, (b, is_first) in enumerate(((p, p_first), (q, ~p_first))):
            a = jnp.where(is_first, jnp.maximum(s - starts[b], 0), 0)
            z = jnp.where(is_first, chip_rows, jnp.minimum(e - starts[b], chip_rows))
            out[RECT + 4 * which + 2 * k] = a
            out[RECT + 4 * which + 2 * k + 1] = jnp.where(ok, z, a)
    out[SIDE] = core * rows
    out[SIDE + 1] = (1 - core) * rows
    has_first = jnp.where(odd, (chip + 3 < chips) | (chip == chips - 3), chip + 2 < chips)
    has_second = jnp.where(odd, chip >= 3, (chip + 2 < chips) | (chip == chips - 2))
    out[HAS] = has_first.astype(jnp.int32)
    out[HAS + 1] = has_second.astype(jnp.int32)
    out[BASE] = starts[0]


def join_kernel(table, own_ref, first_ref, second_ref, mine_ref, other_ref):
    first = jnp.where(table[HAS] == 1, first_ref[...], -1.0)
    second = jnp.where(table[HAS + 1] == 1, second_ref[...], -1.0)
    both = jnp.maximum(own_ref[...], first)
    mine_ref[...] = jnp.maximum(both[0:1], second)
    other_ref[...] = both[1:2]


def unit_of(raw):
    wide = raw.astype(jnp.float32)
    mean = jnp.sum(wide * wide, axis=1, keepdims=True) * (1.0 / raw.shape[1])
    factor = lax.rsqrt(mean + 1e-06) * (1.0 / math.sqrt(raw.shape[1]))
    return (wide * factor).astype(jnp.bfloat16)


def unit_kernel(raw_ref, out):
    rows = raw_ref.shape[0]
    step = math.gcd(128, rows)
    for at in range(0, rows, step):
        out[at : at + step, :] = unit_of(raw_ref[at : at + step, :])


def units_of(raw, which, count):
    depth = raw.shape[1]
    return pl.pallas_call(
        unit_kernel,
        grid=(1,),
        in_specs=[pl.BlockSpec((count, depth), lambda i: (which, 0))],
        out_specs=pl.BlockSpec((count, depth), lambda i: (0, 0)),
        out_shape=jax.ShapeDtypeStruct((count, depth), jnp.bfloat16),
        compiler_params=pltpu.CompilerParams(vmem_limit_bytes=UNIT_VMEM),
        cost_estimate=pl.CostEstimate(
            flops=8 * count * depth, bytes_accessed=4 * count * depth, transcendentals=0
        ),
    )(raw)


def product(left, right):
    return lax.dot_general(
        left, right, (((1,), (1,)), ((), ())), preferred_element_type=jnp.float32
    )


def lanes_max(scores):
    parts = [scores[:, j : j + 128] for j in range(0, scores.shape[1], 128)]
    return functools.reduce(jnp.maximum, parts)


def across(part):
    return jnp.max(part.T, axis=0, keepdims=True)


@dataclasses.dataclass
class Piece:
    rows: jax.Array
    block: int
    side: int
    at: int

    @property
    def n(self):
        return self.rows.shape[0]


def own_kernel(lefts, rights, table, *refs):
    refs = list(refs)
    lines = [refs.pop(0) for _ in lefts]
    fars = [refs.pop(0) for _ in rights] if rights[0].side else lines
    so_far = refs.pop(0)
    best_ref, rowpart = refs
    base = table[BASE]
    best_ref[...] = so_far[...]
    for left, left_ref in zip(lefts, lines):
        size = left_ref.shape[0]
        position = base + table[SIDE] + left.at
        position = position + lax.broadcasted_iota(jnp.int32, (size, 1), 0)
        low = jnp.zeros((size, 1), jnp.int32)
        high = jnp.zeros((size, 1), jnp.int32)
        for c in range(SPAN, table.shape[0], 2):
            here = (position >= table[c]) & (position < table[c + 1])
            low = jnp.where(here, table[c], low)
            high = jnp.where(here, table[c + 1], high)
        part = rowpart.at[0:size]
        part[...] = jnp.full(part.shape, -1.0, jnp.float32)
        for right, right_ref in zip(rights, fars):
            start = base + table[SIDE + right.side] + right.at
            scores = product(left_ref[...], right_ref[...])
            column = start + lax.broadcasted_iota(jnp.int32, (1, right_ref.shape[0]), 1)
            keep = (column >= low) & (column < high) & (column != position)
            part[...] = jnp.maximum(part[...], lanes_max(jnp.where(keep, scores, -1.0)))
        to = (slice(0, 1), slice(left.at, left.at + size))
        best_ref[to] = jnp.maximum(best_ref[to], across(part[...]))


def own_rows(table, lefts, rights, best):
    bare = lambda pieces: [dataclasses.replace(p, rows=None) for p in pieces]
    pieces = lefts + (rights if rights[0].side else [])
    work = sum(l.n for l in lefts) * sum(r.n for r in rights) * lefts[0].rows.shape[1]
    return vmem_call(
        functools.partial(own_kernel, bare(lefts), bare(rights)),
        [table] + [p.rows for p in pieces] + [best],
        [jax.ShapeDtypeStruct(best.shape, best.dtype)],
        [pltpu.VMEM((lefts[0].n, 128), jnp.float32)],
        2 * work,
    )[0]


PAIRS = {(0, 1): 0, (0, 2): 1, (1, 2): 2}


def rect(table, left, right):
    flip = left.block > right.block
    which = PAIRS[(right.block, left.block) if flip else (left.block, right.block)]
    ends = [table[RECT + 4 * which + k] for k in range(4)]
    if flip:
        ends = ends[2:] + ends[:2]
    x, y = table[SIDE + left.side] + left.at, table[SIDE + right.side] + right.at
    return ends[0] - x, ends[1] - x, ends[2] - y, ends[3] - y


def meet_kernel(pieces, groups, table, *refs):
    refs = list(refs)
    held = [refs.pop(0) for _ in pieces]
    acc_in = [refs.pop(0) for _ in range(3)]
    acc = [refs.pop(0) for _ in range(3)]
    (rowpart,) = refs
    for src, dst in zip(acc_in, acc):
        dst[...] = src[...]
    for l, partners in groups:
        left, left_ref = pieces[l], held[l]
        tm = left_ref.shape[0]
        part = rowpart.at[0:tm]
        part[...] = jnp.full(part.shape, -1.0, jnp.float32)
        for r in partners:
            right, right_ref = pieces[r], held[r]
            tn = right_ref.shape[0]
            xa, xb, ya, yb = rect(table, left, right)
            some = (xa < tm) & (xb > 0) & (ya < tn) & (yb > 0) & (xa < xb) & (ya < yb)

            @pl.when(some)
            def _():
                scores = product(left_ref[...], right_ref[...])
                row = lax.broadcasted_iota(jnp.int32, (tm, 1), 0)
                col = lax.broadcasted_iota(jnp.int32, (1, tn), 1)
                keep = ((row >= xa) & (row < xb)) & ((col >= ya) & (col < yb))
                scores = jnp.where(keep, scores, -1.0)
                part[...] = jnp.maximum(part[...], lanes_max(scores))
                to = (slice(right.side, right.side + 1), slice(right.at, right.at + tn))
                best = acc[right.block]
                best[to] = jnp.maximum(best[to], jnp.max(scores, axis=0, keepdims=True))

        to = (slice(left.side, left.side + 1), slice(left.at, left.at + tm))
        best = acc[left.block]
        best[to] = jnp.maximum(best[to], across(part[...]))


def vmem_call(kernel, ins, outs, scratch, flops):
    vm = pl.BlockSpec(memory_space=pltpu.VMEM)
    sm = pl.BlockSpec(memory_space=pltpu.SMEM)
    moved = sum(x.size * x.dtype.itemsize for x in [*ins, *outs])
    return pl.pallas_call(
        kernel,
        out_shape=outs,
        in_specs=[sm] + [vm] * (len(ins) - 1),
        out_specs=[vm] * len(outs),
        scratch_shapes=scratch,
        compiler_params=pltpu.CompilerParams(vmem_limit_bytes=VMEM),
        cost_estimate=pl.CostEstimate(flops=PACE * flops, bytes_accessed=moved, transcendentals=0),
    )(*ins)


def meet(table, pairs, acc):
    pieces, groups = [], []

    def index(piece):
        for i, other in enumerate(pieces):
            if other is piece:
                return i
        pieces.append(piece)
        return len(pieces) - 1

    for left, rights in pairs:
        groups.append((index(left), [index(r) for r in rights]))
    depth = pieces[0].rows.shape[1]
    flops = sum(2 * left.n * r.n * depth for left, rights in pairs for r in rights)
    most = max(left.n for left, _ in pairs)
    return vmem_call(
        functools.partial(
            meet_kernel, [dataclasses.replace(p, rows=None) for p in pieces], groups
        ),
        [table] + [p.rows for p in pieces] + list(acc),
        [jax.ShapeDtypeStruct(a.shape, a.dtype) for a in acc],
        [pltpu.VMEM((most, 128), jnp.float32)],
        flops,
    )


def after(value, *others):
    return lax.optimization_barrier((value, *others))[0]


def shards(embeddings, offsets):
    rows, depth = embeddings.shape
    chips = lax.axis_size(AXES) // CORES
    me = lax.axis_index(AXES)
    chip_rows = CORES * rows
    first, second = routes(chips)
    to_first, to_second = on_cores(first), on_cores(second)
    swap = [(i, i ^ 1) for i in range(CORES * chips)]
    send = lambda x, pairs: lax.ppermute(x, AXES, pairs)

    spans = chip_rows // MIN_C + 2
    scalars = pl.BlockSpec(memory_space=pltpu.SMEM)
    table = pl.pallas_call(
        functools.partial(plan_kernel, chips, chip_rows, spans),
        out_shape=jax.ShapeDtypeStruct((SPAN + 2 * spans,), jnp.int32),
        in_specs=[scalars] * 2,
        out_specs=scalars,
    )(me.reshape(1).astype(jnp.int32), offsets)

    most = rows * 3 // 4
    u1 = units_of(embeddings, 0, most)
    a1, b1 = send(u1, to_first), send(u1, to_second)
    far1 = send(u1, swap)
    u2 = units_of(after(embeddings, far1), most // (rows - most), rows - most)
    a2, b2 = send(u2, to_first), send(u2, to_second)
    far2 = send(u2, swap)

    own = [Piece(u1, 0, 0, 0), Piece(u2, 0, 0, most)]
    far = [Piece(far1, 0, 1, 0), Piece(far2, 0, 1, most)]
    blank = jnp.full((CORES, rows), -1.0, jnp.float32)
    best_near = own_rows(table, own, own, blank)
    best_own = own_rows(table, own, far, best_near)
    acc = [best_own, blank, blank[:1]]
    chip_own = own + far

    pa1, pb1 = Piece(a1, 1, 0, 0), Piece(b1, 2, 0, 0)
    pax1 = Piece(send(after(a1, best_near), swap), 1, 1, 0)
    acc = meet(table, [(pa1, chip_own)], acc)
    acc = meet(table, [(pb1, chip_own + [pa1, pax1])], acc)

    pa2, pb2 = Piece(a2, 1, 0, most), Piece(b2, 2, 0, most)
    pax2 = Piece(send(after(a2, acc[0]), swap), 1, 1, most)
    acc = meet(table, [(pa2, chip_own + [pb1])], acc)
    acc = meet(
        table, [(pb2, chip_own + [pa1, pax1, pa2, pax2]), (pax2, [pb1])], acc
    )

    best_own, best_first, best_second = acc
    from_first = send(best_first, on_cores(flipped(first)))
    from_second = send(best_second, on_cores(flipped(second)))
    line = jax.ShapeDtypeStruct((1, rows), jnp.float32)
    mine, other = vmem_call(
        join_kernel, [table, best_own, from_first, from_second], [line] * 2, [], rows
    )
    return jnp.maximum(mine, send(other, swap)).reshape(rows)


def solution(mesh):
    return jax.shard_map(
        shards,
        mesh=mesh,
        in_specs=(P(AXES, None), P()),
        out_specs=P(AXES),
        check_vma=False,
    )
```

```python
import dataclasses
import functools
import math

import jax
import jax.numpy as jnp
from jax import lax
from jax.experimental import pallas as pl
from jax.experimental.pallas import tpu as pltpu
from jax.sharding import PartitionSpec as P

AXES = ("grp", "work")
CORES = 2
MIN_C = 512
TILE = 512
VMEM = 16 * 1024 * 1024
PACE = 10


def routes(chips):
    last = chips - 1
    first = [(b, b + 1) for b in range(0, chips, 2) if b + 1 != last]
    first += [(b, b + 3) for b in range(1, chips, 2) if b + 3 < chips]
    first += [(last - 2, last)]
    second = [(b, b + 2) for b in range(0, chips, 2) if b + 2 < chips]
    second += [(b, b - 2) for b in range(1, chips, 2) if b >= 3]
    second += [(last - 1, last)]
    return first, second


def on_cores(pairs):
    return [(CORES * s + k, CORES * d + k) for s, d in pairs for k in range(CORES)]


def flipped(pairs):
    return [(d, s) for s, d in pairs]


RECT, SIDE, HAS, BASE, SPAN = 0, 12, 14, 16, 17


def plan_kernel(chips, chip_rows, spans, me_ref, offsets, out):
    chip, core = me_ref[0] // CORES, me_ref[0] % CORES
    rows = chip_rows // CORES
    odd = chip % 2 == 1
    at_end = chip == chips - 1
    first = jnp.where(odd, jnp.where(at_end, chip - 2, chip - 1), chip - 3)
    second = jnp.where(odd, jnp.where(at_end, chip - 1, chip + 2), chip - 2)
    starts = [b * chip_rows for b in (chip, first, second)]
    for k in range(spans):
        out[SPAN + 2 * k] = 0
        out[SPAN + 2 * k + 1] = 0

    def look(c, state):
        lower, upper = offsets[c], offsets[c + 1]
        lows, highs, count = state[:3], state[3:6], state[6]
        here = (upper > starts[0]) & (lower < starts[0] + chip_rows)

        @pl.when(here)
        def _():
            at = SPAN + 2 * jnp.minimum(count, spans - 1)
            out[at] = lower
            out[at + 1] = upper

        holds = [(lower < s + chip_rows) & (upper >= s + chip_rows) for s in starts]
        lows = [jnp.where(h, lower, v) for h, v in zip(holds, lows)]
        highs = [jnp.where(h, upper, v) for h, v in zip(holds, highs)]
        return (*lows, *highs, count + here.astype(jnp.int32))

    none = jnp.int32(-1)
    state = lax.fori_loop(0, offsets.shape[0] - 1, look, (none,) * 6 + (jnp.int32(0),))
    lows, highs = state[:3], state[3:6]
    for which, (p, q) in enumerate(((0, 1), (0, 2), (1, 2))):
        p_first = starts[p] < starts[q]
        s = jnp.where(p_first, lows[p], lows[q])
        e = jnp.where(p_first, highs[p], highs[q])
        later = jnp.where(p_first, starts[q], starts[p])
        ok = (lows[p] >= 0) & (lows[q] >= 0) & (e > later)
        for k, (b, is_first) in enumerate(((p, p_first), (q, ~p_first))):
            a = jnp.where(is_first, jnp.maximum(s - starts[b], 0), 0)
            z = jnp.where(is_first, chip_rows, jnp.minimum(e - starts[b], chip_rows))
            out[RECT + 4 * which + 2 * k] = a
            out[RECT + 4 * which + 2 * k + 1] = jnp.where(ok, z, a)
    out[SIDE] = core * rows
    out[SIDE + 1] = (1 - core) * rows
    has_first = jnp.where(odd, (chip + 3 < chips) | (chip == chips - 3), chip + 2 < chips)
    has_second = jnp.where(odd, chip >= 3, (chip + 2 < chips) | (chip == chips - 2))
    out[HAS] = has_first.astype(jnp.int32)
    out[HAS + 1] = has_second.astype(jnp.int32)
    out[BASE] = starts[0]


def join_kernel(table, own_ref, first_ref, second_ref, mine_ref, other_ref):
    first = jnp.where(table[HAS] == 1, first_ref[...], -1.0)
    second = jnp.where(table[HAS + 1] == 1, second_ref[...], -1.0)
    both = jnp.maximum(own_ref[...], first)
    mine_ref[...] = jnp.maximum(both[0:1], second)
    other_ref[...] = both[1:2]


def unit_of(raw):
    wide = raw.astype(jnp.float32)
    mean = jnp.sum(wide * wide, axis=1, keepdims=True) * (1.0 / raw.shape[1])
    factor = lax.rsqrt(mean + 1e-06) * (1.0 / math.sqrt(raw.shape[1]))
    return (wide * factor).astype(jnp.bfloat16)


def unit_kernel(raw_ref, out):
    rows = raw_ref.shape[0]
    step = math.gcd(128, rows)
    for at in range(0, rows, step):
        out[at : at + step, :] = unit_of(raw_ref[at : at + step, :])


def units_of(raw, which, count):
    depth = raw.shape[1]
    return pl.pallas_call(
        unit_kernel,
        grid=(1,),
        in_specs=[pl.BlockSpec((count, depth), lambda i: (which, 0))],
        out_specs=pl.BlockSpec((count, depth), lambda i: (0, 0)),
        out_shape=jax.ShapeDtypeStruct((count, depth), jnp.bfloat16),
        compiler_params=pltpu.CompilerParams(vmem_limit_bytes=VMEM),
        cost_estimate=pl.CostEstimate(
            flops=8 * count * depth, bytes_accessed=4 * count * depth, transcendentals=0
        ),
    )(raw)


def product(left, right):
    return lax.dot_general(
        left, right, (((1,), (1,)), ((), ())), preferred_element_type=jnp.float32
    )


def lanes_max(scores):
    parts = [scores[:, j : j + 128] for j in range(0, scores.shape[1], 128)]
    return functools.reduce(jnp.maximum, parts)


def across(part):
    return jnp.max(part.T, axis=0, keepdims=True)


@dataclasses.dataclass
class Piece:
    rows: jax.Array
    block: int
    side: int
    at: int

    @property
    def n(self):
        return self.rows.shape[0]


def own_kernel(lefts, rights, table, *refs):
    refs = list(refs)
    lines = [refs.pop(0) for _ in lefts]
    fars = [refs.pop(0) for _ in rights] if rights[0].side else lines
    so_far = refs.pop(0)
    best_ref, rowpart = refs
    base = table[BASE]
    best_ref[...] = so_far[...]
    for left, left_ref in zip(lefts, lines):
        size = left_ref.shape[0]
        position = base + table[SIDE] + left.at
        position = position + lax.broadcasted_iota(jnp.int32, (size, 1), 0)
        low = jnp.zeros((size, 1), jnp.int32)
        high = jnp.zeros((size, 1), jnp.int32)
        for c in range(SPAN, table.shape[0], 2):
            here = (position >= table[c]) & (position < table[c + 1])
            low = jnp.where(here, table[c], low)
            high = jnp.where(here, table[c + 1], high)
        part = rowpart.at[0:size]
        part[...] = jnp.full(part.shape, -1.0, jnp.float32)
        for right, right_ref in zip(rights, fars):
            start = base + table[SIDE + right.side] + right.at
            scores = product(left_ref[...], right_ref[...])
            column = start + lax.broadcasted_iota(jnp.int32, (1, right_ref.shape[0]), 1)
            keep = (column >= low) & (column < high) & (column != position)
            part[...] = jnp.maximum(part[...], lanes_max(jnp.where(keep, scores, -1.0)))
        to = (slice(0, 1), slice(left.at, left.at + size))
        best_ref[to] = jnp.maximum(best_ref[to], across(part[...]))


def own_rows(table, lefts, rights, best):
    bare = lambda pieces: [dataclasses.replace(p, rows=None) for p in pieces]
    pieces = lefts + (rights if rights[0].side else [])
    work = sum(l.n for l in lefts) * sum(r.n for r in rights) * lefts[0].rows.shape[1]
    return vmem_call(
        functools.partial(own_kernel, bare(lefts), bare(rights)),
        [table] + [p.rows for p in pieces] + [best],
        [jax.ShapeDtypeStruct(best.shape, best.dtype)],
        [pltpu.VMEM((lefts[0].n, 128), jnp.float32)],
        2 * work,
    )[0]


PAIRS = {(0, 1): 0, (0, 2): 1, (1, 2): 2}


def rect(table, left, right):
    flip = left.block > right.block
    which = PAIRS[(right.block, left.block) if flip else (left.block, right.block)]
    ends = [table[RECT + 4 * which + k] for k in range(4)]
    if flip:
        ends = ends[2:] + ends[:2]
    x, y = table[SIDE + left.side] + left.at, table[SIDE + right.side] + right.at
    return ends[0] - x, ends[1] - x, ends[2] - y, ends[3] - y


def meet_kernel(pieces, groups, table, *refs):
    refs = list(refs)
    held = [refs.pop(0) for _ in pieces]
    acc_in = [refs.pop(0) for _ in range(3)]
    acc = [refs.pop(0) for _ in range(3)]
    (rowpart,) = refs
    for src, dst in zip(acc_in, acc):
        dst[...] = src[...]
    for l, partners in groups:
        left, left_ref = pieces[l], held[l]
        tm = left_ref.shape[0]
        part = rowpart.at[0:tm]
        part[...] = jnp.full(part.shape, -1.0, jnp.float32)
        shares = {}
        for r in partners:
            shares.setdefault((pieces[r].block, pieces[r].side), []).append(r)
        used = jnp.bool_(False)
        for share in shares.values():
            some = jnp.bool_(False)
            for r in share:
                xa, xb, ya, yb = rect(table, left, pieces[r])
                tn = held[r].shape[0]
                some |= (xa < tm) & (xb > 0) & (ya < tn) & (yb > 0) & (xa < xb) & (ya < yb)
            used |= some

            @pl.when(some)
            def _():
                for r in share:
                    right, right_ref = pieces[r], held[r]
                    tn = right_ref.shape[0]
                    xa, xb, ya, yb = rect(table, left, right)
                    scores = product(left_ref[...], right_ref[...])
                    row = lax.broadcasted_iota(jnp.int32, (tm, 1), 0)
                    col = lax.broadcasted_iota(jnp.int32, (1, tn), 1)
                    keep = ((row >= xa) & (row < xb)) & ((col >= ya) & (col < yb))
                    scores = jnp.where(keep, scores, -1.0)
                    part[...] = jnp.maximum(part[...], lanes_max(scores))
                    to = (slice(right.side, right.side + 1), slice(right.at, right.at + tn))
                    best = acc[right.block]
                    best[to] = jnp.maximum(best[to], jnp.max(scores, axis=0, keepdims=True))

        @pl.when(used)
        def _():
            to = (slice(left.side, left.side + 1), slice(left.at, left.at + tm))
            best = acc[left.block]
            best[to] = jnp.maximum(best[to], across(part[...]))


def vmem_call(kernel, ins, outs, scratch, flops):
    vm = pl.BlockSpec(memory_space=pltpu.VMEM)
    sm = pl.BlockSpec(memory_space=pltpu.SMEM)
    ins = ins[:1] + [pltpu.with_memory_space_constraint(x, pltpu.VMEM) for x in ins[1:]]
    moved = sum(x.size * x.dtype.itemsize for x in [*ins, *outs])
    return pl.pallas_call(
        kernel,
        out_shape=outs,
        in_specs=[sm] + [vm] * (len(ins) - 1),
        out_specs=[vm] * len(outs),
        scratch_shapes=scratch,
        compiler_params=pltpu.CompilerParams(vmem_limit_bytes=VMEM),
        cost_estimate=pl.CostEstimate(flops=PACE * flops, bytes_accessed=moved, transcendentals=0),
    )(*ins)


def meet(table, pairs, acc):
    pieces, groups = [], []

    def index(piece):
        for i, other in enumerate(pieces):
            if other is piece:
                return i
        pieces.append(piece)
        return len(pieces) - 1

    for left, rights in pairs:
        groups.append((index(left), [index(r) for r in rights]))
    depth = pieces[0].rows.shape[1]
    flops = sum(2 * left.n * r.n * depth for left, rights in pairs for r in rights)
    most = max(left.n for left, _ in pairs)
    return vmem_call(
        functools.partial(
            meet_kernel, [dataclasses.replace(p, rows=None) for p in pieces], groups
        ),
        [table] + [p.rows for p in pieces] + list(acc),
        [jax.ShapeDtypeStruct(a.shape, a.dtype) for a in acc],
        [pltpu.VMEM((most, 128), jnp.float32)],
        flops,
    )


def after(value, *others):
    return lax.optimization_barrier((value, *others))[0]


def shards(embeddings, offsets):
    rows, depth = embeddings.shape
    chips = lax.axis_size(AXES) // CORES
    me = lax.axis_index(AXES)
    chip_rows = CORES * rows
    first, second = routes(chips)
    to_first, to_second = on_cores(first), on_cores(second)
    swap = [(i, i ^ 1) for i in range(CORES * chips)]
    send = lambda x, pairs: lax.ppermute(x, AXES, pairs)

    spans = chip_rows // MIN_C + 2
    scalars = pl.BlockSpec(memory_space=pltpu.SMEM)
    table = pl.pallas_call(
        functools.partial(plan_kernel, chips, chip_rows, spans),
        out_shape=jax.ShapeDtypeStruct((SPAN + 2 * spans,), jnp.int32),
        in_specs=[scalars] * 2,
        out_specs=scalars,
    )(me.reshape(1).astype(jnp.int32), offsets)

    most = rows * 3 // 4
    u1 = units_of(embeddings, 0, most)
    a1, b1 = send(u1, to_first), send(u1, to_second)
    far1 = send(u1, swap)
    u2 = units_of(after(embeddings, far1), most // (rows - most), rows - most)
    a2, b2 = send(u2, to_first), send(u2, to_second)
    far2 = send(u2, swap)

    own = [Piece(u1, 0, 0, 0), Piece(u2, 0, 0, most)]
    far = [Piece(far1, 0, 1, 0), Piece(far2, 0, 1, most)]
    blank = jnp.full((CORES, rows), -1.0, jnp.float32)
    best_near = own_rows(table, own, own, blank)
    best_own = own_rows(table, own, far, best_near)
    acc = [best_own, blank, blank[:1]]
    chip_own = own + far

    pa1, pb1 = Piece(a1, 1, 0, 0), Piece(b1, 2, 0, 0)
    pax1 = Piece(send(after(a1, best_own), swap), 1, 1, 0)
    acc = meet(table, [(pa1, chip_own)], acc)
    acc = meet(table, [(pb1, chip_own + [pa1, pax1])], acc)

    pa2, pb2 = Piece(a2, 1, 0, most), Piece(b2, 2, 0, most)
    pax2 = Piece(send(after(a2, acc[0]), swap), 1, 1, most)
    acc = meet(table, [(pa2, chip_own + [pb1])], acc)
    acc = meet(
        table, [(pb2, chip_own + [pa1, pax1, pa2, pax2]), (pax2, [pb1])], acc
    )

    best_own, best_first, best_second = acc
    from_first = send(best_first, on_cores(flipped(first)))
    from_second = send(best_second, on_cores(flipped(second)))
    line = jax.ShapeDtypeStruct((1, rows), jnp.float32)
    mine, other = vmem_call(
        join_kernel, [table, best_own, from_first, from_second], [line] * 2, [], rows
    )
    return jnp.maximum(mine, send(other, swap)).reshape(rows)


def solution(mesh):
    return jax.shard_map(
        shards,
        mesh=mesh,
        in_specs=(P(AXES, None), P()),
        out_specs=P(AXES),
        check_vma=False,
    )
```

```python
import dataclasses
import functools
import math

import jax
import jax.numpy as jnp
from jax import lax
from jax.experimental import pallas as pl
from jax.experimental.pallas import tpu as pltpu
from jax.sharding import PartitionSpec as P

AXES = ("grp", "work")
CORES = 2
MIN_C = 512
TILE = 512
VMEM = 16 * 1024 * 1024
PLAN_VMEM = 1024 * 1024
PACE = 10


def routes(chips):
    last = chips - 1
    first = [(b, b + 1) for b in range(0, chips, 2) if b + 1 != last]
    first += [(b, b + 3) for b in range(1, chips, 2) if b + 3 < chips]
    first += [(last - 2, last)]
    second = [(b, b + 2) for b in range(0, chips, 2) if b + 2 < chips]
    second += [(b, b - 2) for b in range(1, chips, 2) if b >= 3]
    second += [(last - 1, last)]
    return first, second


def on_cores(pairs):
    return [(CORES * s + k, CORES * d + k) for s, d in pairs for k in range(CORES)]


def flipped(pairs):
    return [(d, s) for s, d in pairs]


RECT, SIDE, HAS, BASE, SPAN = 0, 12, 14, 16, 17


def plan_kernel(chips, chip_rows, spans, offsets, out):
    me = lax.axis_index(AXES)
    chip, core = lax.div(me, CORES), lax.rem(me, CORES)
    rows = chip_rows // CORES
    odd = lax.rem(chip, 2) == 1
    at_end = chip == chips - 1
    first = jnp.where(odd, jnp.where(at_end, chip - 2, chip - 1), chip - 3)
    second = jnp.where(odd, jnp.where(at_end, chip - 1, chip + 2), chip - 2)
    starts = [b * chip_rows for b in (chip, first, second)]
    for k in range(spans):
        out[SPAN + 2 * k] = 0
        out[SPAN + 2 * k + 1] = 0

    def look(c, state):
        lower, upper = offsets[c], offsets[c + 1]
        lows, highs, count = state[:3], state[3:6], state[6]
        here = (upper > starts[0]) & (lower < starts[0] + chip_rows)

        @pl.when(here)
        def _():
            at = SPAN + 2 * jnp.minimum(count, spans - 1)
            out[at] = lower
            out[at + 1] = upper

        holds = [(lower < s + chip_rows) & (upper >= s + chip_rows) for s in starts]
        lows = [jnp.where(h, lower, v) for h, v in zip(holds, lows)]
        highs = [jnp.where(h, upper, v) for h, v in zip(holds, highs)]
        return (*lows, *highs, count + here.astype(jnp.int32))

    none = jnp.int32(-1)
    state = lax.fori_loop(0, offsets.shape[0] - 1, look, (none,) * 6 + (jnp.int32(0),))
    lows, highs = state[:3], state[3:6]
    for which, (p, q) in enumerate(((0, 1), (0, 2), (1, 2))):
        p_first = starts[p] < starts[q]
        s = jnp.where(p_first, lows[p], lows[q])
        e = jnp.where(p_first, highs[p], highs[q])
        later = jnp.where(p_first, starts[q], starts[p])
        ok = (lows[p] >= 0) & (lows[q] >= 0) & (e > later)
        for k, (b, is_first) in enumerate(((p, p_first), (q, ~p_first))):
            a = jnp.where(is_first, jnp.maximum(s - starts[b], 0), 0)
            z = jnp.where(is_first, chip_rows, jnp.minimum(e - starts[b], chip_rows))
            out[RECT + 4 * which + 2 * k] = a
            out[RECT + 4 * which + 2 * k + 1] = jnp.where(ok, z, a)
    out[SIDE] = core * rows
    out[SIDE + 1] = (1 - core) * rows
    has_first = jnp.where(odd, (chip + 3 < chips) | (chip == chips - 3), chip + 2 < chips)
    has_second = jnp.where(odd, chip >= 3, (chip + 2 < chips) | (chip == chips - 2))
    out[HAS] = has_first.astype(jnp.int32)
    out[HAS + 1] = has_second.astype(jnp.int32)
    out[BASE] = starts[0]


def join_kernel(table, own_ref, first_ref, second_ref, mine_ref, other_ref):
    first = jnp.where(table[HAS] == 1, first_ref[...], -1.0)
    second = jnp.where(table[HAS + 1] == 1, second_ref[...], -1.0)
    both = jnp.maximum(own_ref[...], first)
    mine_ref[...] = jnp.maximum(both[0:1], second)
    other_ref[...] = both[1:2]


def unit_of(raw):
    wide = raw.astype(jnp.float32)
    mean = jnp.sum(wide * wide, axis=1, keepdims=True) * (1.0 / raw.shape[1])
    factor = lax.rsqrt(mean + 1e-06) * (1.0 / math.sqrt(raw.shape[1]))
    return (wide * factor).astype(jnp.bfloat16)


def unit_kernel(raw_ref, out):
    rows = raw_ref.shape[0]
    step = math.gcd(128, rows)
    for at in range(0, rows, step):
        out[at : at + step, :] = unit_of(raw_ref[at : at + step, :])


def units_of(raw, which, count):
    depth = raw.shape[1]
    return pl.pallas_call(
        unit_kernel,
        grid=(1,),
        in_specs=[pl.BlockSpec((count, depth), lambda i: (which, 0))],
        out_specs=pl.BlockSpec((count, depth), lambda i: (0, 0)),
        out_shape=jax.ShapeDtypeStruct((count, depth), jnp.bfloat16),
        compiler_params=pltpu.CompilerParams(vmem_limit_bytes=VMEM),
        cost_estimate=pl.CostEstimate(
            flops=8 * count * depth, bytes_accessed=4 * count * depth, transcendentals=0
        ),
    )(raw)


def product(left, right):
    return lax.dot_general(
        left, right, (((1,), (1,)), ((), ())), preferred_element_type=jnp.float32
    )


def lanes_max(scores):
    parts = [scores[:, j : j + 128] for j in range(0, scores.shape[1], 128)]
    return functools.reduce(jnp.maximum, parts)


def across(part):
    return jnp.max(part.T, axis=0, keepdims=True)


@dataclasses.dataclass
class Piece:
    rows: jax.Array
    block: int
    side: int
    at: int

    @property
    def n(self):
        return self.rows.shape[0]


def own_kernel(lefts, rights, table, *refs):
    refs = list(refs)
    lines = [refs.pop(0) for _ in lefts]
    if rights[0].side:
        fars = [refs.pop(0) for _ in rights]
        so_far, best_ref, rowpart = refs
        best_ref[...] = so_far[...]
    else:
        fars = lines
        best_ref, first_ref, second_ref, rowpart = refs
        for ref in (best_ref, first_ref, second_ref):
            ref[...] = jnp.full(ref.shape, -1.0, jnp.float32)
    base = table[BASE]
    for left, left_ref in zip(lefts, lines):
        size = left_ref.shape[0]
        position = base + table[SIDE] + left.at
        position = position + lax.broadcasted_iota(jnp.int32, (size, 1), 0)
        low = jnp.zeros((size, 1), jnp.int32)
        high = jnp.zeros((size, 1), jnp.int32)
        for c in range(SPAN, table.shape[0], 2):
            here = (position >= table[c]) & (position < table[c + 1])
            low = jnp.where(here, table[c], low)
            high = jnp.where(here, table[c + 1], high)
        part = rowpart.at[0:size]
        part[...] = jnp.full(part.shape, -1.0, jnp.float32)
        for right, right_ref in zip(rights, fars):
            start = base + table[SIDE + right.side] + right.at
            scores = product(left_ref[...], right_ref[...])
            column = start + lax.broadcasted_iota(jnp.int32, (1, right_ref.shape[0]), 1)
            keep = (column >= low) & (column < high) & (column != position)
            part[...] = jnp.maximum(part[...], lanes_max(jnp.where(keep, scores, -1.0)))
        to = (slice(0, 1), slice(left.at, left.at + size))
        best_ref[to] = jnp.maximum(best_ref[to], across(part[...]))


def own_rows(table, lefts, rights, best):
    bare = lambda pieces: [dataclasses.replace(p, rows=None) for p in pieces]
    rows, depth = sum(p.n for p in lefts), lefts[0].rows.shape[1]
    shares = (CORES,) if best else (CORES, CORES, 1)
    return vmem_call(
        functools.partial(own_kernel, bare(lefts), bare(rights)),
        [table] + [p.rows for p in (lefts + rights if best else lefts)] + best,
        [jax.ShapeDtypeStruct((n, rows), jnp.float32) for n in shares],
        [pltpu.VMEM((lefts[0].n, 128), jnp.float32)],
        2 * rows * sum(p.n for p in rights) * depth,
    )


PAIRS = {(0, 1): 0, (0, 2): 1, (1, 2): 2}


def rect(table, left, right):
    flip = left.block > right.block
    which = PAIRS[(right.block, left.block) if flip else (left.block, right.block)]
    ends = [table[RECT + 4 * which + k] for k in range(4)]
    if flip:
        ends = ends[2:] + ends[:2]
    x, y = table[SIDE + left.side] + left.at, table[SIDE + right.side] + right.at
    return ends[0] - x, ends[1] - x, ends[2] - y, ends[3] - y


def meet_kernel(pieces, groups, table, *refs):
    refs = list(refs)
    held = [refs.pop(0) for _ in pieces]
    acc_in = [refs.pop(0) for _ in range(3)]
    acc = [refs.pop(0) for _ in range(3)]
    (rowpart,) = refs
    for src, dst in zip(acc_in, acc):
        dst[...] = src[...]
    for l, partners in groups:
        left, left_ref = pieces[l], held[l]
        tm = left_ref.shape[0]
        part = rowpart.at[0:tm]
        part[...] = jnp.full(part.shape, -1.0, jnp.float32)
        shares = {}
        for r in partners:
            shares.setdefault((pieces[r].block, pieces[r].side), []).append(r)
        used = jnp.bool_(False)
        for share in shares.values():
            some = jnp.bool_(False)
            for r in share:
                xa, xb, ya, yb = rect(table, left, pieces[r])
                tn = held[r].shape[0]
                some |= (xa < tm) & (xb > 0) & (ya < tn) & (yb > 0) & (xa < xb) & (ya < yb)
            used |= some

            @pl.when(some)
            def _():
                for r in share:
                    right, right_ref = pieces[r], held[r]
                    tn = right_ref.shape[0]
                    xa, xb, ya, yb = rect(table, left, right)
                    scores = product(left_ref[...], right_ref[...])
                    row = lax.broadcasted_iota(jnp.int32, (tm, 1), 0)
                    col = lax.broadcasted_iota(jnp.int32, (1, tn), 1)
                    keep = ((row >= xa) & (row < xb)) & ((col >= ya) & (col < yb))
                    scores = jnp.where(keep, scores, -1.0)
                    part[...] = jnp.maximum(part[...], lanes_max(scores))
                    to = (slice(right.side, right.side + 1), slice(right.at, right.at + tn))
                    best = acc[right.block]
                    best[to] = jnp.maximum(best[to], jnp.max(scores, axis=0, keepdims=True))

        @pl.when(used)
        def _():
            to = (slice(left.side, left.side + 1), slice(left.at, left.at + tm))
            best = acc[left.block]
            best[to] = jnp.maximum(best[to], across(part[...]))


def vmem_call(kernel, ins, outs, scratch, flops):
    vm = pl.BlockSpec(memory_space=pltpu.VMEM)
    sm = pl.BlockSpec(memory_space=pltpu.SMEM)
    ins = ins[:1] + [pltpu.with_memory_space_constraint(x, pltpu.VMEM) for x in ins[1:]]
    moved = sum(x.size * x.dtype.itemsize for x in [*ins, *outs])
    return pl.pallas_call(
        kernel,
        out_shape=outs,
        in_specs=[sm] + [vm] * (len(ins) - 1),
        out_specs=[vm] * len(outs),
        scratch_shapes=scratch,
        compiler_params=pltpu.CompilerParams(vmem_limit_bytes=VMEM),
        cost_estimate=pl.CostEstimate(flops=PACE * flops, bytes_accessed=moved, transcendentals=0),
    )(*ins)


def meet(table, pairs, acc):
    pieces, groups = [], []

    def index(piece):
        for i, other in enumerate(pieces):
            if other is piece:
                return i
        pieces.append(piece)
        return len(pieces) - 1

    for left, rights in pairs:
        groups.append((index(left), [index(r) for r in rights]))
    depth = pieces[0].rows.shape[1]
    flops = sum(2 * left.n * r.n * depth for left, rights in pairs for r in rights)
    most = max(left.n for left, _ in pairs)
    return vmem_call(
        functools.partial(
            meet_kernel, [dataclasses.replace(p, rows=None) for p in pieces], groups
        ),
        [table] + [p.rows for p in pieces] + list(acc),
        [jax.ShapeDtypeStruct(a.shape, a.dtype) for a in acc],
        [pltpu.VMEM((most, 128), jnp.float32)],
        flops,
    )


def after(value, *others):
    return lax.optimization_barrier((value, *others))[0]


def shards(embeddings, offsets):
    rows, depth = embeddings.shape
    chips = lax.axis_size(AXES) // CORES
    chip_rows = CORES * rows
    first, second = routes(chips)
    to_first, to_second = on_cores(first), on_cores(second)
    swap = [(i, i ^ 1) for i in range(CORES * chips)]
    send = lambda x, pairs: lax.ppermute(x, AXES, pairs)

    spans = chip_rows // MIN_C + 2
    scalars = pl.BlockSpec(memory_space=pltpu.SMEM)
    table = pl.pallas_call(
        functools.partial(plan_kernel, chips, chip_rows, spans),
        out_shape=jax.ShapeDtypeStruct((SPAN + 2 * spans,), jnp.int32),
        in_specs=[scalars],
        out_specs=scalars,
        compiler_params=pltpu.CompilerParams(vmem_limit_bytes=PLAN_VMEM),
    )(offsets)

    most = rows * 3 // 4
    u1 = units_of(embeddings, 0, most)
    a1, b1 = send(u1, to_first), send(u1, to_second)
    far1 = send(u1, swap)
    u2 = units_of(after(embeddings, far1), most // (rows - most), rows - most)
    a2, b2 = send(u2, to_first), send(u2, to_second)
    far2 = send(u2, swap)

    own = [Piece(u1, 0, 0, 0), Piece(u2, 0, 0, most)]
    far = [Piece(far1, 0, 1, 0), Piece(far2, 0, 1, most)]
    best_near, *blank = own_rows(table, own, own, [])
    (best_own,) = own_rows(table, own, far, [best_near])
    acc = [best_own, *blank]
    chip_own = own + far

    pa1, pb1 = Piece(a1, 1, 0, 0), Piece(b1, 2, 0, 0)
    pax1 = Piece(send(after(a1, best_own), swap), 1, 1, 0)
    acc = meet(table, [(pa1, chip_own)], acc)
    acc = meet(table, [(pb1, chip_own + [pa1, pax1])], acc)

    pa2, pb2 = Piece(a2, 1, 0, most), Piece(b2, 2, 0, most)
    pax2 = Piece(send(after(a2, acc[0]), swap), 1, 1, most)
    acc = meet(table, [(pa2, chip_own + [pb1])], acc)
    acc = meet(
        table, [(pb2, chip_own + [pa1, pax1, pa2, pax2]), (pax2, [pb1])], acc
    )

    best_own, best_first, best_second = acc
    from_first = send(best_first, on_cores(flipped(first)))
    from_second = send(best_second, on_cores(flipped(second)))
    line = jax.ShapeDtypeStruct((1, rows), jnp.float32)
    mine, other = vmem_call(
        join_kernel, [table, best_own, from_first, from_second], [line] * 2, [], rows
    )
    return jnp.maximum(mine, send(other, swap)).reshape(rows)


def solution(mesh):
    return jax.shard_map(
        shards,
        mesh=mesh,
        in_specs=(P(AXES, None), P()),
        out_specs=P(AXES),
        check_vma=False,
    )
```

```python
import dataclasses
import functools
import math

import jax
import jax.numpy as jnp
from jax import lax
from jax.experimental import pallas as pl
from jax.experimental.pallas import tpu as pltpu
from jax.sharding import PartitionSpec as P

AXES = ("grp", "work")
CORES = 2
MIN_C = 512
TILE = 512
VMEM = 16 * 1024 * 1024
PLAN_VMEM = 1024 * 1024
PACE = 10


def routes(chips):
    last = chips - 1
    first = [(b, b + 1) for b in range(0, chips, 2) if b + 1 != last]
    first += [(b, b + 3) for b in range(1, chips, 2) if b + 3 < chips]
    first += [(last - 2, last)]
    second = [(b, b + 2) for b in range(0, chips, 2) if b + 2 < chips]
    second += [(b, b - 2) for b in range(1, chips, 2) if b >= 3]
    second += [(last - 1, last)]
    return first, second


def on_cores(pairs):
    return [(CORES * s + k, CORES * d + k) for s, d in pairs for k in range(CORES)]


def flipped(pairs):
    return [(d, s) for s, d in pairs]


RECT, SIDE, HAS, BASE, SPAN = 0, 12, 14, 16, 17


def plan_kernel(chips, chip_rows, spans, offsets, out):
    me = lax.axis_index(AXES)
    chip, core = lax.div(me, CORES), lax.rem(me, CORES)
    rows = chip_rows // CORES
    odd = lax.rem(chip, 2) == 1
    at_end = chip == chips - 1
    first = jnp.where(odd, jnp.where(at_end, chip - 2, chip - 1), chip - 3)
    second = jnp.where(odd, jnp.where(at_end, chip - 1, chip + 2), chip - 2)
    starts = [b * chip_rows for b in (chip, first, second)]
    for k in range(spans):
        out[SPAN + 2 * k] = 0
        out[SPAN + 2 * k + 1] = 0

    def look(c, state):
        lower, upper = offsets[c], offsets[c + 1]
        lows, highs, count = state[:3], state[3:6], state[6]
        here = (upper > starts[0]) & (lower < starts[0] + chip_rows)

        @pl.when(here)
        def _():
            at = SPAN + 2 * jnp.minimum(count, spans - 1)
            out[at] = lower
            out[at + 1] = upper

        holds = [(lower < s + chip_rows) & (upper >= s + chip_rows) for s in starts]
        lows = [jnp.where(h, lower, v) for h, v in zip(holds, lows)]
        highs = [jnp.where(h, upper, v) for h, v in zip(holds, highs)]
        return (*lows, *highs, count + here.astype(jnp.int32))

    none = jnp.int32(-1)
    state = lax.fori_loop(0, offsets.shape[0] - 1, look, (none,) * 6 + (jnp.int32(0),))
    lows, highs = state[:3], state[3:6]
    for which, (p, q) in enumerate(((0, 1), (0, 2), (1, 2))):
        p_first = starts[p] < starts[q]
        s = jnp.where(p_first, lows[p], lows[q])
        e = jnp.where(p_first, highs[p], highs[q])
        later = jnp.where(p_first, starts[q], starts[p])
        ok = (lows[p] >= 0) & (lows[q] >= 0) & (e > later)
        for k, (b, is_first) in enumerate(((p, p_first), (q, ~p_first))):
            a = jnp.where(is_first, jnp.maximum(s - starts[b], 0), 0)
            z = jnp.where(is_first, chip_rows, jnp.minimum(e - starts[b], chip_rows))
            out[RECT + 4 * which + 2 * k] = a
            out[RECT + 4 * which + 2 * k + 1] = jnp.where(ok, z, a)
    out[SIDE] = core * rows
    out[SIDE + 1] = (1 - core) * rows
    has_first = jnp.where(odd, (chip + 3 < chips) | (chip == chips - 3), chip + 2 < chips)
    has_second = jnp.where(odd, chip >= 3, (chip + 2 < chips) | (chip == chips - 2))
    out[HAS] = has_first.astype(jnp.int32)
    out[HAS + 1] = has_second.astype(jnp.int32)
    out[BASE] = starts[0]


def join_kernel(near_ref, far_ref, own_ref, first_ref):
    both = jnp.maximum(near_ref[...], far_ref[...])
    own_ref[...] = both[0:1]
    first_ref[...] = both[1:2]


def last_kernel(table, own_ref, first_ref, second_ref, out):
    first = jnp.where(table[HAS] == 1, first_ref[...], -1.0)
    second = jnp.where(table[HAS + 1] == 1, second_ref[...], -1.0)
    out[...] = jnp.maximum(jnp.maximum(own_ref[...], first), second)


def unit_of(raw):
    wide = raw.astype(jnp.float32)
    mean = jnp.sum(wide * wide, axis=1, keepdims=True) * (1.0 / raw.shape[1])
    factor = lax.rsqrt(mean + 1e-06) * (1.0 / math.sqrt(raw.shape[1]))
    return (wide * factor).astype(jnp.bfloat16)


def unit_kernel(first, raw_ref, out, held, sems):
    count, step, _ = held.shape
    copies = []
    for k in range(count):
        rows = raw_ref.at[first + k * step : first + (k + 1) * step]
        copies.append(pltpu.make_async_copy(rows, held.at[k], sems.at[k]))
        copies[-1].start()
    for k, copy in enumerate(copies):
        copy.wait()
        out[k * step : (k + 1) * step, :] = unit_of(held[k])


def units_of(raw, first, rows):
    depth = raw.shape[1]
    step = math.gcd(128, rows)
    return pl.pallas_call(
        functools.partial(unit_kernel, first),
        in_specs=[pl.BlockSpec(memory_space=pl.ANY)],
        out_specs=pl.BlockSpec(memory_space=pltpu.VMEM),
        out_shape=jax.ShapeDtypeStruct((rows, depth), jnp.bfloat16),
        scratch_shapes=[
            pltpu.VMEM((rows // step, step, depth), jnp.bfloat16),
            pltpu.SemaphoreType.DMA((rows // step,)),
        ],
        compiler_params=pltpu.CompilerParams(vmem_limit_bytes=VMEM),
        cost_estimate=pl.CostEstimate(
            flops=8 * rows * depth, bytes_accessed=4 * rows * depth, transcendentals=0
        ),
    )(pltpu.with_memory_space_constraint(raw, pltpu.HBM))


def product(left, right):
    return lax.dot_general(
        left, right, (((1,), (1,)), ((), ())), preferred_element_type=jnp.float32
    )


def lanes_max(scores):
    parts = [scores[:, j : j + 128] for j in range(0, scores.shape[1], 128)]
    return functools.reduce(jnp.maximum, parts)


def across(part):
    return jnp.max(part.T, axis=0, keepdims=True)


@dataclasses.dataclass
class Piece:
    rows: jax.Array
    block: int
    side: int
    at: int
    size: int = 0

    @property
    def n(self):
        return self.rows.shape[0]

    def bare(self):
        return dataclasses.replace(self, rows=None, size=self.n)

    def best(self, acc):
        line = 0 if self.block == 2 else self.block
        which = 2 if self.block == 2 else self.side
        return acc[which].at[line : line + 1, self.at : self.at + self.size]


def own_kernel(lefts, rights, table, *refs):
    refs = list(refs)
    lines = [refs.pop(0) for _ in lefts]
    if rights[0].side:
        fars = [refs.pop(0) for _ in rights]
        so_far, best_ref, rowpart = refs
        best_ref[...] = so_far[...]
    else:
        fars = lines
        best_ref, far_ref, second_ref, rowpart = refs
        for ref in (best_ref, far_ref, second_ref):
            ref[...] = jnp.full(ref.shape, -1.0, jnp.float32)
    base = table[BASE]
    for left, left_ref in zip(lefts, lines):
        size = left_ref.shape[0]
        position = base + table[SIDE] + left.at
        position = position + lax.broadcasted_iota(jnp.int32, (size, 1), 0)
        low = jnp.zeros((size, 1), jnp.int32)
        high = jnp.zeros((size, 1), jnp.int32)
        for c in range(SPAN, table.shape[0], 2):
            here = (position >= table[c]) & (position < table[c + 1])
            low = jnp.where(here, table[c], low)
            high = jnp.where(here, table[c + 1], high)
        part = rowpart.at[0:size]
        part[...] = jnp.full(part.shape, -1.0, jnp.float32)
        for right, right_ref in zip(rights, fars):
            start = base + table[SIDE + right.side] + right.at
            scores = product(left_ref[...], right_ref[...])
            column = start + lax.broadcasted_iota(jnp.int32, (1, right_ref.shape[0]), 1)
            keep = (column >= low) & (column < high) & (column != position)
            part[...] = jnp.maximum(part[...], lanes_max(jnp.where(keep, scores, -1.0)))
        best = left.best([best_ref])
        best[...] = jnp.maximum(best[...], across(part[...]))


def own_rows(table, lefts, rights, best):
    bare = lambda pieces: [p.bare() for p in pieces]
    rows, depth = sum(p.n for p in lefts), lefts[0].rows.shape[1]
    shares = (CORES,) if best else (CORES, CORES, 1)
    return vmem_call(
        functools.partial(own_kernel, bare(lefts), bare(rights)),
        [table] + [p.rows for p in (lefts + rights if best else lefts)] + best,
        [jax.ShapeDtypeStruct((n, rows), jnp.float32) for n in shares],
        [pltpu.VMEM((lefts[0].n, 128), jnp.float32)],
        2 * rows * sum(p.n for p in rights) * depth,
    )


PAIRS = {(0, 1): 0, (0, 2): 1, (1, 2): 2}


def rect(table, left, right):
    flip = left.block > right.block
    which = PAIRS[(right.block, left.block) if flip else (left.block, right.block)]
    ends = [table[RECT + 4 * which + k] for k in range(4)]
    if flip:
        ends = ends[2:] + ends[:2]
    x, y = table[SIDE + left.side] + left.at, table[SIDE + right.side] + right.at
    return ends[0] - x, ends[1] - x, ends[2] - y, ends[3] - y


def meet_kernel(pieces, groups, table, *refs):
    refs = list(refs)
    held = [refs.pop(0) for _ in pieces]
    acc_in = [refs.pop(0) for _ in range(3)]
    acc = [refs.pop(0) for _ in range(3)]
    (rowpart,) = refs
    for src, dst in zip(acc_in, acc):
        dst[...] = src[...]
    for l, partners in groups:
        left, left_ref = pieces[l], held[l]
        tm = left_ref.shape[0]
        part = rowpart.at[0:tm]
        part[...] = jnp.full(part.shape, -1.0, jnp.float32)
        shares = {}
        for r in partners:
            shares.setdefault((pieces[r].block, pieces[r].side), []).append(r)
        used = jnp.bool_(False)
        for share in shares.values():
            some = jnp.bool_(False)
            for r in share:
                xa, xb, ya, yb = rect(table, left, pieces[r])
                tn = held[r].shape[0]
                some |= (xa < tm) & (xb > 0) & (ya < tn) & (yb > 0) & (xa < xb) & (ya < yb)
            used |= some

            @pl.when(some)
            def _():
                for r in share:
                    right, right_ref = pieces[r], held[r]
                    tn = right_ref.shape[0]
                    xa, xb, ya, yb = rect(table, left, right)
                    scores = product(left_ref[...], right_ref[...])
                    row = lax.broadcasted_iota(jnp.int32, (tm, 1), 0)
                    col = lax.broadcasted_iota(jnp.int32, (1, tn), 1)
                    keep = ((row >= xa) & (row < xb)) & ((col >= ya) & (col < yb))
                    scores = jnp.where(keep, scores, -1.0)
                    part[...] = jnp.maximum(part[...], lanes_max(scores))
                    best = right.best(acc)
                    best[...] = jnp.maximum(best[...], jnp.max(scores, axis=0, keepdims=True))

        @pl.when(used)
        def _():
            best = left.best(acc)
            best[...] = jnp.maximum(best[...], across(part[...]))


def vmem_call(kernel, ins, outs, scratch, flops, scalars=1):
    vm = pl.BlockSpec(memory_space=pltpu.VMEM)
    sm = pl.BlockSpec(memory_space=pltpu.SMEM)
    pin = lambda x: pltpu.with_memory_space_constraint(x, pltpu.VMEM)
    ins = ins[:scalars] + [pin(x) for x in ins[scalars:]]
    moved = sum(x.size * x.dtype.itemsize for x in [*ins, *outs])
    return pl.pallas_call(
        kernel,
        out_shape=outs,
        in_specs=[sm] * scalars + [vm] * (len(ins) - scalars),
        out_specs=[vm] * len(outs),
        scratch_shapes=scratch,
        compiler_params=pltpu.CompilerParams(vmem_limit_bytes=VMEM),
        cost_estimate=pl.CostEstimate(flops=PACE * flops, bytes_accessed=moved, transcendentals=0),
    )(*ins)


def meet(table, pairs, acc):
    pieces, groups = [], []

    def index(piece):
        for i, other in enumerate(pieces):
            if other is piece:
                return i
        pieces.append(piece)
        return len(pieces) - 1

    for left, rights in pairs:
        groups.append((index(left), [index(r) for r in rights]))
    depth = pieces[0].rows.shape[1]
    flops = sum(2 * left.n * r.n * depth for left, rights in pairs for r in rights)
    most = max(left.n for left, _ in pairs)
    return vmem_call(
        functools.partial(
            meet_kernel, [p.bare() for p in pieces], groups
        ),
        [table] + [p.rows for p in pieces] + list(acc),
        [jax.ShapeDtypeStruct(a.shape, a.dtype) for a in acc],
        [pltpu.VMEM((most, 128), jnp.float32)],
        flops,
    )


def after(value, *others):
    return lax.optimization_barrier((value, *others))[0]


def shards(embeddings, offsets):
    rows, depth = embeddings.shape
    chips = lax.axis_size(AXES) // CORES
    chip_rows = CORES * rows
    first, second = routes(chips)
    to_first, to_second = on_cores(first), on_cores(second)
    swap = [(i, i ^ 1) for i in range(CORES * chips)]
    send = lambda x, pairs: lax.ppermute(x, AXES, pairs)

    spans = chip_rows // MIN_C + 2
    scalars = pl.BlockSpec(memory_space=pltpu.SMEM)
    table = pl.pallas_call(
        functools.partial(plan_kernel, chips, chip_rows, spans),
        out_shape=jax.ShapeDtypeStruct((SPAN + 2 * spans,), jnp.int32),
        in_specs=[scalars],
        out_specs=scalars,
        compiler_params=pltpu.CompilerParams(vmem_limit_bytes=PLAN_VMEM),
    )(offsets)

    most = rows * 5 // 8
    u1 = units_of(embeddings, 0, most)
    a1, b1 = send(u1, to_first), send(u1, to_second)
    far1 = send(u1, swap)
    u2 = units_of(after(embeddings, far1), most, rows - most)
    a2, b2 = send(u2, to_first), send(u2, to_second)
    far2 = send(u2, swap)

    own = [Piece(u1, 0, 0, 0), Piece(u2, 0, 0, most)]
    far = [Piece(far1, 0, 1, 0), Piece(far2, 0, 1, most)]
    best_near, *blank = own_rows(table, own, own, [])
    (best_own,) = own_rows(table, own, far, [best_near])
    acc = [best_own, *blank]
    chip_own = own + far

    pa1, pb1 = Piece(a1, 1, 0, 0), Piece(b1, 2, 0, 0)
    pax1 = Piece(send(after(a1, best_own), swap), 1, 1, 0)
    acc = meet(table, [(pa1, chip_own)], acc)
    acc = meet(table, [(pb1, chip_own + [pa1, pax1])], acc)

    pa2, pb2 = Piece(a2, 1, 0, most), Piece(b2, 2, 0, most)
    pax2 = Piece(send(after(a2, acc[0]), swap), 1, 1, most)
    acc = meet(table, [(pa2, chip_own + [pb1])], acc)
    acc = meet(
        table, [(pb2, chip_own + [pa1, pax1, pa2, pax2]), (pax2, [pb1])], acc
    )

    near, far_best, best_second = acc
    line = jax.ShapeDtypeStruct((1, rows), jnp.float32)
    own_best, best_first = vmem_call(
        join_kernel, [near, send(far_best, swap)], [line] * 2, [], rows, scalars=0
    )
    from_second = send(best_second, on_cores(flipped(second)))
    from_first = send(best_first, on_cores(flipped(first)))
    (out,) = vmem_call(
        last_kernel, [table, own_best, from_first, from_second], [line], [], rows
    )
    return out.reshape(rows)


def solution(mesh):
    return jax.shard_map(
        shards,
        mesh=mesh,
        in_specs=(P(AXES, None), P()),
        out_specs=P(AXES),
        check_vma=False,
    )
```

```python
import dataclasses
import functools
import math

import jax
import jax.numpy as jnp
from jax import lax
from jax.experimental import pallas as pl
from jax.experimental.pallas import tpu as pltpu
from jax.sharding import PartitionSpec as P

AXES = ("grp", "work")
CORES = 2
MIN_C = 512
TILE = 512
VMEM = 16 * 1024 * 1024
PLAN_VMEM = 1024 * 1024
PACE = 10
SHARES = [4, 2, 2]


def routes(chips):
    last = chips - 1
    first = [(b, b + 1) for b in range(0, chips, 2) if b + 1 != last]
    first += [(b, b + 3) for b in range(1, chips, 2) if b + 3 < chips]
    first += [(last - 2, last)]
    second = [(b, b + 2) for b in range(0, chips, 2) if b + 2 < chips]
    second += [(b, b - 2) for b in range(1, chips, 2) if b >= 3]
    second += [(last - 1, last)]
    return first, second


def on_cores(pairs):
    return [(CORES * s + k, CORES * d + k) for s, d in pairs for k in range(CORES)]


def flipped(pairs):
    return [(d, s) for s, d in pairs]


RECT, SIDE, HAS, BASE, SPAN = 0, 12, 14, 16, 17


def plan_kernel(chips, chip_rows, spans, offsets, out):
    me = lax.axis_index(AXES)
    chip, core = lax.div(me, CORES), lax.rem(me, CORES)
    rows = chip_rows // CORES
    odd = lax.rem(chip, 2) == 1
    at_end = chip == chips - 1
    first = jnp.where(odd, jnp.where(at_end, chip - 2, chip - 1), chip - 3)
    second = jnp.where(odd, jnp.where(at_end, chip - 1, chip + 2), chip - 2)
    starts = [b * chip_rows for b in (chip, first, second)]
    for k in range(spans):
        out[SPAN + 2 * k] = 0
        out[SPAN + 2 * k + 1] = 0

    def look(c, state):
        lower, upper = offsets[c], offsets[c + 1]
        lows, highs, count = state[:3], state[3:6], state[6]
        here = (upper > starts[0]) & (lower < starts[0] + chip_rows)

        @pl.when(here)
        def _():
            at = SPAN + 2 * jnp.minimum(count, spans - 1)
            out[at] = lower
            out[at + 1] = upper

        holds = [(lower < s + chip_rows) & (upper >= s + chip_rows) for s in starts]
        lows = [jnp.where(h, lower, v) for h, v in zip(holds, lows)]
        highs = [jnp.where(h, upper, v) for h, v in zip(holds, highs)]
        return (*lows, *highs, count + here.astype(jnp.int32))

    none = jnp.int32(-1)
    state = lax.fori_loop(0, offsets.shape[0] - 1, look, (none,) * 6 + (jnp.int32(0),))
    lows, highs = state[:3], state[3:6]
    for which, (p, q) in enumerate(((0, 1), (0, 2), (1, 2))):
        p_first = starts[p] < starts[q]
        s = jnp.where(p_first, lows[p], lows[q])
        e = jnp.where(p_first, highs[p], highs[q])
        later = jnp.where(p_first, starts[q], starts[p])
        ok = (lows[p] >= 0) & (lows[q] >= 0) & (e > later)
        for k, (b, is_first) in enumerate(((p, p_first), (q, ~p_first))):
            a = jnp.where(is_first, jnp.maximum(s - starts[b], 0), 0)
            z = jnp.where(is_first, chip_rows, jnp.minimum(e - starts[b], chip_rows))
            out[RECT + 4 * which + 2 * k] = a
            out[RECT + 4 * which + 2 * k + 1] = jnp.where(ok, z, a)
    out[SIDE] = core * rows
    out[SIDE + 1] = (1 - core) * rows
    has_first = jnp.where(odd, (chip + 3 < chips) | (chip == chips - 3), chip + 2 < chips)
    has_second = jnp.where(odd, chip >= 3, (chip + 2 < chips) | (chip == chips - 2))
    out[HAS] = has_first.astype(jnp.int32)
    out[HAS + 1] = has_second.astype(jnp.int32)
    out[BASE] = starts[0]


def join_kernel(near_ref, far_ref, own_ref, first_ref):
    both = jnp.maximum(near_ref[...], far_ref[...])
    own_ref[...] = both[0:1]
    first_ref[...] = both[1:2]


def last_kernel(table, own_ref, first_ref, second_ref, out):
    first = jnp.where(table[HAS] == 1, first_ref[...], -1.0)
    second = jnp.where(table[HAS + 1] == 1, second_ref[...], -1.0)
    out[...] = jnp.maximum(jnp.maximum(own_ref[...], first), second)


def unit_of(raw):
    wide = raw.astype(jnp.float32)
    mean = jnp.sum(wide * wide, axis=1, keepdims=True) * (1.0 / raw.shape[1])
    factor = lax.rsqrt(mean + 1e-06) * (1.0 / math.sqrt(raw.shape[1]))
    return (wide * factor).astype(jnp.bfloat16)


def unit_kernel(first, cuts, raw_ref, *refs):
    outs, (held, sems) = refs[:-2], refs[-2:]
    count, step, _ = held.shape
    copies = []
    for k in range(count):
        rows = raw_ref.at[first + k * step : first + (k + 1) * step]
        copies.append(pltpu.make_async_copy(rows, held.at[k], sems.at[k]))
        copies[-1].start()
    for k, copy in enumerate(copies):
        copy.wait()
        unit = unit_of(held[k])
        for (start, n), out in zip(cuts, outs):
            if start <= k * step < start + n:
                out[k * step - start : (k + 1) * step - start, :] = unit


def units_of(raw, first, rows, cuts):
    depth = raw.shape[1]
    step = math.gcd(128, rows)
    return pl.pallas_call(
        functools.partial(unit_kernel, first, cuts),
        in_specs=[pl.BlockSpec(memory_space=pl.ANY)],
        out_specs=[pl.BlockSpec(memory_space=pltpu.VMEM)] * len(cuts),
        out_shape=[jax.ShapeDtypeStruct((n, depth), jnp.bfloat16) for _, n in cuts],
        scratch_shapes=[
            pltpu.VMEM((rows // step, step, depth), jnp.bfloat16),
            pltpu.SemaphoreType.DMA((rows // step,)),
        ],
        compiler_params=pltpu.CompilerParams(vmem_limit_bytes=VMEM),
        cost_estimate=pl.CostEstimate(
            flops=8 * rows * depth, bytes_accessed=4 * rows * depth, transcendentals=0
        ),
    )(pltpu.with_memory_space_constraint(raw, pltpu.HBM))


def product(left, right):
    return lax.dot_general(
        left, right, (((1,), (1,)), ((), ())), preferred_element_type=jnp.float32
    )


def lanes_max(scores):
    parts = [scores[:, j : j + 128] for j in range(0, scores.shape[1], 128)]
    return functools.reduce(jnp.maximum, parts)


def across(part):
    return jnp.max(part.T, axis=0, keepdims=True)


@dataclasses.dataclass
class Piece:
    rows: jax.Array
    block: int
    side: int
    at: int
    size: int = 0

    @property
    def n(self):
        return self.rows.shape[0]

    def bare(self):
        return dataclasses.replace(self, rows=None, size=self.n)

    def best(self, acc):
        line = 0 if self.block == 2 else self.block
        which = 2 if self.block == 2 else self.side
        return acc[which].at[line : line + 1, self.at : self.at + self.size]


def own_kernel(lefts, rights, table, *refs):
    refs = list(refs)
    lines = [refs.pop(0) for _ in lefts]
    if rights[0].side:
        fars = [refs.pop(0) for _ in rights]
        so_far, best_ref, rowpart = refs
        best_ref[...] = so_far[...]
    else:
        fars = lines
        best_ref, far_ref, second_ref, rowpart = refs
        for ref in (best_ref, far_ref, second_ref):
            ref[...] = jnp.full(ref.shape, -1.0, jnp.float32)
    base = table[BASE]
    for left, left_ref in zip(lefts, lines):
        size = left_ref.shape[0]
        position = base + table[SIDE] + left.at
        position = position + lax.broadcasted_iota(jnp.int32, (size, 1), 0)
        low = jnp.zeros((size, 1), jnp.int32)
        high = jnp.zeros((size, 1), jnp.int32)
        for c in range(SPAN, table.shape[0], 2):
            here = (position >= table[c]) & (position < table[c + 1])
            low = jnp.where(here, table[c], low)
            high = jnp.where(here, table[c + 1], high)
        part = rowpart.at[0:size]
        part[...] = jnp.full(part.shape, -1.0, jnp.float32)
        for right, right_ref in zip(rights, fars):
            start = base + table[SIDE + right.side] + right.at
            scores = product(left_ref[...], right_ref[...])
            column = start + lax.broadcasted_iota(jnp.int32, (1, right_ref.shape[0]), 1)
            keep = (column >= low) & (column < high) & (column != position)
            part[...] = jnp.maximum(part[...], lanes_max(jnp.where(keep, scores, -1.0)))
        best = left.best([best_ref])
        best[...] = jnp.maximum(best[...], across(part[...]))


def own_rows(table, lefts, rights, best):
    bare = lambda pieces: [p.bare() for p in pieces]
    rows, depth = sum(p.n for p in lefts), lefts[0].rows.shape[1]
    shares = (CORES,) if best else (CORES, CORES, 1)
    return vmem_call(
        functools.partial(own_kernel, bare(lefts), bare(rights)),
        [table] + [p.rows for p in (lefts + rights if best else lefts)] + best,
        [jax.ShapeDtypeStruct((n, rows), jnp.float32) for n in shares],
        [pltpu.VMEM((lefts[0].n, 128), jnp.float32)],
        2 * rows * sum(p.n for p in rights) * depth,
    )


PAIRS = {(0, 1): 0, (0, 2): 1, (1, 2): 2}


def rect(table, left, right):
    flip = left.block > right.block
    which = PAIRS[(right.block, left.block) if flip else (left.block, right.block)]
    ends = [table[RECT + 4 * which + k] for k in range(4)]
    if flip:
        ends = ends[2:] + ends[:2]
    x, y = table[SIDE + left.side] + left.at, table[SIDE + right.side] + right.at
    return ends[0] - x, ends[1] - x, ends[2] - y, ends[3] - y


def meet_kernel(pieces, groups, table, *refs):
    refs = list(refs)
    held = [refs.pop(0) for _ in pieces]
    acc_in = [refs.pop(0) for _ in range(3)]
    acc = [refs.pop(0) for _ in range(3)]
    (rowpart,) = refs
    for src, dst in zip(acc_in, acc):
        dst[...] = src[...]
    for l, partners in groups:
        left, left_ref = pieces[l], held[l]
        tm = left_ref.shape[0]
        part = rowpart.at[0:tm]
        part[...] = jnp.full(part.shape, -1.0, jnp.float32)
        shares = {}
        for r in partners:
            shares.setdefault((pieces[r].block, pieces[r].side), []).append(r)
        used = jnp.bool_(False)
        for share in shares.values():
            some = jnp.bool_(False)
            for r in share:
                xa, xb, ya, yb = rect(table, left, pieces[r])
                tn = held[r].shape[0]
                some |= (xa < tm) & (xb > 0) & (ya < tn) & (yb > 0) & (xa < xb) & (ya < yb)
            used |= some

            @pl.when(some)
            def _():
                for r in share:
                    right, right_ref = pieces[r], held[r]
                    tn = right_ref.shape[0]
                    xa, xb, ya, yb = rect(table, left, right)
                    scores = product(left_ref[...], right_ref[...])
                    row = lax.broadcasted_iota(jnp.int32, (tm, 1), 0)
                    col = lax.broadcasted_iota(jnp.int32, (1, tn), 1)
                    keep = ((row >= xa) & (row < xb)) & ((col >= ya) & (col < yb))
                    scores = jnp.where(keep, scores, -1.0)
                    part[...] = jnp.maximum(part[...], lanes_max(scores))
                    best = right.best(acc)
                    best[...] = jnp.maximum(best[...], jnp.max(scores, axis=0, keepdims=True))

        @pl.when(used)
        def _():
            best = left.best(acc)
            best[...] = jnp.maximum(best[...], across(part[...]))


def vmem_call(kernel, ins, outs, scratch, flops, scalars=1):
    vm = pl.BlockSpec(memory_space=pltpu.VMEM)
    sm = pl.BlockSpec(memory_space=pltpu.SMEM)
    pin = lambda x: pltpu.with_memory_space_constraint(x, pltpu.VMEM)
    ins = ins[:scalars] + [pin(x) for x in ins[scalars:]]
    moved = sum(x.size * x.dtype.itemsize for x in [*ins, *outs])
    return pl.pallas_call(
        kernel,
        out_shape=outs,
        in_specs=[sm] * scalars + [vm] * (len(ins) - scalars),
        out_specs=[vm] * len(outs),
        scratch_shapes=scratch,
        compiler_params=pltpu.CompilerParams(vmem_limit_bytes=VMEM),
        cost_estimate=pl.CostEstimate(flops=PACE * flops, bytes_accessed=moved, transcendentals=0),
    )(*ins)


def meet(table, pairs, acc):
    pieces, groups = [], []

    def index(piece):
        for i, other in enumerate(pieces):
            if other is piece:
                return i
        pieces.append(piece)
        return len(pieces) - 1

    for left, rights in pairs:
        groups.append((index(left), [index(r) for r in rights]))
    depth = pieces[0].rows.shape[1]
    flops = sum(2 * left.n * r.n * depth for left, rights in pairs for r in rights)
    most = max(left.n for left, _ in pairs)
    return vmem_call(
        functools.partial(
            meet_kernel, [p.bare() for p in pieces], groups
        ),
        [table] + [p.rows for p in pieces] + list(acc),
        [jax.ShapeDtypeStruct(a.shape, a.dtype) for a in acc],
        [pltpu.VMEM((most, 128), jnp.float32)],
        flops,
    )


def after(value, *others):
    return lax.optimization_barrier((value, *others))[0]


def shards(embeddings, offsets):
    rows, depth = embeddings.shape
    chips = lax.axis_size(AXES) // CORES
    chip_rows = CORES * rows
    first, second = routes(chips)
    to_first, to_second = on_cores(first), on_cores(second)
    swap = [(i, i ^ 1) for i in range(CORES * chips)]
    send = lambda x, pairs: lax.ppermute(x, AXES, pairs)

    spans = chip_rows // MIN_C + 2
    scalars = pl.BlockSpec(memory_space=pltpu.SMEM)
    table = pl.pallas_call(
        functools.partial(plan_kernel, chips, chip_rows, spans),
        out_shape=jax.ShapeDtypeStruct((SPAN + 2 * spans,), jnp.int32),
        in_specs=[scalars],
        out_specs=scalars,
        compiler_params=pltpu.CompilerParams(vmem_limit_bytes=PLAN_VMEM),
    )(offsets)

    eighth = rows // 8
    sizes = [eighth * k for k in SHARES]
    places = [sum(sizes[:k]) for k in range(len(sizes))]
    lead = sizes[0]
    (u1,) = units_of(embeddings, 0, lead, [(0, lead)])
    firsts, seconds = [send(u1, to_first)], [send(u1, to_second)]
    far1 = send(u1, swap)
    u2, *others = units_of(
        after(embeddings, far1),
        lead,
        rows - lead,
        [(0, rows - lead)] + [(p - lead, n) for p, n in zip(places[1:], sizes[1:])][: 2 * (len(sizes) - 2)],
    )
    far2 = send(u2, swap)
    others = others or [u2]
    firsts.append(send(others[0], to_first))
    seconds.append(send(others[0], to_second))

    own = [Piece(u1, 0, 0, 0), Piece(u2, 0, 0, lead)]
    far = [Piece(far1, 0, 1, 0), Piece(far2, 0, 1, lead)]
    best_near, *blank = own_rows(table, own, own, [])
    (best_own,) = own_rows(table, own, far, [best_near])
    acc = [best_own, *blank]
    seconds += [send(after(u, best_own), to_second) for u in others[1:]]
    chip_own = own + far

    near_firsts, far_firsts, near_seconds = [], [], []
    for k, at in enumerate(places):
        x = Piece(send(after(firsts[k], acc[0]), swap), 1, 1, at)
        a = Piece(firsts[k], 1, 0, at)
        acc = meet(table, [(a, chip_own + near_seconds)], acc)
        if k == 0:
            firsts += [send(after(u, acc[0]), to_first) for u in others[1:]]
        b = Piece(seconds[k], 2, 0, at)
        near_firsts.append(a)
        far_firsts.append(x)
        pairs = [(b, chip_own + near_firsts + far_firsts)]
        if near_seconds:
            pairs.append((x, list(near_seconds)))
        acc = meet(table, pairs, acc)
        near_seconds.append(b)

    near, far_best, best_second = acc
    line = jax.ShapeDtypeStruct((1, rows), jnp.float32)
    own_best, best_first = vmem_call(
        join_kernel, [near, send(far_best, swap)], [line] * 2, [], rows, scalars=0
    )
    from_second = send(best_second, on_cores(flipped(second)))
    from_first = send(best_first, on_cores(flipped(first)))
    (out,) = vmem_call(
        last_kernel, [table, own_best, from_first, from_second], [line], [], rows
    )
    return out.reshape(rows)


def solution(mesh):
    return jax.shard_map(
        shards,
        mesh=mesh,
        in_specs=(P(AXES, None), P()),
        out_specs=P(AXES),
        check_vma=False,
    )
```

```python
import dataclasses
import functools
import math

import jax
import jax.numpy as jnp
from jax import lax
from jax.experimental import pallas as pl
from jax.experimental.pallas import tpu as pltpu
from jax.sharding import PartitionSpec as P

AXES = ("grp", "work")
CORES = 2
MIN_C = 512
TILE = 512
VMEM = 16 * 1024 * 1024
PLAN_VMEM = 1024 * 1024
PACE = 10
SHARES = [5, 2, 1]


def routes(chips):
    last = chips - 1
    first = [(b, b + 1) for b in range(0, chips, 2) if b + 1 != last]
    first += [(b, b + 3) for b in range(1, chips, 2) if b + 3 < chips]
    first += [(last - 2, last)]
    second = [(b, b + 2) for b in range(0, chips, 2) if b + 2 < chips]
    second += [(b, b - 2) for b in range(1, chips, 2) if b >= 3]
    second += [(last - 1, last)]
    return first, second


def on_cores(pairs):
    return [(CORES * s + k, CORES * d + k) for s, d in pairs for k in range(CORES)]


def flipped(pairs):
    return [(d, s) for s, d in pairs]


BIG = 3.0e38
RECT, SIDE, HAS, BASE, SPAN = 0, 12, 14, 16, 17


def plan_kernel(chips, chip_rows, spans, offsets, out):
    me = lax.axis_index(AXES)
    chip, core = lax.div(me, CORES), lax.rem(me, CORES)
    rows = chip_rows // CORES
    odd = lax.rem(chip, 2) == 1
    at_end = chip == chips - 1
    first = jnp.where(odd, jnp.where(at_end, chip - 2, chip - 1), chip - 3)
    second = jnp.where(odd, jnp.where(at_end, chip - 1, chip + 2), chip - 2)
    starts = [b * chip_rows for b in (chip, first, second)]
    for k in range(spans):
        out[SPAN + 2 * k] = 0
        out[SPAN + 2 * k + 1] = 0

    def look(c, state):
        lower, upper = offsets[c], offsets[c + 1]
        lows, highs, count = state[:3], state[3:6], state[6]
        here = (upper > starts[0]) & (lower < starts[0] + chip_rows)

        @pl.when(here)
        def _():
            at = SPAN + 2 * jnp.minimum(count, spans - 1)
            out[at] = lower
            out[at + 1] = upper

        holds = [(lower < s + chip_rows) & (upper >= s + chip_rows) for s in starts]
        lows = [jnp.where(h, lower, v) for h, v in zip(holds, lows)]
        highs = [jnp.where(h, upper, v) for h, v in zip(holds, highs)]
        return (*lows, *highs, count + here.astype(jnp.int32))

    none = jnp.int32(-1)
    state = lax.fori_loop(0, offsets.shape[0] - 1, look, (none,) * 6 + (jnp.int32(0),))
    lows, highs = state[:3], state[3:6]
    for which, (p, q) in enumerate(((0, 1), (0, 2), (1, 2))):
        p_first = starts[p] < starts[q]
        s = jnp.where(p_first, lows[p], lows[q])
        e = jnp.where(p_first, highs[p], highs[q])
        later = jnp.where(p_first, starts[q], starts[p])
        ok = (lows[p] >= 0) & (lows[q] >= 0) & (e > later)
        for k, (b, is_first) in enumerate(((p, p_first), (q, ~p_first))):
            a = jnp.where(is_first, jnp.maximum(s - starts[b], 0), 0)
            z = jnp.where(is_first, chip_rows, jnp.minimum(e - starts[b], chip_rows))
            out[RECT + 4 * which + 2 * k] = a
            out[RECT + 4 * which + 2 * k + 1] = jnp.where(ok, z, a)
    out[SIDE] = core * rows
    out[SIDE + 1] = (1 - core) * rows
    has_first = jnp.where(odd, (chip + 3 < chips) | (chip == chips - 3), chip + 2 < chips)
    has_second = jnp.where(odd, chip >= 3, (chip + 2 < chips) | (chip == chips - 2))
    out[HAS] = has_first.astype(jnp.int32)
    out[HAS + 1] = has_second.astype(jnp.int32)
    out[BASE] = starts[0]


def join_kernel(near_ref, far_ref, own_ref, first_ref):
    both = jnp.maximum(near_ref[...], far_ref[...])
    own_ref[...] = both[0:1]
    first_ref[...] = both[1:2]


def unit_of(raw):
    wide = raw.astype(jnp.float32)
    mean = jnp.sum(wide * wide, axis=1, keepdims=True) * (1.0 / raw.shape[1])
    factor = lax.rsqrt(mean + 1e-06) * (1.0 / math.sqrt(raw.shape[1]))
    return (wide * factor).astype(jnp.bfloat16)


def unit_kernel(first, cuts, raw_ref, *refs):
    outs, (held, sems) = refs[:-2], refs[-2:]
    count, step, _ = held.shape
    copies = []
    for k in range(count):
        rows = raw_ref.at[first + k * step : first + (k + 1) * step]
        copies.append(pltpu.make_async_copy(rows, held.at[k], sems.at[k]))
        copies[-1].start()
    for k, copy in enumerate(copies):
        copy.wait()
        unit = unit_of(held[k])
        for (start, n), out in zip(cuts, outs):
            if start <= k * step < start + n:
                out[k * step - start : (k + 1) * step - start, :] = unit


def units_of(raw, first, rows, cuts):
    depth = raw.shape[1]
    step = math.gcd(128, rows)
    return pl.pallas_call(
        functools.partial(unit_kernel, first, cuts),
        in_specs=[pl.BlockSpec(memory_space=pl.ANY)],
        out_specs=[pl.BlockSpec(memory_space=pltpu.VMEM)] * len(cuts),
        out_shape=[jax.ShapeDtypeStruct((n, depth), jnp.bfloat16) for _, n in cuts],
        scratch_shapes=[
            pltpu.VMEM((rows // step, step, depth), jnp.bfloat16),
            pltpu.SemaphoreType.DMA((rows // step,)),
        ],
        compiler_params=pltpu.CompilerParams(vmem_limit_bytes=VMEM),
        cost_estimate=pl.CostEstimate(
            flops=8 * rows * depth, bytes_accessed=4 * rows * depth, transcendentals=0
        ),
    )(pltpu.with_memory_space_constraint(raw, pltpu.HBM))


def product(left, right):
    return lax.dot_general(
        left, right, (((1,), (1,)), ((), ())), preferred_element_type=jnp.float32
    )


def lanes_max(scores):
    parts = [scores[:, j : j + 128] for j in range(0, scores.shape[1], 128)]
    return functools.reduce(jnp.maximum, parts)


def across(part):
    return jnp.max(part.T, axis=0, keepdims=True)


@dataclasses.dataclass
class Piece:
    rows: jax.Array
    block: int
    side: int
    at: int
    size: int = 0

    @property
    def n(self):
        return self.rows.shape[0]

    def bare(self):
        return dataclasses.replace(self, rows=None, size=self.n)

    def best(self, acc):
        line = 0 if self.block == 2 else self.block
        which = 2 if self.block == 2 else self.side
        return acc[which].at[line : line + 1, self.at : self.at + self.size]


def own_kernel(lefts, rights, table, *refs):
    refs = list(refs)
    lines = [refs.pop(0) for _ in lefts]
    if rights[0].side:
        fars = [refs.pop(0) for _ in rights]
        so_far, best_ref, rowpart = refs
        best_ref[...] = so_far[...]
    else:
        fars = lines
        best_ref, far_ref, second_ref, cap_first, cap_second, rowpart = refs
        for ref in (best_ref, far_ref, second_ref):
            ref[...] = jnp.full(ref.shape, -1.0, jnp.float32)
        for k, ref in enumerate((cap_first, cap_second)):
            ref[...] = jnp.full(ref.shape, jnp.where(table[HAS + k] == 1, BIG, -1.0))
    base = table[BASE]
    for left, left_ref in zip(lefts, lines):
        size = left_ref.shape[0]
        position = base + table[SIDE] + left.at
        position = position + lax.broadcasted_iota(jnp.int32, (size, 1), 0)
        low = jnp.zeros((size, 1), jnp.int32)
        high = jnp.zeros((size, 1), jnp.int32)
        for c in range(SPAN, table.shape[0], 2):
            here = (position >= table[c]) & (position < table[c + 1])
            low = jnp.where(here, table[c], low)
            high = jnp.where(here, table[c + 1], high)
        part = rowpart.at[0:size]
        part[...] = jnp.full(part.shape, -1.0, jnp.float32)
        for right, right_ref in zip(rights, fars):
            start = base + table[SIDE + right.side] + right.at
            scores = product(left_ref[...], right_ref[...])
            column = start + lax.broadcasted_iota(jnp.int32, (1, right_ref.shape[0]), 1)
            keep = (column >= low) & (column < high) & (column != position)
            part[...] = jnp.maximum(part[...], lanes_max(jnp.where(keep, scores, -1.0)))
        best = left.best([best_ref])
        best[...] = jnp.maximum(best[...], across(part[...]))


def own_rows(table, lefts, rights, best):
    bare = lambda pieces: [p.bare() for p in pieces]
    rows, depth = sum(p.n for p in lefts), lefts[0].rows.shape[1]
    shares = (CORES,) if best else (CORES, CORES, 1, 1, 1)
    return vmem_call(
        functools.partial(own_kernel, bare(lefts), bare(rights)),
        [table] + [p.rows for p in (lefts + rights if best else lefts)] + best,
        [jax.ShapeDtypeStruct((n, rows), jnp.float32) for n in shares],
        [pltpu.VMEM((lefts[0].n, 128), jnp.float32)],
        2 * rows * sum(p.n for p in rights) * depth,
    )


PAIRS = {(0, 1): 0, (0, 2): 1, (1, 2): 2}


def rect(table, left, right):
    flip = left.block > right.block
    which = PAIRS[(right.block, left.block) if flip else (left.block, right.block)]
    ends = [table[RECT + 4 * which + k] for k in range(4)]
    if flip:
        ends = ends[2:] + ends[:2]
    x, y = table[SIDE + left.side] + left.at, table[SIDE + right.side] + right.at
    return ends[0] - x, ends[1] - x, ends[2] - y, ends[3] - y


def meet_kernel(pieces, groups, table, *refs):
    refs = list(refs)
    held = [refs.pop(0) for _ in pieces]
    acc_in = [refs.pop(0) for _ in range(3)]
    acc = [refs.pop(0) for _ in range(3)]
    (rowpart,) = refs
    for src, dst in zip(acc_in, acc):
        dst[...] = src[...]
    for l, partners in groups:
        left, left_ref = pieces[l], held[l]
        tm = left_ref.shape[0]
        part = rowpart.at[0:tm]
        part[...] = jnp.full(part.shape, -1.0, jnp.float32)
        shares = {}
        for r in partners:
            shares.setdefault((pieces[r].block, pieces[r].side), []).append(r)
        used = jnp.bool_(False)
        for share in shares.values():
            some = jnp.bool_(False)
            for r in share:
                xa, xb, ya, yb = rect(table, left, pieces[r])
                tn = held[r].shape[0]
                some |= (xa < tm) & (xb > 0) & (ya < tn) & (yb > 0) & (xa < xb) & (ya < yb)
            used |= some

            @pl.when(some)
            def _():
                for r in share:
                    right, right_ref = pieces[r], held[r]
                    tn = right_ref.shape[0]
                    xa, xb, ya, yb = rect(table, left, right)
                    scores = product(left_ref[...], right_ref[...])
                    row = lax.broadcasted_iota(jnp.int32, (tm, 1), 0)
                    col = lax.broadcasted_iota(jnp.int32, (1, tn), 1)
                    keep = ((row >= xa) & (row < xb)) & ((col >= ya) & (col < yb))
                    scores = jnp.where(keep, scores, -1.0)
                    part[...] = jnp.maximum(part[...], lanes_max(scores))
                    best = right.best(acc)
                    best[...] = jnp.maximum(best[...], jnp.max(scores, axis=0, keepdims=True))

        @pl.when(used)
        def _():
            best = left.best(acc)
            best[...] = jnp.maximum(best[...], across(part[...]))


def vmem_call(kernel, ins, outs, scratch, flops, scalars=1):
    vm = pl.BlockSpec(memory_space=pltpu.VMEM)
    sm = pl.BlockSpec(memory_space=pltpu.SMEM)
    pin = lambda x: pltpu.with_memory_space_constraint(x, pltpu.VMEM)
    ins = ins[:scalars] + [pin(x) for x in ins[scalars:]]
    moved = sum(x.size * x.dtype.itemsize for x in [*ins, *outs])
    return pl.pallas_call(
        kernel,
        out_shape=outs,
        in_specs=[sm] * scalars + [vm] * (len(ins) - scalars),
        out_specs=[vm] * len(outs),
        scratch_shapes=scratch,
        compiler_params=pltpu.CompilerParams(vmem_limit_bytes=VMEM),
        cost_estimate=pl.CostEstimate(flops=PACE * flops, bytes_accessed=moved, transcendentals=0),
    )(*ins)


def meet(table, pairs, acc):
    pieces, groups = [], []

    def index(piece):
        for i, other in enumerate(pieces):
            if other is piece:
                return i
        pieces.append(piece)
        return len(pieces) - 1

    for left, rights in pairs:
        groups.append((index(left), [index(r) for r in rights]))
    depth = pieces[0].rows.shape[1]
    flops = sum(2 * left.n * r.n * depth for left, rights in pairs for r in rights)
    most = max(left.n for left, _ in pairs)
    return vmem_call(
        functools.partial(
            meet_kernel, [p.bare() for p in pieces], groups
        ),
        [table] + [p.rows for p in pieces] + list(acc),
        [jax.ShapeDtypeStruct(a.shape, a.dtype) for a in acc],
        [pltpu.VMEM((most, 128), jnp.float32)],
        flops,
    )


def after(value, *others):
    return lax.optimization_barrier((value, *others))[0]


def shards(embeddings, offsets):
    rows, depth = embeddings.shape
    chips = lax.axis_size(AXES) // CORES
    chip_rows = CORES * rows
    first, second = routes(chips)
    to_first, to_second = on_cores(first), on_cores(second)
    swap = [(i, i ^ 1) for i in range(CORES * chips)]
    send = lambda x, pairs: lax.ppermute(x, AXES, pairs)

    spans = chip_rows // MIN_C + 2
    scalars = pl.BlockSpec(memory_space=pltpu.SMEM)
    table = pl.pallas_call(
        functools.partial(plan_kernel, chips, chip_rows, spans),
        out_shape=jax.ShapeDtypeStruct((SPAN + 2 * spans,), jnp.int32),
        in_specs=[scalars],
        out_specs=scalars,
        compiler_params=pltpu.CompilerParams(vmem_limit_bytes=PLAN_VMEM),
    )(offsets)

    eighth = rows // 8
    sizes = [eighth * k for k in SHARES]
    places = [sum(sizes[:k]) for k in range(len(sizes))]
    lead = sizes[0]
    (u1,) = units_of(embeddings, 0, lead, [(0, lead)])
    firsts, seconds = [send(u1, to_first)], [send(u1, to_second)]
    u2, *others = units_of(
        after(embeddings, table),
        lead,
        rows - lead,
        [(0, rows - lead)] + [(p - lead, n) for p, n in zip(places[1:], sizes[1:])][: 2 * (len(sizes) - 2)],
    )
    far1, far2 = send(after(u1, u2), swap), send(u2, swap)
    others = others or [u2]
    firsts.append(send(others[0], to_first))
    seconds.append(send(others[0], to_second))

    own = [Piece(u1, 0, 0, 0), Piece(u2, 0, 0, lead)]
    far = [Piece(far1, 0, 1, 0), Piece(far2, 0, 1, lead)]
    best_near, *blank, cap_first, cap_second = own_rows(table, own, own, [])
    (best_own,) = own_rows(table, own, far, [best_near])
    acc = [best_own, *blank]
    seconds += [send(after(u, best_own), to_second) for u in others[1:]]
    chip_own = own + far

    near_firsts, far_firsts, near_seconds = [], [], []
    for k, at in enumerate(places):
        x = Piece(send(after(firsts[k], acc[0]), swap), 1, 1, at)
        a = Piece(firsts[k], 1, 0, at)
        acc = meet(table, [(a, chip_own + near_seconds)], acc)
        if k == 0:
            firsts += [send(after(u, acc[0]), to_first) for u in others[1:]]
        b = Piece(seconds[k], 2, 0, at)
        near_firsts.append(a)
        far_firsts.append(x)
        pairs = [(b, chip_own + near_firsts + far_firsts)]
        if near_seconds:
            pairs.append((x, list(near_seconds)))
        acc = meet(table, pairs, acc)
        near_seconds.append(b)

    near, far_best, best_second = acc
    line = jax.ShapeDtypeStruct((1, rows), jnp.float32)
    own_best, best_first = vmem_call(
        join_kernel, [near, send(far_best, swap)], [line] * 2, [], rows, scalars=0
    )
    from_second = send(best_second, on_cores(flipped(second)))
    from_first = send(best_first, on_cores(flipped(first)))
    from_first = jnp.minimum(from_first, cap_first)
    from_second = jnp.minimum(from_second, cap_second)
    return jnp.maximum(jnp.maximum(own_best, from_first), from_second).reshape(rows)


def solution(mesh):
    return jax.shard_map(
        shards,
        mesh=mesh,
        in_specs=(P(AXES, None), P()),
        out_specs=P(AXES),
        check_vma=False,
    )
```

```python
import dataclasses
import functools
import math

import jax
import jax.numpy as jnp
from jax import lax
from jax.experimental import pallas as pl
from jax.experimental.pallas import tpu as pltpu
from jax.sharding import PartitionSpec as P

AXES = ("grp", "work")
CORES = 2
MIN_C = 512
TILE = 512
VMEM = 16 * 1024 * 1024
PLAN_VMEM = 1024 * 1024
PACE = 10
SHARES = [4, 2, 2]


def routes(chips):
    last = chips - 1
    first = [(b, b + 1) for b in range(0, chips, 2) if b + 1 != last]
    first += [(b, b + 3) for b in range(1, chips, 2) if b + 3 < chips]
    first += [(last - 2, last)]
    second = [(b, b + 2) for b in range(0, chips, 2) if b + 2 < chips]
    second += [(b, b - 2) for b in range(1, chips, 2) if b >= 3]
    second += [(last - 1, last)]
    return first, second


def on_cores(pairs):
    return [(CORES * s + k, CORES * d + k) for s, d in pairs for k in range(CORES)]


def flipped(pairs):
    return [(d, s) for s, d in pairs]


BIG = 3.0e38
RECT, SIDE, HAS, BASE, SPAN = 0, 12, 14, 16, 17


def plan_kernel(chips, chip_rows, spans, offsets, out):
    me = lax.axis_index(AXES)
    chip, core = lax.div(me, CORES), lax.rem(me, CORES)
    rows = chip_rows // CORES
    odd = lax.rem(chip, 2) == 1
    at_end = chip == chips - 1
    first = jnp.where(odd, jnp.where(at_end, chip - 2, chip - 1), chip - 3)
    second = jnp.where(odd, jnp.where(at_end, chip - 1, chip + 2), chip - 2)
    starts = [b * chip_rows for b in (chip, first, second)]
    for k in range(spans):
        out[SPAN + 2 * k] = 0
        out[SPAN + 2 * k + 1] = 0

    def look(c, state):
        lower, upper = offsets[c], offsets[c + 1]
        lows, highs, count = state[:3], state[3:6], state[6]
        here = (upper > starts[0]) & (lower < starts[0] + chip_rows)

        @pl.when(here)
        def _():
            at = SPAN + 2 * jnp.minimum(count, spans - 1)
            out[at] = lower
            out[at + 1] = upper

        holds = [(lower < s + chip_rows) & (upper >= s + chip_rows) for s in starts]
        lows = [jnp.where(h, lower, v) for h, v in zip(holds, lows)]
        highs = [jnp.where(h, upper, v) for h, v in zip(holds, highs)]
        return (*lows, *highs, count + here.astype(jnp.int32))

    none = jnp.int32(-1)
    state = lax.fori_loop(0, offsets.shape[0] - 1, look, (none,) * 6 + (jnp.int32(0),))
    lows, highs = state[:3], state[3:6]
    for which, (p, q) in enumerate(((0, 1), (0, 2), (1, 2))):
        p_first = starts[p] < starts[q]
        s = jnp.where(p_first, lows[p], lows[q])
        e = jnp.where(p_first, highs[p], highs[q])
        later = jnp.where(p_first, starts[q], starts[p])
        ok = (lows[p] >= 0) & (lows[q] >= 0) & (e > later)
        if which == 0:
            ok &= ~at_end
        for k, (b, is_first) in enumerate(((p, p_first), (q, ~p_first))):
            a = jnp.where(is_first, jnp.maximum(s - starts[b], 0), 0)
            z = jnp.where(is_first, chip_rows, jnp.minimum(e - starts[b], chip_rows))
            out[RECT + 4 * which + 2 * k] = a
            out[RECT + 4 * which + 2 * k + 1] = jnp.where(ok, z, a)
    out[SIDE] = core * rows
    out[SIDE + 1] = (1 - core) * rows
    has_first = jnp.where(odd, (chip + 3 < chips) | (chip == chips - 3), chip + 2 < chips)
    has_second = jnp.where(odd, chip >= 3, (chip + 2 < chips) | (chip == chips - 2))
    out[HAS] = has_first.astype(jnp.int32)
    out[HAS + 1] = has_second.astype(jnp.int32)
    out[BASE] = starts[0]


def join_kernel(near_ref, far_ref, own_ref, first_ref):
    both = jnp.maximum(near_ref[...], far_ref[...])
    own_ref[...] = both[0:1]
    first_ref[...] = both[1:2]


def unit_of(raw):
    wide = raw.astype(jnp.float32)
    mean = jnp.sum(wide * wide, axis=1, keepdims=True) * (1.0 / raw.shape[1])
    factor = lax.rsqrt(mean + 1e-06) * (1.0 / math.sqrt(raw.shape[1]))
    return (wide * factor).astype(jnp.bfloat16)


def unit_kernel(first, cuts, raw_ref, *refs):
    outs, (held, sems) = refs[:-2], refs[-2:]
    count, step, _ = held.shape
    copies = []
    for k in range(count):
        rows = raw_ref.at[first + k * step : first + (k + 1) * step]
        copies.append(pltpu.make_async_copy(rows, held.at[k], sems.at[k]))
        copies[-1].start()
    for k, copy in enumerate(copies):
        copy.wait()
        unit = unit_of(held[k])
        for (start, n), out in zip(cuts, outs):
            if start <= k * step < start + n:
                out[k * step - start : (k + 1) * step - start, :] = unit


def units_of(raw, first, rows, cuts):
    depth = raw.shape[1]
    step = math.gcd(128, rows)
    return pl.pallas_call(
        functools.partial(unit_kernel, first, cuts),
        in_specs=[pl.BlockSpec(memory_space=pl.ANY)],
        out_specs=[pl.BlockSpec(memory_space=pltpu.VMEM)] * len(cuts),
        out_shape=[jax.ShapeDtypeStruct((n, depth), jnp.bfloat16) for _, n in cuts],
        scratch_shapes=[
            pltpu.VMEM((rows // step, step, depth), jnp.bfloat16),
            pltpu.SemaphoreType.DMA((rows // step,)),
        ],
        compiler_params=pltpu.CompilerParams(vmem_limit_bytes=VMEM),
        cost_estimate=pl.CostEstimate(
            flops=8 * rows * depth, bytes_accessed=4 * rows * depth, transcendentals=0
        ),
    )(pltpu.with_memory_space_constraint(raw, pltpu.HBM))


def product(left, right):
    return lax.dot_general(
        left, right, (((1,), (1,)), ((), ())), preferred_element_type=jnp.float32
    )


def lanes_max(scores):
    parts = [scores[:, j : j + 128] for j in range(0, scores.shape[1], 128)]
    return functools.reduce(jnp.maximum, parts)


def across(part):
    return jnp.max(part.T, axis=0, keepdims=True)


@dataclasses.dataclass
class Piece:
    rows: jax.Array
    block: int
    side: int
    at: int
    size: int = 0

    @property
    def n(self):
        return self.rows.shape[0]

    def bare(self):
        return dataclasses.replace(self, rows=None, size=self.n)

    def best(self, acc):
        line = 0 if self.block == 2 else self.block
        which = 2 if self.block == 2 else self.side
        return acc[which].at[line : line + 1, self.at : self.at + self.size]


def own_kernel(lefts, rights, table, *refs):
    refs = list(refs)
    lines = [refs.pop(0) for _ in lefts]
    if rights[0].side:
        fars = [refs.pop(0) for _ in rights]
        so_far, best_ref, rowpart = refs
        best_ref[...] = so_far[...]
    else:
        fars = lines
        best_ref, far_ref, second_ref, cap_first, cap_second, rowpart = refs
        for ref in (best_ref, far_ref, second_ref):
            ref[...] = jnp.full(ref.shape, -1.0, jnp.float32)
        for k, ref in enumerate((cap_first, cap_second)):
            ref[...] = jnp.full(ref.shape, jnp.where(table[HAS + k] == 1, BIG, -1.0))
    base = table[BASE]
    for left, left_ref in zip(lefts, lines):
        size = left_ref.shape[0]
        position = base + table[SIDE] + left.at
        position = position + lax.broadcasted_iota(jnp.int32, (size, 1), 0)
        low = jnp.zeros((size, 1), jnp.int32)
        high = jnp.zeros((size, 1), jnp.int32)
        for c in range(SPAN, table.shape[0], 2):
            here = (position >= table[c]) & (position < table[c + 1])
            low = jnp.where(here, table[c], low)
            high = jnp.where(here, table[c + 1], high)
        part = rowpart.at[0:size]
        part[...] = jnp.full(part.shape, -1.0, jnp.float32)
        for right, right_ref in zip(rights, fars):
            start = base + table[SIDE + right.side] + right.at
            scores = product(left_ref[...], right_ref[...])
            column = start + lax.broadcasted_iota(jnp.int32, (1, right_ref.shape[0]), 1)
            keep = (column >= low) & (column < high) & (column != position)
            part[...] = jnp.maximum(part[...], lanes_max(jnp.where(keep, scores, -1.0)))
        best = left.best([best_ref])
        best[...] = jnp.maximum(best[...], across(part[...]))


def own_rows(table, lefts, rights, best):
    bare = lambda pieces: [p.bare() for p in pieces]
    rows, depth = sum(p.n for p in lefts), lefts[0].rows.shape[1]
    shares = (CORES,) if best else (CORES, CORES, 1, 1, 1)
    return vmem_call(
        functools.partial(own_kernel, bare(lefts), bare(rights)),
        [table] + [p.rows for p in (lefts + rights if best else lefts)] + best,
        [jax.ShapeDtypeStruct((n, rows), jnp.float32) for n in shares],
        [pltpu.VMEM((lefts[0].n, 128), jnp.float32)],
        2 * rows * sum(p.n for p in rights) * depth,
    )


PAIRS = {(0, 1): 0, (0, 2): 1, (1, 2): 2}


def rect(table, left, right):
    flip = left.block > right.block
    which = PAIRS[(right.block, left.block) if flip else (left.block, right.block)]
    ends = [table[RECT + 4 * which + k] for k in range(4)]
    if flip:
        ends = ends[2:] + ends[:2]
    x, y = table[SIDE + left.side] + left.at, table[SIDE + right.side] + right.at
    return ends[0] - x, ends[1] - x, ends[2] - y, ends[3] - y


def meet_kernel(pieces, groups, table, *refs):
    refs = list(refs)
    held = [refs.pop(0) for _ in pieces]
    acc_in = [refs.pop(0) for _ in range(3)]
    acc = [refs.pop(0) for _ in range(3)]
    (rowpart,) = refs
    for src, dst in zip(acc_in, acc):
        dst[...] = src[...]
    for l, partners in groups:
        left, left_ref = pieces[l], held[l]
        tm = left_ref.shape[0]
        part = rowpart.at[0:tm]
        part[...] = jnp.full(part.shape, -1.0, jnp.float32)
        shares = {}
        for r in partners:
            shares.setdefault((pieces[r].block, pieces[r].side), []).append(r)
        used = jnp.bool_(False)
        for share in shares.values():
            some = jnp.bool_(False)
            for r in share:
                xa, xb, ya, yb = rect(table, left, pieces[r])
                tn = held[r].shape[0]
                some |= (xa < tm) & (xb > 0) & (ya < tn) & (yb > 0) & (xa < xb) & (ya < yb)
            used |= some

            @pl.when(some)
            def _():
                for r in share:
                    right, right_ref = pieces[r], held[r]
                    tn = right_ref.shape[0]
                    xa, xb, ya, yb = rect(table, left, right)
                    scores = product(left_ref[...], right_ref[...])
                    row = lax.broadcasted_iota(jnp.int32, (tm, 1), 0)
                    col = lax.broadcasted_iota(jnp.int32, (1, tn), 1)
                    keep = ((row >= xa) & (row < xb)) & ((col >= ya) & (col < yb))
                    scores = jnp.where(keep, scores, -1.0)
                    part[...] = jnp.maximum(part[...], lanes_max(scores))
                    best = right.best(acc)
                    best[...] = jnp.maximum(best[...], jnp.max(scores, axis=0, keepdims=True))

        @pl.when(used)
        def _():
            best = left.best(acc)
            best[...] = jnp.maximum(best[...], across(part[...]))


def vmem_call(kernel, ins, outs, scratch, flops, scalars=1):
    vm = pl.BlockSpec(memory_space=pltpu.VMEM)
    sm = pl.BlockSpec(memory_space=pltpu.SMEM)
    pin = lambda x: pltpu.with_memory_space_constraint(x, pltpu.VMEM)
    ins = ins[:scalars] + [pin(x) for x in ins[scalars:]]
    moved = sum(x.size * x.dtype.itemsize for x in [*ins, *outs])
    return pl.pallas_call(
        kernel,
        out_shape=outs,
        in_specs=[sm] * scalars + [vm] * (len(ins) - scalars),
        out_specs=[vm] * len(outs),
        scratch_shapes=scratch,
        compiler_params=pltpu.CompilerParams(vmem_limit_bytes=VMEM),
        cost_estimate=pl.CostEstimate(flops=PACE * flops, bytes_accessed=moved, transcendentals=0),
    )(*ins)


def meet(table, pairs, acc):
    pieces, groups = [], []

    def index(piece):
        for i, other in enumerate(pieces):
            if other is piece:
                return i
        pieces.append(piece)
        return len(pieces) - 1

    for left, rights in pairs:
        groups.append((index(left), [index(r) for r in rights]))
    depth = pieces[0].rows.shape[1]
    flops = sum(2 * left.n * r.n * depth for left, rights in pairs for r in rights)
    most = max(left.n for left, _ in pairs)
    return vmem_call(
        functools.partial(
            meet_kernel, [p.bare() for p in pieces], groups
        ),
        [table] + [p.rows for p in pieces] + list(acc),
        [jax.ShapeDtypeStruct(a.shape, a.dtype) for a in acc],
        [pltpu.VMEM((most, 128), jnp.float32)],
        flops,
    )


def after(value, *others):
    return lax.optimization_barrier((value, *others))[0]


def shards(embeddings, offsets):
    rows, depth = embeddings.shape
    chips = lax.axis_size(AXES) // CORES
    chip_rows = CORES * rows
    first, second = routes(chips)
    to_first, to_second = on_cores(first), on_cores(second)
    swap = [(i, i ^ 1) for i in range(CORES * chips)]
    send = lambda x, pairs: lax.ppermute(x, AXES, pairs)

    spans = chip_rows // MIN_C + 2
    scalars = pl.BlockSpec(memory_space=pltpu.SMEM)
    table = pl.pallas_call(
        functools.partial(plan_kernel, chips, chip_rows, spans),
        out_shape=jax.ShapeDtypeStruct((SPAN + 2 * spans,), jnp.int32),
        in_specs=[scalars],
        out_specs=scalars,
        compiler_params=pltpu.CompilerParams(vmem_limit_bytes=PLAN_VMEM),
    )(offsets)

    eighth = rows // 8
    sizes = [eighth * k for k in SHARES]
    places = [sum(sizes[:k]) for k in range(len(sizes))]
    lead = sizes[0]
    (u1,) = units_of(embeddings, 0, lead, [(0, lead)])
    firsts, seconds = [send(u1, to_first)], [send(u1, to_second)]
    u2, *others = units_of(
        after(embeddings, table),
        lead,
        rows - lead,
        [(0, rows - lead)] + [(p - lead, n) for p, n in zip(places[1:], sizes[1:])][: 2 * (len(sizes) - 2)],
    )
    far1, far2 = send(after(u1, u2), swap), send(u2, swap)
    others = others or [u2]
    firsts.append(send(others[0], to_first))
    seconds.append(send(others[0], to_second))

    own = [Piece(u1, 0, 0, 0), Piece(u2, 0, 0, lead)]
    far = [Piece(far1, 0, 1, 0), Piece(far2, 0, 1, lead)]
    best_near, *blank, cap_first, cap_second = own_rows(table, own, own, [])
    (best_own,) = own_rows(table, own, far, [best_near])
    acc = [best_own, *blank]
    seconds += [send(after(u, best_near), to_second) for u in others[1:]]
    chip_own = own + far

    near_firsts, far_firsts, near_seconds = [], [], []
    for k, at in enumerate(places[:-1]):
        x = Piece(send(after(firsts[k], acc[0]), swap), 1, 1, at)
        a = Piece(firsts[k], 1, 0, at)
        acc = meet(table, [(a, chip_own + near_seconds)], acc)
        if k == 0:
            firsts += [send(after(u, acc[0]), to_first) for u in others[1:]]
        b = Piece(seconds[k], 2, 0, at)
        near_firsts.append(a)
        far_firsts.append(x)
        pairs = [(b, chip_own + near_firsts + far_firsts)]
        if near_seconds:
            pairs.append((x, list(near_seconds)))
        acc = meet(table, pairs, acc)
        near_seconds.append(b)
    at = places[-1]
    b = Piece(seconds[-1], 2, 0, at)
    acc = meet(table, [(b, chip_own + near_firsts + far_firsts)], acc)
    near_seconds.append(b)
    x = Piece(send(after(firsts[-1], acc[0]), swap), 1, 1, at)
    acc = meet(table, [(Piece(firsts[-1], 1, 0, at), chip_own + near_seconds)], acc)
    acc = meet(table, [(x, near_seconds)], acc)

    near, far_best, best_second = acc
    line = jax.ShapeDtypeStruct((1, rows), jnp.float32)
    own_best, best_first = vmem_call(
        join_kernel, [near, send(far_best, swap)], [line] * 2, [], rows, scalars=0
    )
    from_second = send(best_second, on_cores(flipped(second)))
    from_first = send(best_first, on_cores(flipped(first)))
    from_first = jnp.minimum(from_first, cap_first)
    from_second = jnp.minimum(from_second, cap_second)
    return jnp.maximum(jnp.maximum(own_best, from_first), from_second).reshape(rows)


def solution(mesh):
    return jax.shard_map(
        shards,
        mesh=mesh,
        in_specs=(P(AXES, None), P()),
        out_specs=P(AXES),
        check_vma=False,
    )
```

```python
import dataclasses
import functools
import math

import jax
import jax.numpy as jnp
from jax import lax
from jax.experimental import pallas as pl
from jax.experimental.pallas import tpu as pltpu
from jax.sharding import PartitionSpec as P

AXES = ("grp", "work")
CORES = 2
MIN_C = 512
VMEM = 16 * 1024 * 1024
PLAN_VMEM = 1024 * 1024
PACE = 10
FIRST_SHARES = (4, 2, 2)
SECOND_SHARES = (4, 2, 2)


def routes(chips):
    last = chips - 1
    first = [(b, b + 1) for b in range(0, chips, 2) if b + 1 != last]
    first += [(b, b + 3) for b in range(1, chips, 2) if b + 3 < chips]
    first += [(last - 2, last)]
    second = [(b, b + 2) for b in range(0, chips, 2) if b + 2 < chips]
    second += [(b, b - 2) for b in range(1, chips, 2) if b >= 3]
    second += [(last - 1, last)]
    return first, second


def on_cores(pairs):
    return [(CORES * s + k, CORES * d + k) for s, d in pairs for k in range(CORES)]


def flipped(pairs):
    return [(d, s) for s, d in pairs]


BIG = 3.0e38
RECT, SIDE, HAS, BASE, SPAN = 0, 12, 14, 16, 17


def plan_kernel(chips, chip_rows, spans, offsets, out):
    me = lax.axis_index(AXES)
    chip, core = lax.div(me, CORES), lax.rem(me, CORES)
    rows = chip_rows // CORES
    odd = lax.rem(chip, 2) == 1
    at_end = chip == chips - 1
    first = jnp.where(odd, jnp.where(at_end, chip - 2, chip - 1), chip - 3)
    second = jnp.where(odd, jnp.where(at_end, chip - 1, chip + 2), chip - 2)
    starts = [b * chip_rows for b in (chip, first, second)]
    for k in range(spans):
        out[SPAN + 2 * k] = 0
        out[SPAN + 2 * k + 1] = 0

    def look(c, state):
        lower, upper = offsets[c], offsets[c + 1]
        lows, highs, count = state[:3], state[3:6], state[6]
        here = (upper > starts[0]) & (lower < starts[0] + chip_rows)

        @pl.when(here)
        def _():
            at = SPAN + 2 * jnp.minimum(count, spans - 1)
            out[at] = lower
            out[at + 1] = upper

        holds = [(lower < s + chip_rows) & (upper >= s + chip_rows) for s in starts]
        lows = [jnp.where(h, lower, v) for h, v in zip(holds, lows)]
        highs = [jnp.where(h, upper, v) for h, v in zip(holds, highs)]
        return (*lows, *highs, count + here.astype(jnp.int32))

    none = jnp.int32(-1)
    state = lax.fori_loop(0, offsets.shape[0] - 1, look, (none,) * 6 + (jnp.int32(0),))
    lows, highs = state[:3], state[3:6]
    for which, (p, q) in enumerate(((0, 1), (0, 2), (1, 2))):
        p_first = starts[p] < starts[q]
        s = jnp.where(p_first, lows[p], lows[q])
        e = jnp.where(p_first, highs[p], highs[q])
        later = jnp.where(p_first, starts[q], starts[p])
        ok = (lows[p] >= 0) & (lows[q] >= 0) & (e > later)
        if which == 0:
            ok &= ~at_end
        for k, (b, is_first) in enumerate(((p, p_first), (q, ~p_first))):
            a = jnp.where(is_first, jnp.maximum(s - starts[b], 0), 0)
            z = jnp.where(is_first, chip_rows, jnp.minimum(e - starts[b], chip_rows))
            out[RECT + 4 * which + 2 * k] = a
            out[RECT + 4 * which + 2 * k + 1] = jnp.where(ok, z, a)
    out[SIDE] = core * rows
    out[SIDE + 1] = (1 - core) * rows
    has_first = jnp.where(odd, (chip + 3 < chips) | (chip == chips - 3), chip + 2 < chips)
    has_second = jnp.where(odd, chip >= 3, (chip + 2 < chips) | (chip == chips - 2))
    out[HAS] = has_first.astype(jnp.int32)
    out[HAS + 1] = has_second.astype(jnp.int32)
    out[BASE] = starts[0]


def join_kernel(near_ref, far_ref, own_ref, first_ref):
    both = jnp.maximum(near_ref[...], far_ref[...])
    own_ref[...] = both[0:1]
    first_ref[...] = both[1:2]


def unit_of(raw):
    wide = raw.astype(jnp.float32)
    mean = jnp.sum(wide * wide, axis=1, keepdims=True) * (1.0 / raw.shape[1])
    factor = lax.rsqrt(mean + 1e-06) * (1.0 / math.sqrt(raw.shape[1]))
    return (wide * factor).astype(jnp.bfloat16)


def unit_kernel(first, cuts, raw_ref, *refs):
    outs, (held, sems) = refs[:-2], refs[-2:]
    count, step, _ = held.shape
    copies = []
    for k in range(count):
        rows = raw_ref.at[first + k * step : first + (k + 1) * step]
        copies.append(pltpu.make_async_copy(rows, held.at[k], sems.at[k]))
        copies[-1].start()
    for k, copy in enumerate(copies):
        copy.wait()
        part = math.gcd(128, step)
        for at in range(0, step, part):
            unit = unit_of(held[k, at : at + part, :])
            for (start, n), out in zip(cuts, outs):
                row = k * step + at - start
                if 0 <= row < n:
                    out[row : row + part, :] = unit


def units_of(raw, first, rows, cuts):
    depth = raw.shape[1]
    step = math.gcd(256, rows)
    return pl.pallas_call(
        functools.partial(unit_kernel, first, cuts),
        in_specs=[pl.BlockSpec(memory_space=pl.ANY)],
        out_specs=[pl.BlockSpec(memory_space=pltpu.VMEM)] * len(cuts),
        out_shape=[jax.ShapeDtypeStruct((n, depth), jnp.bfloat16) for _, n in cuts],
        scratch_shapes=[
            pltpu.VMEM((rows // step, step, depth), jnp.bfloat16),
            pltpu.SemaphoreType.DMA((rows // step,)),
        ],
        compiler_params=pltpu.CompilerParams(vmem_limit_bytes=VMEM),
        cost_estimate=pl.CostEstimate(
            flops=8 * rows * depth, bytes_accessed=4 * rows * depth, transcendentals=0
        ),
    )(pltpu.with_memory_space_constraint(raw, pltpu.HBM))


def product(left, right):
    return lax.dot_general(
        left, right, (((1,), (1,)), ((), ())), preferred_element_type=jnp.float32
    )


def lanes_max(scores):
    parts = [scores[:, j : j + 128] for j in range(0, scores.shape[1], 128)]
    return functools.reduce(jnp.maximum, parts)


def across(part):
    return jnp.max(part.T, axis=0, keepdims=True)


@dataclasses.dataclass
class Piece:
    rows: jax.Array
    block: int
    side: int
    at: int
    size: int = 0

    @property
    def n(self):
        return self.rows.shape[0]

    def bare(self):
        return dataclasses.replace(self, rows=None, size=self.n)

    def best(self, acc):
        line = 0 if self.block == 2 else self.block
        which = 2 if self.block == 2 else self.side
        return acc[which].at[line : line + 1, self.at : self.at + self.size]


def own_kernel(lefts, rights, table, *refs):
    refs = list(refs)
    lines = [refs.pop(0) for _ in lefts]
    if rights[0].side:
        fars = [refs.pop(0) for _ in rights]
        so_far, best_ref, rowpart = refs
        best_ref[...] = so_far[...]
    else:
        fars = lines
        best_ref, far_ref, second_ref, cap_first, cap_second, rowpart = refs
        for ref in (best_ref, far_ref, second_ref):
            ref[...] = jnp.full(ref.shape, -1.0, jnp.float32)
        for k, ref in enumerate((cap_first, cap_second)):
            ref[...] = jnp.full(ref.shape, jnp.where(table[HAS + k] == 1, BIG, -1.0))
    base = table[BASE]
    for left, left_ref in zip(lefts, lines):
        size = left_ref.shape[0]
        position = base + table[SIDE] + left.at
        position = position + lax.broadcasted_iota(jnp.int32, (size, 1), 0)
        low = jnp.zeros((size, 1), jnp.int32)
        high = jnp.zeros((size, 1), jnp.int32)
        for c in range(SPAN, table.shape[0], 2):
            here = (position >= table[c]) & (position < table[c + 1])
            low = jnp.where(here, table[c], low)
            high = jnp.where(here, table[c + 1], high)
        part = rowpart.at[0:size]
        part[...] = jnp.full(part.shape, -1.0, jnp.float32)
        for right, right_ref in zip(rights, fars):
            start = base + table[SIDE + right.side] + right.at
            scores = product(left_ref[...], right_ref[...])
            column = start + lax.broadcasted_iota(jnp.int32, (1, right_ref.shape[0]), 1)
            keep = (column >= low) & (column < high) & (column != position)
            part[...] = jnp.maximum(part[...], lanes_max(jnp.where(keep, scores, -1.0)))
        best = left.best([best_ref])
        best[...] = jnp.maximum(best[...], across(part[...]))


def own_rows(table, lefts, rights, best):
    bare = lambda pieces: [p.bare() for p in pieces]
    rows, depth = sum(p.n for p in lefts), lefts[0].rows.shape[1]
    shares = (CORES,) if best else (CORES, CORES, 1, 1, 1)
    return vmem_call(
        functools.partial(own_kernel, bare(lefts), bare(rights)),
        [table] + [p.rows for p in (lefts + rights if best else lefts)] + best,
        [jax.ShapeDtypeStruct((n, rows), jnp.float32) for n in shares],
        [pltpu.VMEM((max(p.n for p in lefts), 128), jnp.float32)],
        2 * rows * sum(p.n for p in rights) * depth,
    )


PAIRS = {(0, 1): 0, (0, 2): 1, (1, 2): 2}


def rect(table, left, right):
    flip = left.block > right.block
    which = PAIRS[(right.block, left.block) if flip else (left.block, right.block)]
    ends = [table[RECT + 4 * which + k] for k in range(4)]
    if flip:
        ends = ends[2:] + ends[:2]
    x, y = table[SIDE + left.side] + left.at, table[SIDE + right.side] + right.at
    return ends[0] - x, ends[1] - x, ends[2] - y, ends[3] - y


def meet_kernel(pieces, groups, table, *refs):
    refs = list(refs)
    held = [refs.pop(0) for _ in pieces]
    acc_in = [refs.pop(0) for _ in range(3)]
    acc = [refs.pop(0) for _ in range(3)]
    (rowpart,) = refs
    for src, dst in zip(acc_in, acc):
        dst[...] = src[...]
    for l, partners in groups:
        left, left_ref = pieces[l], held[l]
        tm = left_ref.shape[0]
        part = rowpart.at[0:tm]
        part[...] = jnp.full(part.shape, -1.0, jnp.float32)
        shares = {}
        for r in partners:
            shares.setdefault((pieces[r].block, pieces[r].side), []).append(r)
        used = jnp.bool_(False)
        for share in shares.values():
            some = jnp.bool_(False)
            for r in share:
                xa, xb, ya, yb = rect(table, left, pieces[r])
                tn = held[r].shape[0]
                some |= (xa < tm) & (xb > 0) & (ya < tn) & (yb > 0) & (xa < xb) & (ya < yb)
            used |= some

            @pl.when(some)
            def _():
                for r in share:
                    right, right_ref = pieces[r], held[r]
                    tn = right_ref.shape[0]
                    xa, xb, ya, yb = rect(table, left, right)
                    scores = product(left_ref[...], right_ref[...])
                    row = lax.broadcasted_iota(jnp.int32, (tm, 1), 0)
                    col = lax.broadcasted_iota(jnp.int32, (1, tn), 1)
                    keep = ((row >= xa) & (row < xb)) & ((col >= ya) & (col < yb))
                    scores = jnp.where(keep, scores, -1.0)
                    part[...] = jnp.maximum(part[...], lanes_max(scores))
                    best = right.best(acc)
                    best[...] = jnp.maximum(best[...], jnp.max(scores, axis=0, keepdims=True))

        @pl.when(used)
        def _():
            best = left.best(acc)
            best[...] = jnp.maximum(best[...], across(part[...]))


def vmem_call(kernel, ins, outs, scratch, flops, scalars=1):
    vm = pl.BlockSpec(memory_space=pltpu.VMEM)
    sm = pl.BlockSpec(memory_space=pltpu.SMEM)
    pin = lambda x: pltpu.with_memory_space_constraint(x, pltpu.VMEM)
    ins = ins[:scalars] + [pin(x) for x in ins[scalars:]]
    moved = sum(x.size * x.dtype.itemsize for x in [*ins, *outs])
    return pl.pallas_call(
        kernel,
        out_shape=outs,
        in_specs=[sm] * scalars + [vm] * (len(ins) - scalars),
        out_specs=[vm] * len(outs),
        scratch_shapes=scratch,
        compiler_params=pltpu.CompilerParams(vmem_limit_bytes=VMEM),
        cost_estimate=pl.CostEstimate(flops=PACE * flops, bytes_accessed=moved, transcendentals=0),
    )(*ins)


def meet(table, pairs, acc):
    pieces, groups = [], []

    def index(piece):
        for i, other in enumerate(pieces):
            if other is piece:
                return i
        pieces.append(piece)
        return len(pieces) - 1

    for left, rights in pairs:
        groups.append((index(left), [index(r) for r in rights]))
    depth = pieces[0].rows.shape[1]
    flops = sum(2 * left.n * r.n * depth for left, rights in pairs for r in rights)
    most = max(left.n for left, _ in pairs)
    return vmem_call(
        functools.partial(
            meet_kernel, [p.bare() for p in pieces], groups
        ),
        [table] + [p.rows for p in pieces] + list(acc),
        [jax.ShapeDtypeStruct(a.shape, a.dtype) for a in acc],
        [pltpu.VMEM((most, 128), jnp.float32)],
        flops,
    )


def cuts_of(rows, shares):
    sizes = [rows * k // sum(shares) for k in shares]
    return [(sum(sizes[:i]), n) for i, n in enumerate(sizes)]


def after(value, *others):
    return lax.optimization_barrier((value, *others))[0]


def shards(embeddings, offsets):
    rows, depth = embeddings.shape
    chips = lax.axis_size(AXES) // CORES
    chip_rows = CORES * rows
    first, second = routes(chips)
    to_first, to_second = on_cores(first), on_cores(second)
    swap = [(i, i ^ 1) for i in range(CORES * chips)]
    send = lambda x, pairs: lax.ppermute(x, AXES, pairs)

    spans = chip_rows // MIN_C + 2
    scalars = pl.BlockSpec(memory_space=pltpu.SMEM)
    table = pl.pallas_call(
        functools.partial(plan_kernel, chips, chip_rows, spans),
        out_shape=jax.ShapeDtypeStruct((SPAN + 2 * spans,), jnp.int32),
        in_specs=[scalars],
        out_specs=scalars,
        compiler_params=pltpu.CompilerParams(vmem_limit_bytes=PLAN_VMEM),
    )(offsets)

    first_cuts, second_cuts = cuts_of(rows, FIRST_SHARES), cuts_of(rows, SECOND_SHARES)
    lead = first_cuts[0][1]
    (u1,) = units_of(embeddings, 0, lead, [(0, lead)])
    firsts, seconds = [send(u1, to_first)], [send(u1, to_second)]
    rest = first_cuts[1:] + second_cuts[1:]
    cuts = list(dict.fromkeys([(lead, rows - lead)] + rest))
    u2, *_ = units = units_of(
        after(embeddings, table), lead, rows - lead, [(at - lead, n) for at, n in cuts]
    )
    unit = dict(zip(cuts, units))
    far1, far2 = send(after(u1, u2), swap), send(u2, swap)
    firsts.append(send(unit[first_cuts[1]], to_first))
    seconds.append(send(unit[second_cuts[1]], to_second))

    own = [Piece(u1, 0, 0, 0), Piece(u2, 0, 0, lead)]
    far = [Piece(far1, 0, 1, 0), Piece(far2, 0, 1, lead)]
    best_near, *blank, cap_first, cap_second = own_rows(table, own, own, [])
    (best_own,) = own_rows(table, own, far, [best_near])
    acc = [best_own, *blank]
    chip_own = own + far

    near_firsts, far_firsts, near_seconds = [], [], []
    for k in range(len(first_cuts) - 1):
        b = Piece(seconds[k], 2, 0, second_cuts[k][0])
        acc = meet(table, [(b, chip_own)], acc)
        if k == 0:
            firsts += [send(after(unit[c], acc[0]), to_first) for c in first_cuts[2:]]
            seconds += [send(after(unit[c], acc[0]), to_second) for c in second_cuts[2:]]
        near_seconds.append(b)
        at = first_cuts[k][0]
        x = Piece(send(after(firsts[k], acc[0]), swap), 1, 1, at)
        a = Piece(firsts[k], 1, 0, at)
        pairs = [(a, chip_own + near_seconds)]
        if near_firsts:
            pairs.append((b, near_firsts + far_firsts))
        acc = meet(table, pairs, acc)
        acc = meet(table, [(x, list(near_seconds))], acc)
        near_firsts.append(a)
        far_firsts.append(x)
    at = first_cuts[-1][0]
    x = Piece(send(after(firsts[-1], acc[0]), swap), 1, 1, at)
    a, b = Piece(firsts[-1], 1, 0, at), Piece(seconds[-1], 2, 0, second_cuts[-1][0])
    acc = meet(table, [(a, chip_own + near_seconds)], acc)
    pairs = [(b, chip_own + near_firsts + [a] + far_firsts + [x]), (x, near_seconds)]
    acc = meet(table, pairs, acc)

    near, far_best, best_second = acc
    line = jax.ShapeDtypeStruct((1, rows), jnp.float32)
    own_best, best_first = vmem_call(
        join_kernel, [near, send(far_best, swap)], [line] * 2, [], rows, scalars=0
    )
    from_second = send(best_second, on_cores(flipped(second)))
    from_first = send(best_first, on_cores(flipped(first)))
    from_first = jnp.minimum(from_first, cap_first)
    from_second = jnp.minimum(from_second, cap_second)
    return jnp.maximum(jnp.maximum(own_best, from_first), from_second).reshape(rows)


def solution(mesh):
    return jax.shard_map(
        shards,
        mesh=mesh,
        in_specs=(P(AXES, None), P()),
        out_specs=P(AXES),
        check_vma=False,
    )
```

```python
import dataclasses
import functools
import math

import jax
import jax.numpy as jnp
from jax import lax
from jax.experimental import pallas as pl
from jax.experimental.pallas import tpu as pltpu
from jax.sharding import PartitionSpec as P

AXES = ("grp", "work")
CORES = 2
MIN_C = 512
TILE = 512
VMEM = 16 * 1024 * 1024
PLAN_VMEM = 1024 * 1024
PACE = 10
SHARES = [4, 2, 2]


def routes(chips):
    last = chips - 1
    first = [(b, b + 1) for b in range(0, chips, 2) if b + 1 != last]
    first += [(b, b + 3) for b in range(1, chips, 2) if b + 3 < chips]
    first += [(last - 2, last)]
    second = [(b, b + 2) for b in range(0, chips, 2) if b + 2 < chips]
    second += [(b, b - 2) for b in range(1, chips, 2) if b >= 3]
    second += [(last - 1, last)]
    return first, second


def on_cores(pairs):
    return [(CORES * s + k, CORES * d + k) for s, d in pairs for k in range(CORES)]


def flipped(pairs):
    return [(d, s) for s, d in pairs]


BIG = 3.0e38
RECT, SIDE, HAS, BASE, SPAN = 0, 12, 14, 16, 17


def plan_kernel(chips, chip_rows, spans, offsets, out):
    me = lax.axis_index(AXES)
    chip, core = lax.div(me, CORES), lax.rem(me, CORES)
    rows = chip_rows // CORES
    odd = lax.rem(chip, 2) == 1
    at_end = chip == chips - 1
    first = jnp.where(odd, jnp.where(at_end, chip - 2, chip - 1), chip - 3)
    second = jnp.where(odd, jnp.where(at_end, chip - 1, chip + 2), chip - 2)
    starts = [b * chip_rows for b in (chip, first, second)]
    for k in range(spans):
        out[SPAN + 2 * k] = 0
        out[SPAN + 2 * k + 1] = 0

    def look(c, state):
        lower, upper = offsets[c], offsets[c + 1]
        lows, highs, count = state[:3], state[3:6], state[6]
        here = (upper > starts[0]) & (lower < starts[0] + chip_rows)

        @pl.when(here)
        def _():
            at = SPAN + 2 * jnp.minimum(count, spans - 1)
            out[at] = lower
            out[at + 1] = upper

        holds = [(lower < s + chip_rows) & (upper >= s + chip_rows) for s in starts]
        lows = [jnp.where(h, lower, v) for h, v in zip(holds, lows)]
        highs = [jnp.where(h, upper, v) for h, v in zip(holds, highs)]
        return (*lows, *highs, count + here.astype(jnp.int32))

    none = jnp.int32(-1)
    state = lax.fori_loop(0, offsets.shape[0] - 1, look, (none,) * 6 + (jnp.int32(0),))
    lows, highs = state[:3], state[3:6]
    for which, (p, q) in enumerate(((0, 1), (0, 2), (1, 2))):
        p_first = starts[p] < starts[q]
        s = jnp.where(p_first, lows[p], lows[q])
        e = jnp.where(p_first, highs[p], highs[q])
        later = jnp.where(p_first, starts[q], starts[p])
        ok = (lows[p] >= 0) & (lows[q] >= 0) & (e > later)
        if which == 0:
            ok &= ~at_end
        for k, (b, is_first) in enumerate(((p, p_first), (q, ~p_first))):
            a = jnp.where(is_first, jnp.maximum(s - starts[b], 0), 0)
            z = jnp.where(is_first, chip_rows, jnp.minimum(e - starts[b], chip_rows))
            out[RECT + 4 * which + 2 * k] = a
            out[RECT + 4 * which + 2 * k + 1] = jnp.where(ok, z, a)
    out[SIDE] = core * rows
    out[SIDE + 1] = (1 - core) * rows
    has_first = jnp.where(odd, (chip + 3 < chips) | (chip == chips - 3), chip + 2 < chips)
    has_second = jnp.where(odd, chip >= 3, (chip + 2 < chips) | (chip == chips - 2))
    out[HAS] = has_first.astype(jnp.int32)
    out[HAS + 1] = has_second.astype(jnp.int32)
    out[BASE] = starts[0]


def join_kernel(near_ref, far_ref, own_ref, first_ref):
    both = jnp.maximum(near_ref[...], far_ref[...])
    own_ref[...] = both[0:1]
    first_ref[...] = both[1:2]


def unit_of(raw):
    wide = raw.astype(jnp.float32)
    mean = jnp.sum(wide * wide, axis=1, keepdims=True) * (1.0 / raw.shape[1])
    factor = lax.rsqrt(mean + 1e-06) * (1.0 / math.sqrt(raw.shape[1]))
    return (wide * factor).astype(jnp.bfloat16)


def unit_kernel(first, cuts, raw_ref, *refs):
    outs, (held, sems) = refs[:-2], refs[-2:]
    count, step, _ = held.shape
    copies = []
    for k in range(count):
        rows = raw_ref.at[first + k * step : first + (k + 1) * step]
        copies.append(pltpu.make_async_copy(rows, held.at[k], sems.at[k]))
        copies[-1].start()
    for k, copy in enumerate(copies):
        copy.wait()
        part = math.gcd(128, step)
        for at in range(0, step, part):
            unit = unit_of(held[k, at : at + part, :])
            for (start, n), out in zip(cuts, outs):
                row = k * step + at - start
                if 0 <= row < n:
                    out[row : row + part, :] = unit


def units_of(raw, first, rows, cuts):
    depth = raw.shape[1]
    step = math.gcd(256, rows)
    return pl.pallas_call(
        functools.partial(unit_kernel, first, cuts),
        in_specs=[pl.BlockSpec(memory_space=pl.ANY)],
        out_specs=[pl.BlockSpec(memory_space=pltpu.VMEM)] * len(cuts),
        out_shape=[jax.ShapeDtypeStruct((n, depth), jnp.bfloat16) for _, n in cuts],
        scratch_shapes=[
            pltpu.VMEM((rows // step, step, depth), jnp.bfloat16),
            pltpu.SemaphoreType.DMA((rows // step,)),
        ],
        compiler_params=pltpu.CompilerParams(vmem_limit_bytes=VMEM),
        cost_estimate=pl.CostEstimate(
            flops=8 * rows * depth, bytes_accessed=4 * rows * depth, transcendentals=0
        ),
    )(pltpu.with_memory_space_constraint(raw, pltpu.HBM))


def product(left, right):
    return lax.dot_general(
        left, right, (((1,), (1,)), ((), ())), preferred_element_type=jnp.float32
    )


def lanes_max(scores):
    parts = [scores[:, j : j + 128] for j in range(0, scores.shape[1], 128)]
    return functools.reduce(jnp.maximum, parts)


def across(part):
    return jnp.max(part.T, axis=0, keepdims=True)


@dataclasses.dataclass
class Piece:
    rows: jax.Array
    block: int
    side: int
    at: int
    size: int = 0

    @property
    def n(self):
        return self.rows.shape[0]

    def bare(self):
        return dataclasses.replace(self, rows=None, size=self.n)

    def best(self, acc):
        line = 0 if self.block == 2 else self.block
        which = 2 if self.block == 2 else self.side
        return acc[which].at[line : line + 1, self.at : self.at + self.size]


def own_kernel(lefts, rights, table, *refs):
    refs = list(refs)
    lines = [refs.pop(0) for _ in lefts]
    if rights[0].side:
        fars = [refs.pop(0) for _ in rights]
        so_far, best_ref, rowpart = refs
        best_ref[...] = so_far[...]
    else:
        fars = lines
        best_ref, far_ref, second_ref, cap_first, cap_second, rowpart = refs
        for ref in (best_ref, far_ref, second_ref):
            ref[...] = jnp.full(ref.shape, -1.0, jnp.float32)
        for k, ref in enumerate((cap_first, cap_second)):
            ref[...] = jnp.full(ref.shape, jnp.where(table[HAS + k] == 1, BIG, -1.0))
    base = table[BASE]
    for left, left_ref in zip(lefts, lines):
        size = left_ref.shape[0]
        position = base + table[SIDE] + left.at
        position = position + lax.broadcasted_iota(jnp.int32, (size, 1), 0)
        low = jnp.zeros((size, 1), jnp.int32)
        high = jnp.zeros((size, 1), jnp.int32)
        for c in range(SPAN, table.shape[0], 2):
            here = (position >= table[c]) & (position < table[c + 1])
            low = jnp.where(here, table[c], low)
            high = jnp.where(here, table[c + 1], high)
        part = rowpart.at[0:size]
        part[...] = jnp.full(part.shape, -1.0, jnp.float32)
        for right, right_ref in zip(rights, fars):
            start = base + table[SIDE + right.side] + right.at
            scores = product(left_ref[...], right_ref[...])
            column = start + lax.broadcasted_iota(jnp.int32, (1, right_ref.shape[0]), 1)
            keep = (column >= low) & (column < high) & (column != position)
            part[...] = jnp.maximum(part[...], lanes_max(jnp.where(keep, scores, -1.0)))
        best = left.best([best_ref])
        best[...] = jnp.maximum(best[...], across(part[...]))


def own_rows(table, lefts, rights, best):
    bare = lambda pieces: [p.bare() for p in pieces]
    rows, depth = sum(p.n for p in lefts), lefts[0].rows.shape[1]
    shares = (CORES,) if best else (CORES, CORES, 1, 1, 1)
    return vmem_call(
        functools.partial(own_kernel, bare(lefts), bare(rights)),
        [table] + [p.rows for p in (lefts + rights if best else lefts)] + best,
        [jax.ShapeDtypeStruct((n, rows), jnp.float32) for n in shares],
        [pltpu.VMEM((lefts[0].n, 128), jnp.float32)],
        2 * rows * sum(p.n for p in rights) * depth,
    )


PAIRS = {(0, 1): 0, (0, 2): 1, (1, 2): 2}


def rect(table, left, right):
    flip = left.block > right.block
    which = PAIRS[(right.block, left.block) if flip else (left.block, right.block)]
    ends = [table[RECT + 4 * which + k] for k in range(4)]
    if flip:
        ends = ends[2:] + ends[:2]
    x, y = table[SIDE + left.side] + left.at, table[SIDE + right.side] + right.at
    return ends[0] - x, ends[1] - x, ends[2] - y, ends[3] - y


def meet_kernel(pieces, groups, table, *refs):
    refs = list(refs)
    held = [refs.pop(0) for _ in pieces]
    acc_in = [refs.pop(0) for _ in range(3)]
    acc = [refs.pop(0) for _ in range(3)]
    (rowpart,) = refs
    for src, dst in zip(acc_in, acc):
        dst[...] = src[...]
    for l, partners in groups:
        left, left_ref = pieces[l], held[l]
        tm = left_ref.shape[0]
        part = rowpart.at[0:tm]
        part[...] = jnp.full(part.shape, -1.0, jnp.float32)
        shares = {}
        for r in partners:
            shares.setdefault((pieces[r].block, pieces[r].side), []).append(r)
        used = jnp.bool_(False)
        for share in shares.values():
            some = jnp.bool_(False)
            for r in share:
                xa, xb, ya, yb = rect(table, left, pieces[r])
                tn = held[r].shape[0]
                some |= (xa < tm) & (xb > 0) & (ya < tn) & (yb > 0) & (xa < xb) & (ya < yb)
            used |= some

            @pl.when(some)
            def _():
                for r in share:
                    right, right_ref = pieces[r], held[r]
                    tn = right_ref.shape[0]
                    xa, xb, ya, yb = rect(table, left, right)
                    scores = product(left_ref[...], right_ref[...])
                    row = lax.broadcasted_iota(jnp.int32, (tm, 1), 0)
                    col = lax.broadcasted_iota(jnp.int32, (1, tn), 1)
                    keep = ((row >= xa) & (row < xb)) & ((col >= ya) & (col < yb))
                    scores = jnp.where(keep, scores, -1.0)
                    part[...] = jnp.maximum(part[...], lanes_max(scores))
                    best = right.best(acc)
                    best[...] = jnp.maximum(best[...], jnp.max(scores, axis=0, keepdims=True))

        @pl.when(used)
        def _():
            best = left.best(acc)
            best[...] = jnp.maximum(best[...], across(part[...]))


def vmem_call(kernel, ins, outs, scratch, flops, scalars=1):
    vm = pl.BlockSpec(memory_space=pltpu.VMEM)
    sm = pl.BlockSpec(memory_space=pltpu.SMEM)
    pin = lambda x: pltpu.with_memory_space_constraint(x, pltpu.VMEM)
    ins = ins[:scalars] + [pin(x) for x in ins[scalars:]]
    moved = sum(x.size * x.dtype.itemsize for x in [*ins, *outs])
    return pl.pallas_call(
        kernel,
        out_shape=outs,
        in_specs=[sm] * scalars + [vm] * (len(ins) - scalars),
        out_specs=[vm] * len(outs),
        scratch_shapes=scratch,
        compiler_params=pltpu.CompilerParams(vmem_limit_bytes=VMEM),
        cost_estimate=pl.CostEstimate(flops=PACE * flops, bytes_accessed=moved, transcendentals=0),
    )(*ins)


def meet(table, pairs, acc):
    pieces, groups = [], []

    def index(piece):
        for i, other in enumerate(pieces):
            if other is piece:
                return i
        pieces.append(piece)
        return len(pieces) - 1

    for left, rights in pairs:
        groups.append((index(left), [index(r) for r in rights]))
    depth = pieces[0].rows.shape[1]
    flops = sum(2 * left.n * r.n * depth for left, rights in pairs for r in rights)
    most = max(left.n for left, _ in pairs)
    return vmem_call(
        functools.partial(
            meet_kernel, [p.bare() for p in pieces], groups
        ),
        [table] + [p.rows for p in pieces] + list(acc),
        [jax.ShapeDtypeStruct(a.shape, a.dtype) for a in acc],
        [pltpu.VMEM((most, 128), jnp.float32)],
        flops,
    )


def after(value, *others):
    return lax.optimization_barrier((value, *others))[0]


def shards(embeddings, offsets):
    rows, depth = embeddings.shape
    chips = lax.axis_size(AXES) // CORES
    chip_rows = CORES * rows
    first, second = routes(chips)
    to_first, to_second = on_cores(first), on_cores(second)
    swap = [(i, i ^ 1) for i in range(CORES * chips)]
    send = lambda x, pairs: lax.ppermute(x, AXES, pairs)

    spans = chip_rows // MIN_C + 2
    scalars = pl.BlockSpec(memory_space=pltpu.SMEM)
    table = pl.pallas_call(
        functools.partial(plan_kernel, chips, chip_rows, spans),
        out_shape=jax.ShapeDtypeStruct((SPAN + 2 * spans,), jnp.int32),
        in_specs=[scalars],
        out_specs=scalars,
        compiler_params=pltpu.CompilerParams(vmem_limit_bytes=PLAN_VMEM),
    )(offsets)

    eighth = rows // 8
    sizes = [eighth * k for k in SHARES]
    places = [sum(sizes[:k]) for k in range(len(sizes))]
    lead = sizes[0]
    (u1,) = units_of(embeddings, 0, lead, [(0, lead)])
    firsts, seconds = [send(u1, to_first)], [send(u1, to_second)]
    u2, *others = units_of(
        after(embeddings, table),
        lead,
        rows - lead,
        [(0, rows - lead)] + [(p - lead, n) for p, n in zip(places[1:], sizes[1:])][: 2 * (len(sizes) - 2)],
    )
    far1, far2 = send(after(u1, u2), swap), send(u2, swap)
    others = others or [u2]
    firsts.append(send(others[0], to_first))
    seconds.append(send(others[0], to_second))

    own = [Piece(u1, 0, 0, 0), Piece(u2, 0, 0, lead)]
    far = [Piece(far1, 0, 1, 0), Piece(far2, 0, 1, lead)]
    best_near, *blank, cap_first, cap_second = own_rows(table, own, own, [])
    (best_own,) = own_rows(table, own, far, [best_near])
    acc = [best_own, *blank]
    seconds += [send(after(u, best_near), to_second) for u in others[1:]]
    chip_own = own + far

    near_firsts, far_firsts, near_seconds = [], [], []
    for k, at in enumerate(places[:-1]):
        x = Piece(send(after(firsts[k], acc[0]), swap), 1, 1, at)
        a = Piece(firsts[k], 1, 0, at)
        acc = meet(table, [(a, chip_own + near_seconds)], acc)
        if k == 0:
            firsts += [send(after(u, acc[0]), to_first) for u in others[1:]]
        b = Piece(seconds[k], 2, 0, at)
        near_firsts.append(a)
        far_firsts.append(x)
        pairs = [(b, chip_own + near_firsts + far_firsts)]
        if near_seconds:
            pairs.append((x, list(near_seconds)))
        acc = meet(table, pairs, acc)
        near_seconds.append(b)
    at = places[-1]
    b = Piece(seconds[-1], 2, 0, at)
    acc = meet(table, [(b, chip_own + near_firsts + far_firsts)], acc)
    near_seconds.append(b)
    x = Piece(send(after(firsts[-1], acc[0]), swap), 1, 1, at)
    acc = meet(table, [(Piece(firsts[-1], 1, 0, at), chip_own + near_seconds)], acc)
    acc = meet(table, [(x, near_seconds)], acc)

    near, far_best, best_second = acc
    line = jax.ShapeDtypeStruct((1, rows), jnp.float32)
    own_best, best_first = vmem_call(
        join_kernel, [near, send(far_best, swap)], [line] * 2, [], rows, scalars=0
    )
    from_second = send(best_second, on_cores(flipped(second)))
    from_first = send(best_first, on_cores(flipped(first)))
    from_first = jnp.minimum(from_first, cap_first)
    from_second = jnp.minimum(from_second, cap_second)
    return jnp.maximum(jnp.maximum(own_best, from_first), from_second).reshape(rows)


def solution(mesh):
    return jax.shard_map(
        shards,
        mesh=mesh,
        in_specs=(P(AXES, None), P()),
        out_specs=P(AXES),
        check_vma=False,
    )
```

```python
import dataclasses
import functools
import math

import jax
import jax.numpy as jnp
from jax import lax
from jax.experimental import pallas as pl
from jax.experimental.pallas import tpu as pltpu
from jax.sharding import PartitionSpec as P

AXES = ("grp", "work")
CORES = 2
MIN_C = 512
TILE = 512
VMEM = 16 * 1024 * 1024
PLAN_VMEM = 1024 * 1024
PACE = 10
SHARES = [4, 2, 2]


def routes(chips):
    last = chips - 1
    first = [(b, b + 1) for b in range(0, chips, 2) if b + 1 != last]
    first += [(b, b + 3) for b in range(1, chips, 2) if b + 3 < chips]
    first += [(last - 2, last)]
    second = [(b, b + 2) for b in range(0, chips, 2) if b + 2 < chips]
    second += [(b, b - 2) for b in range(1, chips, 2) if b >= 3]
    second += [(last - 1, last)]
    return second, first


def on_cores(pairs):
    return [(CORES * s + k, CORES * d + k) for s, d in pairs for k in range(CORES)]


def flipped(pairs):
    return [(d, s) for s, d in pairs]


BIG = 3.0e38
RECT, SIDE, HAS, BASE, SPAN = 0, 12, 14, 16, 17


def plan_kernel(chips, chip_rows, spans, offsets, out):
    me = lax.axis_index(AXES)
    chip, core = lax.div(me, CORES), lax.rem(me, CORES)
    rows = chip_rows // CORES
    odd = lax.rem(chip, 2) == 1
    at_end = chip == chips - 1
    first = jnp.where(odd, jnp.where(at_end, chip - 2, chip - 1), chip - 3)
    second = jnp.where(odd, jnp.where(at_end, chip - 1, chip + 2), chip - 2)
    starts = [b * chip_rows for b in (chip, second, first)]
    for k in range(spans):
        out[SPAN + 2 * k] = 0
        out[SPAN + 2 * k + 1] = 0

    def look(c, state):
        lower, upper = offsets[c], offsets[c + 1]
        lows, highs, count = state[:3], state[3:6], state[6]
        here = (upper > starts[0]) & (lower < starts[0] + chip_rows)

        @pl.when(here)
        def _():
            at = SPAN + 2 * jnp.minimum(count, spans - 1)
            out[at] = lower
            out[at + 1] = upper

        holds = [(lower < s + chip_rows) & (upper >= s + chip_rows) for s in starts]
        lows = [jnp.where(h, lower, v) for h, v in zip(holds, lows)]
        highs = [jnp.where(h, upper, v) for h, v in zip(holds, highs)]
        return (*lows, *highs, count + here.astype(jnp.int32))

    none = jnp.int32(-1)
    state = lax.fori_loop(0, offsets.shape[0] - 1, look, (none,) * 6 + (jnp.int32(0),))
    lows, highs = state[:3], state[3:6]
    for which, (p, q) in enumerate(((0, 1), (0, 2), (1, 2))):
        p_first = starts[p] < starts[q]
        s = jnp.where(p_first, lows[p], lows[q])
        e = jnp.where(p_first, highs[p], highs[q])
        later = jnp.where(p_first, starts[q], starts[p])
        ok = (lows[p] >= 0) & (lows[q] >= 0) & (e > later)
        if which == 1:
            ok &= ~at_end
        for k, (b, is_first) in enumerate(((p, p_first), (q, ~p_first))):
            a = jnp.where(is_first, jnp.maximum(s - starts[b], 0), 0)
            z = jnp.where(is_first, chip_rows, jnp.minimum(e - starts[b], chip_rows))
            out[RECT + 4 * which + 2 * k] = a
            out[RECT + 4 * which + 2 * k + 1] = jnp.where(ok, z, a)
    out[SIDE] = core * rows
    out[SIDE + 1] = (1 - core) * rows
    has_first = jnp.where(odd, (chip + 3 < chips) | (chip == chips - 3), chip + 2 < chips)
    has_second = jnp.where(odd, chip >= 3, (chip + 2 < chips) | (chip == chips - 2))
    out[HAS + 1] = has_first.astype(jnp.int32)
    out[HAS] = has_second.astype(jnp.int32)
    out[BASE] = starts[0]


def join_kernel(near_ref, far_ref, own_ref, first_ref):
    both = jnp.maximum(near_ref[...], far_ref[...])
    own_ref[...] = both[0:1]
    first_ref[...] = both[1:2]


def unit_of(raw):
    wide = raw.astype(jnp.float32)
    mean = jnp.sum(wide * wide, axis=1, keepdims=True) * (1.0 / raw.shape[1])
    factor = lax.rsqrt(mean + 1e-06) * (1.0 / math.sqrt(raw.shape[1]))
    return (wide * factor).astype(jnp.bfloat16)


def unit_kernel(first, cuts, raw_ref, *refs):
    outs, (held, sems) = refs[:-2], refs[-2:]
    count, step, _ = held.shape
    copies = []
    for k in range(count):
        rows = raw_ref.at[first + k * step : first + (k + 1) * step]
        copies.append(pltpu.make_async_copy(rows, held.at[k], sems.at[k]))
        copies[-1].start()
    for k, copy in enumerate(copies):
        copy.wait()
        unit = unit_of(held[k])
        for (start, n), out in zip(cuts, outs):
            if start <= k * step < start + n:
                out[k * step - start : (k + 1) * step - start, :] = unit


def units_of(raw, first, rows, cuts):
    depth = raw.shape[1]
    step = math.gcd(128, rows)
    return pl.pallas_call(
        functools.partial(unit_kernel, first, cuts),
        in_specs=[pl.BlockSpec(memory_space=pl.ANY)],
        out_specs=[pl.BlockSpec(memory_space=pltpu.VMEM)] * len(cuts),
        out_shape=[jax.ShapeDtypeStruct((n, depth), jnp.bfloat16) for _, n in cuts],
        scratch_shapes=[
            pltpu.VMEM((rows // step, step, depth), jnp.bfloat16),
            pltpu.SemaphoreType.DMA((rows // step,)),
        ],
        compiler_params=pltpu.CompilerParams(vmem_limit_bytes=VMEM),
        cost_estimate=pl.CostEstimate(
            flops=8 * rows * depth, bytes_accessed=4 * rows * depth, transcendentals=0
        ),
    )(pltpu.with_memory_space_constraint(raw, pltpu.HBM))


def product(left, right):
    return lax.dot_general(
        left, right, (((1,), (1,)), ((), ())), preferred_element_type=jnp.float32
    )


def lanes_max(scores):
    parts = [scores[:, j : j + 128] for j in range(0, scores.shape[1], 128)]
    return functools.reduce(jnp.maximum, parts)


def across(part):
    return jnp.max(part.T, axis=0, keepdims=True)


@dataclasses.dataclass
class Piece:
    rows: jax.Array
    block: int
    side: int
    at: int
    size: int = 0

    @property
    def n(self):
        return self.rows.shape[0]

    def bare(self):
        return dataclasses.replace(self, rows=None, size=self.n)

    def best(self, acc):
        line = 0 if self.block == 2 else self.block
        which = 2 if self.block == 2 else self.side
        return acc[which].at[line : line + 1, self.at : self.at + self.size]


def own_kernel(lefts, rights, table, *refs):
    refs = list(refs)
    lines = [refs.pop(0) for _ in lefts]
    if rights[0].side:
        fars = [refs.pop(0) for _ in rights]
        so_far, best_ref, rowpart = refs
        best_ref[...] = so_far[...]
    else:
        fars = lines
        best_ref, far_ref, second_ref, cap_first, cap_second, rowpart = refs
        for ref in (best_ref, far_ref, second_ref):
            ref[...] = jnp.full(ref.shape, -1.0, jnp.float32)
        for k, ref in enumerate((cap_first, cap_second)):
            ref[...] = jnp.full(ref.shape, jnp.where(table[HAS + k] == 1, BIG, -1.0))
    base = table[BASE]
    for left, left_ref in zip(lefts, lines):
        size = left_ref.shape[0]
        position = base + table[SIDE] + left.at
        position = position + lax.broadcasted_iota(jnp.int32, (size, 1), 0)
        low = jnp.zeros((size, 1), jnp.int32)
        high = jnp.zeros((size, 1), jnp.int32)
        for c in range(SPAN, table.shape[0], 2):
            here = (position >= table[c]) & (position < table[c + 1])
            low = jnp.where(here, table[c], low)
            high = jnp.where(here, table[c + 1], high)
        part = rowpart.at[0:size]
        part[...] = jnp.full(part.shape, -1.0, jnp.float32)
        for right, right_ref in zip(rights, fars):
            start = base + table[SIDE + right.side] + right.at
            scores = product(left_ref[...], right_ref[...])
            column = start + lax.broadcasted_iota(jnp.int32, (1, right_ref.shape[0]), 1)
            keep = (column >= low) & (column < high) & (column != position)
            part[...] = jnp.maximum(part[...], lanes_max(jnp.where(keep, scores, -1.0)))
        best = left.best([best_ref])
        best[...] = jnp.maximum(best[...], across(part[...]))


def own_rows(table, lefts, rights, best):
    bare = lambda pieces: [p.bare() for p in pieces]
    rows, depth = sum(p.n for p in lefts), lefts[0].rows.shape[1]
    shares = (CORES,) if best else (CORES, CORES, 1, 1, 1)
    return vmem_call(
        functools.partial(own_kernel, bare(lefts), bare(rights)),
        [table] + [p.rows for p in (lefts + rights if best else lefts)] + best,
        [jax.ShapeDtypeStruct((n, rows), jnp.float32) for n in shares],
        [pltpu.VMEM((lefts[0].n, 128), jnp.float32)],
        2 * rows * sum(p.n for p in rights) * depth,
    )


PAIRS = {(0, 1): 0, (0, 2): 1, (1, 2): 2}


def rect(table, left, right):
    flip = left.block > right.block
    which = PAIRS[(right.block, left.block) if flip else (left.block, right.block)]
    ends = [table[RECT + 4 * which + k] for k in range(4)]
    if flip:
        ends = ends[2:] + ends[:2]
    x, y = table[SIDE + left.side] + left.at, table[SIDE + right.side] + right.at
    return ends[0] - x, ends[1] - x, ends[2] - y, ends[3] - y


def meet_kernel(pieces, groups, table, *refs):
    refs = list(refs)
    held = [refs.pop(0) for _ in pieces]
    acc_in = [refs.pop(0) for _ in range(3)]
    acc = [refs.pop(0) for _ in range(3)]
    (rowpart,) = refs
    for src, dst in zip(acc_in, acc):
        dst[...] = src[...]
    for l, partners in groups:
        left, left_ref = pieces[l], held[l]
        tm = left_ref.shape[0]
        part = rowpart.at[0:tm]
        part[...] = jnp.full(part.shape, -1.0, jnp.float32)
        shares = {}
        for r in partners:
            shares.setdefault((pieces[r].block, pieces[r].side), []).append(r)
        used = jnp.bool_(False)
        for share in shares.values():
            some = jnp.bool_(False)
            for r in share:
                xa, xb, ya, yb = rect(table, left, pieces[r])
                tn = held[r].shape[0]
                some |= (xa < tm) & (xb > 0) & (ya < tn) & (yb > 0) & (xa < xb) & (ya < yb)
            used |= some

            @pl.when(some)
            def _():
                for r in share:
                    right, right_ref = pieces[r], held[r]
                    tn = right_ref.shape[0]
                    xa, xb, ya, yb = rect(table, left, right)
                    scores = product(left_ref[...], right_ref[...])
                    row = lax.broadcasted_iota(jnp.int32, (tm, 1), 0)
                    col = lax.broadcasted_iota(jnp.int32, (1, tn), 1)
                    keep = ((row >= xa) & (row < xb)) & ((col >= ya) & (col < yb))
                    scores = jnp.where(keep, scores, -1.0)
                    part[...] = jnp.maximum(part[...], lanes_max(scores))
                    best = right.best(acc)
                    best[...] = jnp.maximum(best[...], jnp.max(scores, axis=0, keepdims=True))

        @pl.when(used)
        def _():
            best = left.best(acc)
            best[...] = jnp.maximum(best[...], across(part[...]))


def vmem_call(kernel, ins, outs, scratch, flops, scalars=1):
    vm = pl.BlockSpec(memory_space=pltpu.VMEM)
    sm = pl.BlockSpec(memory_space=pltpu.SMEM)
    pin = lambda x: pltpu.with_memory_space_constraint(x, pltpu.VMEM)
    ins = ins[:scalars] + [pin(x) for x in ins[scalars:]]
    moved = sum(x.size * x.dtype.itemsize for x in [*ins, *outs])
    return pl.pallas_call(
        kernel,
        out_shape=outs,
        in_specs=[sm] * scalars + [vm] * (len(ins) - scalars),
        out_specs=[vm] * len(outs),
        scratch_shapes=scratch,
        compiler_params=pltpu.CompilerParams(vmem_limit_bytes=VMEM),
        cost_estimate=pl.CostEstimate(flops=PACE * flops, bytes_accessed=moved, transcendentals=0),
    )(*ins)


def meet(table, pairs, acc):
    pieces, groups = [], []

    def index(piece):
        for i, other in enumerate(pieces):
            if other is piece:
                return i
        pieces.append(piece)
        return len(pieces) - 1

    for left, rights in pairs:
        groups.append((index(left), [index(r) for r in rights]))
    depth = pieces[0].rows.shape[1]
    flops = sum(2 * left.n * r.n * depth for left, rights in pairs for r in rights)
    most = max(left.n for left, _ in pairs)
    return vmem_call(
        functools.partial(
            meet_kernel, [p.bare() for p in pieces], groups
        ),
        [table] + [p.rows for p in pieces] + list(acc),
        [jax.ShapeDtypeStruct(a.shape, a.dtype) for a in acc],
        [pltpu.VMEM((most, 128), jnp.float32)],
        flops,
    )


def after(value, *others):
    return lax.optimization_barrier((value, *others))[0]


def shards(embeddings, offsets):
    rows, depth = embeddings.shape
    chips = lax.axis_size(AXES) // CORES
    chip_rows = CORES * rows
    first, second = routes(chips)
    to_first, to_second = on_cores(first), on_cores(second)
    swap = [(i, i ^ 1) for i in range(CORES * chips)]
    send = lambda x, pairs: lax.ppermute(x, AXES, pairs)

    spans = chip_rows // MIN_C + 2
    scalars = pl.BlockSpec(memory_space=pltpu.SMEM)
    table = pl.pallas_call(
        functools.partial(plan_kernel, chips, chip_rows, spans),
        out_shape=jax.ShapeDtypeStruct((SPAN + 2 * spans,), jnp.int32),
        in_specs=[scalars],
        out_specs=scalars,
        compiler_params=pltpu.CompilerParams(vmem_limit_bytes=PLAN_VMEM),
    )(offsets)

    eighth = rows // 8
    sizes = [eighth * k for k in SHARES]
    places = [sum(sizes[:k]) for k in range(len(sizes))]
    lead = sizes[0]
    (u1,) = units_of(embeddings, 0, lead, [(0, lead)])
    firsts, seconds = [send(u1, to_first)], [send(u1, to_second)]
    u2, *others = units_of(
        after(embeddings, table),
        lead,
        rows - lead,
        [(0, rows - lead)] + [(p - lead, n) for p, n in zip(places[1:], sizes[1:])][: 2 * (len(sizes) - 2)],
    )
    far1, far2 = send(after(u1, u2), swap), send(u2, swap)
    others = others or [u2]
    firsts.append(send(others[0], to_first))
    seconds.append(send(others[0], to_second))

    own = [Piece(u1, 0, 0, 0), Piece(u2, 0, 0, lead)]
    far = [Piece(far1, 0, 1, 0), Piece(far2, 0, 1, lead)]
    best_near, *blank, cap_first, cap_second = own_rows(table, own, own, [])
    (best_own,) = own_rows(table, own, far, [best_near])
    acc = [best_own, *blank]
    seconds += [send(after(u, best_near), to_second) for u in others[1:]]
    chip_own = own + far

    near_firsts, far_firsts, near_seconds = [], [], []
    for k, at in enumerate(places[:-1]):
        x = Piece(send(after(firsts[k], acc[0]), swap), 1, 1, at)
        a = Piece(firsts[k], 1, 0, at)
        acc = meet(table, [(a, chip_own + near_seconds)], acc)
        if k == 0:
            firsts += [send(after(u, acc[0]), to_first) for u in others[1:]]
        b = Piece(seconds[k], 2, 0, at)
        near_firsts.append(a)
        far_firsts.append(x)
        pairs = [(b, chip_own + near_firsts + far_firsts)]
        if near_seconds:
            pairs.append((x, list(near_seconds)))
        acc = meet(table, pairs, acc)
        near_seconds.append(b)
    at = places[-1]
    b = Piece(seconds[-1], 2, 0, at)
    acc = meet(table, [(b, chip_own + near_firsts + far_firsts)], acc)
    near_seconds.append(b)
    x = Piece(send(after(firsts[-1], acc[0]), swap), 1, 1, at)
    acc = meet(table, [(Piece(firsts[-1], 1, 0, at), chip_own + near_seconds)], acc)
    acc = meet(table, [(x, near_seconds)], acc)

    near, far_best, best_second = acc
    line = jax.ShapeDtypeStruct((1, rows), jnp.float32)
    own_best, best_first = vmem_call(
        join_kernel, [near, send(far_best, swap)], [line] * 2, [], rows, scalars=0
    )
    from_second = send(best_second, on_cores(flipped(second)))
    from_first = send(best_first, on_cores(flipped(first)))
    from_first = jnp.minimum(from_first, cap_first)
    from_second = jnp.minimum(from_second, cap_second)
    return jnp.maximum(jnp.maximum(own_best, from_first), from_second).reshape(rows)


def solution(mesh):
    return jax.shard_map(
        shards,
        mesh=mesh,
        in_specs=(P(AXES, None), P()),
        out_specs=P(AXES),
        check_vma=False,
    )
```

```python
import dataclasses
import functools
import math

import jax
import jax.numpy as jnp
from jax import lax
from jax.experimental import pallas as pl
from jax.experimental.pallas import tpu as pltpu
from jax.sharding import PartitionSpec as P

AXES = ("grp", "work")
CORES = 2
MIN_C = 512
TILE = 512
VMEM = 16 * 1024 * 1024
PLAN_VMEM = 1024 * 1024
PACE = 10
SHARES = [4, 2, 2]


def routes(chips):
    last = chips - 1
    first = [(b, b + 1) for b in range(0, chips, 2) if b + 1 != last]
    first += [(b, b + 3) for b in range(1, chips, 2) if b + 3 < chips]
    first += [(last - 2, last)]
    second = [(b, b + 2) for b in range(0, chips, 2) if b + 2 < chips]
    second += [(b, b - 2) for b in range(1, chips, 2) if b >= 3]
    second += [(last - 1, last)]
    return first, second


def on_cores(pairs):
    return [(CORES * s + k, CORES * d + k) for s, d in pairs for k in range(CORES)]


def flipped(pairs):
    return [(d, s) for s, d in pairs]


BIG = 3.0e38
RECT, SIDE, HAS, BASE, SPAN = 0, 12, 14, 16, 17


def plan_kernel(chips, chip_rows, spans, offsets, out):
    me = lax.axis_index(AXES)
    chip, core = lax.div(me, CORES), lax.rem(me, CORES)
    rows = chip_rows // CORES
    odd = lax.rem(chip, 2) == 1
    at_end = chip == chips - 1
    first = jnp.where(odd, jnp.where(at_end, chip - 2, chip - 1), chip - 3)
    second = jnp.where(odd, jnp.where(at_end, chip - 1, chip + 2), chip - 2)
    starts = [b * chip_rows for b in (chip, first, second)]
    for k in range(spans):
        out[SPAN + 2 * k] = 0
        out[SPAN + 2 * k + 1] = 0

    def look(c, state):
        lower, upper = offsets[c], offsets[c + 1]
        lows, highs, count = state[:3], state[3:6], state[6]
        here = (upper > starts[0]) & (lower < starts[0] + chip_rows)

        @pl.when(here)
        def _():
            at = SPAN + 2 * jnp.minimum(count, spans - 1)
            out[at] = lower
            out[at + 1] = upper

        holds = [(lower < s + chip_rows) & (upper >= s + chip_rows) for s in starts]
        lows = [jnp.where(h, lower, v) for h, v in zip(holds, lows)]
        highs = [jnp.where(h, upper, v) for h, v in zip(holds, highs)]
        return (*lows, *highs, count + here.astype(jnp.int32))

    none = jnp.int32(-1)
    state = lax.fori_loop(0, offsets.shape[0] - 1, look, (none,) * 6 + (jnp.int32(0),))
    lows, highs = state[:3], state[3:6]
    for which, (p, q) in enumerate(((0, 1), (0, 2), (1, 2))):
        p_first = starts[p] < starts[q]
        s = jnp.where(p_first, lows[p], lows[q])
        e = jnp.where(p_first, highs[p], highs[q])
        later = jnp.where(p_first, starts[q], starts[p])
        ok = (lows[p] >= 0) & (lows[q] >= 0) & (e > later)
        if which == 0:
            ok &= ~at_end
        for k, (b, is_first) in enumerate(((p, p_first), (q, ~p_first))):
            a = jnp.where(is_first, jnp.maximum(s - starts[b], 0), 0)
            z = jnp.where(is_first, chip_rows, jnp.minimum(e - starts[b], chip_rows))
            out[RECT + 4 * which + 2 * k] = a
            out[RECT + 4 * which + 2 * k + 1] = jnp.where(ok, z, a)
    out[SIDE] = core * rows
    out[SIDE + 1] = (1 - core) * rows
    has_first = jnp.where(odd, (chip + 3 < chips) | (chip == chips - 3), chip + 2 < chips)
    has_second = jnp.where(odd, chip >= 3, (chip + 2 < chips) | (chip == chips - 2))
    out[HAS] = has_first.astype(jnp.int32)
    out[HAS + 1] = has_second.astype(jnp.int32)
    out[BASE] = starts[0]


def join_kernel(near_ref, far_ref, own_ref, first_ref):
    both = jnp.maximum(near_ref[...], far_ref[...])
    own_ref[...] = both[0:1]
    first_ref[...] = both[1:2]


def unit_of(raw):
    wide = raw.astype(jnp.float32)
    mean = jnp.sum(wide * wide, axis=1, keepdims=True) * (1.0 / raw.shape[1])
    factor = lax.rsqrt(mean + 1e-06) * (1.0 / math.sqrt(raw.shape[1]))
    return (wide * factor).astype(jnp.bfloat16)


def unit_kernel(first, cuts, raw_ref, *refs):
    outs, (held, sems) = refs[:-2], refs[-2:]
    count, step, _ = held.shape
    copies = []
    for k in range(count):
        rows = raw_ref.at[first + k * step : first + (k + 1) * step]
        copies.append(pltpu.make_async_copy(rows, held.at[k], sems.at[k]))
        copies[-1].start()
    for k, copy in enumerate(copies):
        copy.wait()
        unit = unit_of(held[k])
        for (start, n), out in zip(cuts, outs):
            if start <= k * step < start + n:
                out[k * step - start : (k + 1) * step - start, :] = unit


def units_of(raw, first, rows, cuts):
    depth = raw.shape[1]
    step = math.gcd(128, rows)
    return pl.pallas_call(
        functools.partial(unit_kernel, first, cuts),
        in_specs=[pl.BlockSpec(memory_space=pl.ANY)],
        out_specs=[pl.BlockSpec(memory_space=pltpu.VMEM)] * len(cuts),
        out_shape=[jax.ShapeDtypeStruct((n, depth), jnp.bfloat16) for _, n in cuts],
        scratch_shapes=[
            pltpu.VMEM((rows // step, step, depth), jnp.bfloat16),
            pltpu.SemaphoreType.DMA((rows // step,)),
        ],
        compiler_params=pltpu.CompilerParams(vmem_limit_bytes=VMEM),
        cost_estimate=pl.CostEstimate(
            flops=8 * rows * depth, bytes_accessed=4 * rows * depth, transcendentals=0
        ),
    )(pltpu.with_memory_space_constraint(raw, pltpu.HBM))


def product(left, right):
    return lax.dot_general(
        left, right, (((1,), (1,)), ((), ())), preferred_element_type=jnp.float32
    )


def lanes_max(scores):
    parts = [scores[:, j : j + 128] for j in range(0, scores.shape[1], 128)]
    return functools.reduce(jnp.maximum, parts)


def across(part):
    return jnp.max(part.T, axis=0, keepdims=True)


@dataclasses.dataclass
class Piece:
    rows: jax.Array
    block: int
    side: int
    at: int
    size: int = 0

    @property
    def n(self):
        return self.rows.shape[0]

    def bare(self):
        return dataclasses.replace(self, rows=None, size=self.n)

    def best(self, acc):
        line = 0 if self.block == 2 else self.block
        which = 2 if self.block == 2 else self.side
        return acc[which].at[line : line + 1, self.at : self.at + self.size]


def own_kernel(lefts, rights, table, *refs):
    refs = list(refs)
    lines = [refs.pop(0) for _ in lefts]
    if rights[0].side:
        fars = [refs.pop(0) for _ in rights]
        so_far, best_ref, rowpart = refs
        best_ref[...] = so_far[...]
    else:
        fars = lines
        best_ref, far_ref, second_ref, cap_first, cap_second, rowpart = refs
        for ref in (best_ref, far_ref, second_ref):
            ref[...] = jnp.full(ref.shape, -1.0, jnp.float32)
        for k, ref in enumerate((cap_first, cap_second)):
            ref[...] = jnp.full(ref.shape, jnp.where(table[HAS + k] == 1, BIG, -1.0))
    base = table[BASE]
    for left, left_ref in zip(lefts, lines):
        size = left_ref.shape[0]
        position = base + table[SIDE] + left.at
        position = position + lax.broadcasted_iota(jnp.int32, (size, 1), 0)
        low = jnp.zeros((size, 1), jnp.int32)
        high = jnp.zeros((size, 1), jnp.int32)
        for c in range(SPAN, table.shape[0], 2):
            here = (position >= table[c]) & (position < table[c + 1])
            low = jnp.where(here, table[c], low)
            high = jnp.where(here, table[c + 1], high)
        part = rowpart.at[0:size]
        part[...] = jnp.full(part.shape, -1.0, jnp.float32)
        for right, right_ref in zip(rights, fars):
            start = base + table[SIDE + right.side] + right.at
            scores = product(left_ref[...], right_ref[...])
            column = start + lax.broadcasted_iota(jnp.int32, (1, right_ref.shape[0]), 1)
            keep = (column >= low) & (column < high) & (column != position)
            part[...] = jnp.maximum(part[...], lanes_max(jnp.where(keep, scores, -1.0)))
        best = left.best([best_ref])
        best[...] = jnp.maximum(best[...], across(part[...]))


def own_rows(table, lefts, rights, best):
    bare = lambda pieces: [p.bare() for p in pieces]
    rows, depth = sum(p.n for p in lefts), lefts[0].rows.shape[1]
    shares = (CORES,) if best else (CORES, CORES, 1, 1, 1)
    return vmem_call(
        functools.partial(own_kernel, bare(lefts), bare(rights)),
        [table] + [p.rows for p in (lefts + rights if best else lefts)] + best,
        [jax.ShapeDtypeStruct((n, rows), jnp.float32) for n in shares],
        [pltpu.VMEM((lefts[0].n, 128), jnp.float32)],
        2 * rows * sum(p.n for p in rights) * depth,
    )


PAIRS = {(0, 1): 0, (0, 2): 1, (1, 2): 2}


def rect(table, left, right):
    flip = left.block > right.block
    which = PAIRS[(right.block, left.block) if flip else (left.block, right.block)]
    ends = [table[RECT + 4 * which + k] for k in range(4)]
    if flip:
        ends = ends[2:] + ends[:2]
    x, y = table[SIDE + left.side] + left.at, table[SIDE + right.side] + right.at
    return ends[0] - x, ends[1] - x, ends[2] - y, ends[3] - y


def meet_kernel(pieces, groups, table, *refs):
    refs = list(refs)
    held = [refs.pop(0) for _ in pieces]
    acc_in = [refs.pop(0) for _ in range(3)]
    acc = [refs.pop(0) for _ in range(3)]
    (rowpart,) = refs
    for src, dst in zip(acc_in, acc):
        dst[...] = src[...]
    for l, partners in groups:
        left, left_ref = pieces[l], held[l]
        tm = left_ref.shape[0]
        part = rowpart.at[0:tm]
        part[...] = jnp.full(part.shape, -1.0, jnp.float32)
        shares = {}
        for r in partners:
            shares.setdefault((pieces[r].block, pieces[r].side), []).append(r)
        used = jnp.bool_(False)
        for share in shares.values():
            some = jnp.bool_(False)
            for r in share:
                xa, xb, ya, yb = rect(table, left, pieces[r])
                tn = held[r].shape[0]
                some |= (xa < tm) & (xb > 0) & (ya < tn) & (yb > 0) & (xa < xb) & (ya < yb)
            used |= some

            @pl.when(some)
            def _():
                for r in share:
                    right, right_ref = pieces[r], held[r]
                    tn = right_ref.shape[0]
                    xa, xb, ya, yb = rect(table, left, right)
                    scores = product(left_ref[...], right_ref[...])
                    row = lax.broadcasted_iota(jnp.int32, (tm, 1), 0)
                    col = lax.broadcasted_iota(jnp.int32, (1, tn), 1)
                    keep = ((row >= xa) & (row < xb)) & ((col >= ya) & (col < yb))
                    scores = jnp.where(keep, scores, -1.0)
                    part[...] = jnp.maximum(part[...], lanes_max(scores))
                    best = right.best(acc)
                    best[...] = jnp.maximum(best[...], jnp.max(scores, axis=0, keepdims=True))

        @pl.when(used)
        def _():
            best = left.best(acc)
            best[...] = jnp.maximum(best[...], across(part[...]))


def vmem_call(kernel, ins, outs, scratch, flops, scalars=1):
    vm = pl.BlockSpec(memory_space=pltpu.VMEM)
    sm = pl.BlockSpec(memory_space=pltpu.SMEM)
    pin = lambda x: pltpu.with_memory_space_constraint(x, pltpu.VMEM)
    ins = ins[:scalars] + [pin(x) for x in ins[scalars:]]
    moved = sum(x.size * x.dtype.itemsize for x in [*ins, *outs])
    return pl.pallas_call(
        kernel,
        out_shape=outs,
        in_specs=[sm] * scalars + [vm] * (len(ins) - scalars),
        out_specs=[vm] * len(outs),
        scratch_shapes=scratch,
        compiler_params=pltpu.CompilerParams(vmem_limit_bytes=VMEM),
        cost_estimate=pl.CostEstimate(flops=PACE * flops, bytes_accessed=moved, transcendentals=0),
    )(*ins)


def meet(table, pairs, acc):
    pieces, groups = [], []

    def index(piece):
        for i, other in enumerate(pieces):
            if other is piece:
                return i
        pieces.append(piece)
        return len(pieces) - 1

    for left, rights in pairs:
        groups.append((index(left), [index(r) for r in rights]))
    depth = pieces[0].rows.shape[1]
    flops = sum(2 * left.n * r.n * depth for left, rights in pairs for r in rights)
    most = max(left.n for left, _ in pairs)
    return vmem_call(
        functools.partial(
            meet_kernel, [p.bare() for p in pieces], groups
        ),
        [table] + [p.rows for p in pieces] + list(acc),
        [jax.ShapeDtypeStruct(a.shape, a.dtype) for a in acc],
        [pltpu.VMEM((most, 128), jnp.float32)],
        flops,
    )


def after(value, *others):
    return lax.optimization_barrier((value, *others))[0]


def shards(embeddings, offsets):
    rows, depth = embeddings.shape
    chips = lax.axis_size(AXES) // CORES
    chip_rows = CORES * rows
    first, second = routes(chips)
    to_first, to_second = on_cores(first), on_cores(second)
    swap = [(i, i ^ 1) for i in range(CORES * chips)]
    send = lambda x, pairs: lax.ppermute(x, AXES, pairs)

    spans = chip_rows // MIN_C + 2
    scalars = pl.BlockSpec(memory_space=pltpu.SMEM)
    table = pl.pallas_call(
        functools.partial(plan_kernel, chips, chip_rows, spans),
        out_shape=jax.ShapeDtypeStruct((SPAN + 2 * spans,), jnp.int32),
        in_specs=[scalars],
        out_specs=scalars,
        compiler_params=pltpu.CompilerParams(vmem_limit_bytes=PLAN_VMEM),
    )(offsets)

    eighth = rows // 8
    sizes = [eighth * k for k in SHARES]
    places = [sum(sizes[:k]) for k in range(len(sizes))]
    lead = sizes[0]
    (u1,) = units_of(embeddings, 0, lead, [(0, lead)])
    firsts, seconds = [send(u1, to_first)], [send(u1, to_second)]
    u2, *others = units_of(
        after(embeddings, table),
        lead,
        rows - lead,
        [(0, rows - lead)] + [(p - lead, n) for p, n in zip(places[1:], sizes[1:])][: 2 * (len(sizes) - 2)],
    )
    far1, far2 = send(after(u1, u2), swap), send(u2, swap)
    others = others or [u2]
    firsts.append(send(others[0], to_first))
    seconds.append(send(others[0], to_second))

    own = [Piece(u1, 0, 0, 0), Piece(u2, 0, 0, lead)]
    far = [Piece(far1, 0, 1, 0), Piece(far2, 0, 1, lead)]
    best_near, *blank, cap_first, cap_second = own_rows(table, own, own, [])
    (best_own,) = own_rows(table, own, far, [best_near])
    acc = [best_own, *blank]
    seconds += [send(after(u, best_near), to_second) for u in others[1:]]
    chip_own = own + far

    near_firsts, far_firsts, near_seconds = [], [], []
    for k, at in enumerate(places[:-1]):
        x = Piece(send(after(firsts[k], acc[0]), swap), 1, 1, at)
        a = Piece(firsts[k], 1, 0, at)
        acc = meet(table, [(a, chip_own + near_seconds)], acc)
        if k == 0:
            firsts += [send(after(u, acc[0]), to_first) for u in others[1:]]
        b = Piece(seconds[k], 2, 0, at)
        near_firsts.append(a)
        far_firsts.append(x)
        pairs = [(b, chip_own + near_firsts + far_firsts)]
        if near_seconds:
            pairs.append((x, list(near_seconds)))
        acc = meet(table, pairs, acc)
        near_seconds.append(b)
    at = places[-1]
    b = Piece(seconds[-1], 2, 0, at)
    acc = meet(table, [(b, chip_own)], acc)
    near_seconds.append(b)
    x = Piece(send(after(firsts[-1], acc[0]), swap), 1, 1, at)
    a = Piece(firsts[-1], 1, 0, at)
    acc = meet(table, [(a, chip_own + near_seconds), (b, near_firsts + far_firsts)], acc)
    acc = meet(table, [(x, near_seconds)], acc)

    near, far_best, best_second = acc
    line = jax.ShapeDtypeStruct((1, rows), jnp.float32)
    own_best, best_first = vmem_call(
        join_kernel, [near, send(far_best, swap)], [line] * 2, [], rows, scalars=0
    )
    from_second = send(best_second, on_cores(flipped(second)))
    from_first = send(best_first, on_cores(flipped(first)))
    from_first = jnp.minimum(from_first, cap_first)
    from_second = jnp.minimum(from_second, cap_second)
    return jnp.maximum(jnp.maximum(own_best, from_first), from_second).reshape(rows)


def solution(mesh):
    return jax.shard_map(
        shards,
        mesh=mesh,
        in_specs=(P(AXES, None), P()),
        out_specs=P(AXES),
        check_vma=False,
    )
```
